32 devices in a mesh: dp: 8 (over z, x), rows: 4 (over y, core).
Axes of the slice: x: 2, y: 2, z: 4, core: 2. Of those that a mesh axis runs over, the one named last changes fastest.
Arguments:
- atoms_big: bfloat16 [4, 8, 256, 512], P(None, 'dp', 'rows'), may hold values from -6 to 6
- atoms_mid: bfloat16 [4, 8, 128, 512], P(None, 'dp', 'rows'), may hold values from -6 to 6
- atoms_small: bfloat16 [4, 16, 64, 512], P(None, 'dp', 'rows'), may hold values from -6 to 6
- pair_big: bfloat16 [4, 8, 64, 256, 256], P(None, 'dp', None, 'rows'), may hold values from -6 to 6
- pair_mid: bfloat16 [4, 8, 64, 128, 128], P(None, 'dp', None, 'rows'), may hold values from -6 to 6
- pair_small: bfloat16 [4, 16, 64, 64, 64], P(None, 'dp', None, 'rows'), may hold values from -6 to 6
- lengths_big: int32 [4, 8], P(None, 'dp'), may hold values from 129 to 256, as said below
- lengths_mid: int32 [4, 8], P(None, 'dp'), may hold values from 65 to 128, as said below
- lengths_small: int32 [4, 16], P(None, 'dp'), may hold values from 33 to 64, as said below
- query_weight: bfloat16 [512, 512], replicated, may hold values from -0.25 to 0.25
- key_weight: bfloat16 [512, 512], replicated, may hold values from -0.25 to 0.25
- value_weight: bfloat16 [512, 512], replicated, may hold values from -0.25 to 0.25
- out_weight: bfloat16 [512, 512], replicated, may hold values from -1.5 to 1.5
- up_weight: bfloat16 [512, 2048], replicated, may hold values from -0.25 to 0.25
- down_weight: bfloat16 [2048, 512], replicated, may hold values from -0.125 to 0.125
- gain_one: float32 [512], replicated, may hold values from 0.25 to 1.75
- shift_one: float32 [512], replicated, may hold values from -1.8 to 1.8
- gain_two: float32 [512], replicated, may hold values from 0.25 to 1.75
- shift_two: float32 [512], replicated, may hold values from -1.8 to 1.8
- cotangent_big: bfloat16 [4, 8, 256, 512], P(None, 'dp', 'rows'), may hold values from -6 to 6
- cotangent_mid: bfloat16 [4, 8, 128, 512], P(None, 'dp', 'rows'), may hold values from -6 to 6
- cotangent_small: bfloat16 [4, 16, 64, 512], P(None, 'dp', 'rows'), may hold values from -6 to 6
- cotangent_pair_big: bfloat16 [4, 8, 64, 256, 256], P(None, 'dp', None, 'rows'), may hold values from -0.29882812 to 0.29882812
- cotangent_pair_mid: bfloat16 [4, 8, 64, 128, 128], P(None, 'dp', None, 'rows'), may hold values from -0.29882812 to 0.29882812
- cotangent_pair_small: bfloat16 [4, 16, 64, 64, 64], P(None, 'dp', None, 'rows'), may hold values from -0.29882812 to 0.29882812
Outputs:
- atoms_out_big: bfloat16 [4, 8, 256, 512], P(None, 'dp', 'rows')
- atoms_out_mid: bfloat16 [4, 8, 128, 512], P(None, 'dp', 'rows')
- atoms_out_small: bfloat16 [4, 16, 64, 512], P(None, 'dp', 'rows')
- pair_out_big: bfloat16 [4, 8, 64, 256, 256], P(None, 'dp', None, 'rows')
- pair_out_mid: bfloat16 [4, 8, 64, 128, 128], P(None, 'dp', None, 'rows')
- pair_out_small: bfloat16 [4, 16, 64, 64, 64], P(None, 'dp', None, 'rows')
- grad_atoms_big: bfloat16 [4, 8, 256, 512], P(None, 'dp', 'rows')
- grad_atoms_mid: bfloat16 [4, 8, 128, 512], P(None, 'dp', 'rows')
- grad_atoms_small: bfloat16 [4, 16, 64, 512], P(None, 'dp', 'rows')
- grad_pair_big: bfloat16 [4, 8, 64, 256, 256], P(None, 'dp', None, 'rows')
- grad_pair_mid: bfloat16 [4, 8, 64, 128, 128], P(None, 'dp', None, 'rows')
- grad_pair_small: bfloat16 [4, 16, 64, 64, 64], P(None, 'dp', None, 'rows')
- grad_query_weight: float32 [512, 512], replicated
- grad_key_weight: float32 [512, 512], replicated
- grad_value_weight: float32 [512, 512], replicated
- grad_out_weight: float32 [512, 512], replicated
- grad_up_weight: float32 [512, 2048], replicated
- grad_down_weight: float32 [2048, 512], replicated
- grad_gain_one: float32 [512], replicated
- grad_shift_one: float32 [512], replicated
- grad_gain_two: float32 [512], replicated
- grad_shift_two: float32 [512], replicated
The draws below stay inside these ranges and needn't reach their ends.
Inputs may be any that keep to these rules, and one draw needn't show every extreme that they name: `lengths_big`: atoms of each molecule; keys at or beyond the length are padding; some molecule fills the bucket. `lengths_mid`: atoms of each molecule; keys at or beyond the length are padding; some molecule fills the bucket. `lengths_small`: atoms of each molecule; keys at or beyond the length are padding; some molecule fills the bucket.
All inputs are finite; a program needn't handle non-finite values.
Results may differ from the reference program's by a relative error of at most 0.012.
The reference program's roundings to bfloat16 on the way count: a program that leaves them out, or rounds other values in their place, can miss the bound.
Values may be sent and summed in bfloat16 or wider, within the bound.
No kernel may reach another device: no remote copies, remote signals or barrier semaphores. Data moves between devices by JAX's collectives and lax.ppermute only.
A program may use at most 320 MiB of HBM per device.

```python
import jax
import jax.numpy as jnp
from jax import lax

D = 512
FF = 2048
HEADS = 64
BIG = 256
MID = 128
SMALL = 64
MICRO = 4
MOLS_BIG = 8
MOLS_MID = 8
MOLS_SMALL = 16


def lengths_law(key, count, bucket):
    drawn = jax.random.randint(key, (MICRO, count), bucket // 2 + 1, bucket + 1, dtype=jnp.int32)
    return drawn.at[0, 0].set(bucket)


def draw_lengths_big(key, part):
    return lengths_law(jax.random.fold_in(key, 11), MOLS_BIG, BIG)


def draw_lengths_mid(key, part):
    return lengths_law(jax.random.fold_in(key, 12), MOLS_MID, MID)


def draw_lengths_small(key, part):
    return lengths_law(jax.random.fold_in(key, 13), MOLS_SMALL, SMALL)


def steps_of(rng, dims, pieces, least, high):
    factor_of, own = 1.0, jax.random.fold_in(rng, 6)
    for axis_at, parts in pieces:
        heights = jnp.exp(jax.random.uniform(jax.random.fold_in(own, axis_at), (parts,), jnp.float32, least / len(pieces), high / len(pieces)))
        factor_of = factor_of * jnp.repeat(heights, dims[axis_at] // parts).reshape([-1 if axis == axis_at else 1 for axis in range(len(dims))])
    return factor_of


def bell_draw(stream_key, shape, scale, bound, shards=(), held_as=jnp.bfloat16):
    values = scale * jax.random.normal(stream_key, shape, jnp.float32)
    if shards:
        values = values * steps_of(stream_key, shape, shards, -0.22, 0.18)
    return jnp.clip(values, -bound, bound).astype(held_as)


def setup_inputs(seed: int = 0) -> dict:
    key_list = jax.random.split(jax.random.key(seed), 26)
    return {
        "atoms_big": bell_draw(key_list[0], (MICRO, MOLS_BIG, BIG, D), 1.0, 6.0, ((1, 8), (2, 4))),
        "atoms_mid": bell_draw(key_list[1], (MICRO, MOLS_MID, MID, D), 1.0, 6.0, ((1, 8), (2, 4))),
        "atoms_small": bell_draw(key_list[2], (MICRO, MOLS_SMALL, SMALL, D), 1.0, 6.0, ((1, 8), (2, 4))),
        "pair_big": bell_draw(key_list[3], (MICRO, MOLS_BIG, HEADS, BIG, BIG), 1.0, 6.0, ((1, 8), (3, 4))),
        "pair_mid": bell_draw(key_list[4], (MICRO, MOLS_MID, HEADS, MID, MID), 1.0, 6.0, ((1, 8), (3, 4))),
        "pair_small": bell_draw(key_list[5], (MICRO, MOLS_SMALL, HEADS, SMALL, SMALL), 1.0, 6.0, ((1, 8), (3, 4))),
        "lengths_big": draw_lengths_big(jax.random.fold_in(key_list[25], 71), 0),
        "lengths_mid": draw_lengths_mid(jax.random.fold_in(key_list[25], 71), 0),
        "lengths_small": draw_lengths_small(jax.random.fold_in(key_list[25], 71), 0),
        "query_weight": bell_draw(key_list[9], (D, D), D ** -0.5, 0.25),
        "key_weight": bell_draw(key_list[10], (D, D), D ** -0.5, 0.25),
        "value_weight": bell_draw(key_list[11], (D, D), D ** -0.5, 0.25),
        "out_weight": bell_draw(key_list[12], (D, D), (D // 32) ** -0.5, 1.5),
        "up_weight": bell_draw(key_list[13], (D, FF), D ** -0.5, 0.25),
        "down_weight": bell_draw(key_list[14], (FF, D), FF ** -0.5, 0.125),
        "gain_one": jnp.clip(1.0 + 0.15 * jax.random.normal(key_list[15], (D,), jnp.float32), 0.25, 1.75),
        "shift_one": bell_draw(key_list[16], (D,), 0.3, 1.8, (), jnp.float32),
        "gain_two": jnp.clip(1.0 + 0.15 * jax.random.normal(key_list[17], (D,), jnp.float32), 0.25, 1.75),
        "shift_two": bell_draw(key_list[18], (D,), 0.3, 1.8, (), jnp.float32),
        "cotangent_big": bell_draw(key_list[19], (MICRO, MOLS_BIG, BIG, D), 1.0, 6.0, ((1, 8), (2, 4))),
        "cotangent_mid": bell_draw(key_list[20], (MICRO, MOLS_MID, MID, D), 1.0, 6.0, ((1, 8), (2, 4))),
        "cotangent_small": bell_draw(key_list[21], (MICRO, MOLS_SMALL, SMALL, D), 1.0, 6.0, ((1, 8), (2, 4))),
        "cotangent_pair_big": bell_draw(key_list[22], (MICRO, MOLS_BIG, HEADS, BIG, BIG), 0.05, 0.29882812, ((1, 8), (3, 4))),
        "cotangent_pair_mid": bell_draw(key_list[23], (MICRO, MOLS_MID, HEADS, MID, MID), 0.05, 0.29882812, ((1, 8), (3, 4))),
        "cotangent_pair_small": bell_draw(key_list[24], (MICRO, MOLS_SMALL, HEADS, SMALL, SMALL), 0.05, 0.29882812, ((1, 8), (3, 4))),
    }


@jax.custom_vjp
def low(v):
    return lax.optimization_barrier(v.astype(jnp.bfloat16)).astype(jnp.float32)

@jax.custom_vjp
def low_back(v):
    return v

def low_keep(v):
    return (low(v), None)

def low_pass(kept, grad):
    return (grad,)

def back_keep(v):
    return (v, None)

def back_low(kept, grad):
    return (low(grad),)
low.defvjp(low_keep, low_pass)
low_back.defvjp(back_keep, back_low)
EPSILON = 1e-05
MASKED_LOGIT = -1e+30
PRECISE = lax.Precision.HIGHEST

def norm_rows(inputs, gain, shift):
    center = lax.optimization_barrier(jnp.mean(inputs, axis=-1, keepdims=True))
    centred = inputs - center
    spread = lax.optimization_barrier(jnp.mean(centred * centred, axis=-1, keepdims=True))
    return centred * lax.rsqrt(spread + EPSILON) * gain + shift

def precise_dot(left, right):
    return jnp.dot(left, right, precision=PRECISE, preferred_element_type=jnp.float32)

def molecule(params, atom_block, pair_block, length):
    query_weight, key_weight, value_weight, out_weight, up_weight, down_weight, gain_one, shift_one, gain_two, shift_two = params
    slots = atom_block.shape[0]
    width = atom_block.shape[1]
    head_count = pair_block.shape[0]
    head_width = width // head_count
    normed = low(norm_rows(atom_block, gain_one, shift_one))
    queries = low_back(low(precise_dot(normed, query_weight))).reshape(slots, head_count, head_width)
    key_rows = low_back(low(precise_dot(normed, key_weight))).reshape(slots, head_count, head_width)
    values = low_back(low(precise_dot(normed, value_weight))).reshape(slots, head_count, head_width)
    products = jnp.einsum('ihc,jhc->hij', queries, key_rows, precision=PRECISE)
    logits = low_back(products * head_width ** (-0.5) + pair_block)
    key_valid = lax.broadcasted_iota(jnp.int32, (1, 1, slots), 2) < length
    softmax = low(jax.nn.softmax(jnp.where(key_valid, logits, MASKED_LOGIT), axis=-1))
    mixed_heads = jnp.einsum('hij,jhc->ihc', softmax, values, precision=PRECISE).reshape(slots, width)
    mixed_heads = low_back(low(mixed_heads))
    hidden = atom_block + low_back(precise_dot(mixed_heads, out_weight))
    normed_two = low(norm_rows(hidden, gain_two, shift_two))
    up_proj = low_back(precise_dot(normed_two, up_weight))
    gelu_out = low(jax.nn.gelu(up_proj, approximate=True))
    return (hidden + low_back(precise_dot(gelu_out, down_weight)), logits)

def flatten_mols(array):
    return array.reshape((-1,) + array.shape[2:]).astype(jnp.float32)

def reference(atoms_big, atoms_mid, atoms_small, pair_big, pair_mid, pair_small, lengths_big, lengths_mid, lengths_small, query_weight, key_weight, value_weight, out_weight, up_weight, down_weight, gain_one, shift_one, gain_two, shift_two, cotangent_big, cotangent_mid, cotangent_small, cotangent_pair_big, cotangent_pair_mid, cotangent_pair_small):
    params = tuple((weight.astype(jnp.float32) for weight in (query_weight, key_weight, value_weight, out_weight, up_weight, down_weight, gain_one, shift_one, gain_two, shift_two)))
    atom_list = tuple((flatten_mols(array) for array in (atoms_big, atoms_mid, atoms_small)))
    pair_list = tuple((flatten_mols(array) for array in (pair_big, pair_mid, pair_small)))
    length_list = tuple((array.reshape(-1).astype(jnp.int32) for array in (lengths_big, lengths_mid, lengths_small)))

    def forward(weights, atom_inputs, pair_inputs):
        results = []
        logit_list = []
        for bucket in range(3):

            def per_molecule(molecule_item):
                return jax.checkpoint(molecule)(weights, molecule_item[0], molecule_item[1], molecule_item[2])
            result, logits = lax.map(per_molecule, (atom_inputs[bucket], pair_inputs[bucket], length_list[bucket]))
            results.append(result)
            logit_list.append(logits)
        return (tuple(results), tuple(logit_list))
    outputs, pullback = jax.vjp(forward, params, atom_list, pair_list)
    atom_cots = tuple((flatten_mols(array) for array in (cotangent_big, cotangent_mid, cotangent_small)))
    pair_cots = tuple((flatten_mols(array) for array in (cotangent_pair_big, cotangent_pair_mid, cotangent_pair_small)))
    weight_grads, atom_grads, pair_grads = pullback((atom_cots, pair_cots))
    shapes_atoms = (atoms_big.shape, atoms_mid.shape, atoms_small.shape)
    shapes_pair = (pair_big.shape, pair_mid.shape, pair_small.shape)
    atoms_out = [outputs[0][bucket].reshape(shapes_atoms[bucket]).astype(jnp.bfloat16) for bucket in range(3)]
    pair_out = [outputs[1][bucket].reshape(shapes_pair[bucket]).astype(jnp.bfloat16) for bucket in range(3)]
    grad_atoms = [atom_grads[bucket].reshape(shapes_atoms[bucket]).astype(jnp.bfloat16) for bucket in range(3)]
    grad_pair = [pair_grads[bucket].reshape(shapes_pair[bucket]).astype(jnp.bfloat16) for bucket in range(3)]
    return (atoms_out[0], atoms_out[1], atoms_out[2], pair_out[0], pair_out[1], pair_out[2], grad_atoms[0], grad_atoms[1], grad_atoms[2], grad_pair[0], grad_pair[1], grad_pair[2], weight_grads[0], weight_grads[1], weight_grads[2], weight_grads[3], weight_grads[4], weight_grads[5], weight_grads[6], weight_grads[7], weight_grads[8], weight_grads[9])
```

```python
import functools

import jax
import jax.numpy as jnp
from jax import lax
from jax.experimental import pallas as pl
from jax.experimental.pallas import tpu as pltpu
from jax.sharding import PartitionSpec as P

EPSILON = 1e-05
MASKED = -1e30
BF = jnp.bfloat16
F32 = jnp.float32
LANES = 128
GELU_C = 0.7978845608028654
GELU_A = 0.044715
MIB = 1 << 20


def dot_nn(a, b):
    return lax.dot_general(a, b, (((1,), (0,)), ((), ())), preferred_element_type=F32)


def dot_nt(a, b):
    return lax.dot_general(a, b, (((1,), (1,)), ((), ())), preferred_element_type=F32)


def dot_tn(a, b):
    return lax.dot_general(a, b, (((0,), (0,)), ((), ())), preferred_element_type=F32)


def normalize(x):
    centred = x - jnp.mean(x, axis=-1, keepdims=True)
    spread = jnp.mean(centred * centred, axis=-1, keepdims=True)
    inv = lax.rsqrt(spread + EPSILON)
    return centred * inv, inv


def norm_back(grad, gain, xhat, inv):
    g = grad * gain
    return inv * (
        g
        - jnp.mean(g, axis=-1, keepdims=True)
        - xhat * jnp.mean(g * xhat, axis=-1, keepdims=True)
    )


def front_kernel(
    layout, me_ref, x0, x1, x2, x3, wq, wk, wv, gain, shift, q_out, *outs
):
    me = me_ref[0]
    for piece, x_ref in enumerate((x0, x1, x2, x3)):
        xhat, _ = normalize(x_ref[...].astype(F32))
        a1 = (xhat * gain[...] + shift[...]).astype(BF)
        xhat = xhat.astype(BF)
        keys = dot_nn(a1, wk[...]).astype(BF)
        values = dot_nn(a1, wv[...]).astype(BF)
        if piece == 0:
            q_out[...] = dot_nn(a1, wq[...]).astype(BF)
        row = me ^ piece
        for bucket, (start, mols, rows, slots) in enumerate(layout):
            for mol in range(mols):
                src = slice(start + mol * rows, start + (mol + 1) * rows)
                at = pl.multiple_of(mol * slots + row * rows, rows)
                for kind, value in enumerate((keys, values, a1, xhat)):
                    outs[4 * bucket + kind][pl.ds(at, rows), :] = value[src]


def head_mask(heads, first):
    lane = lax.broadcasted_iota(jnp.int32, (1, LANES), 1) // (LANES // heads)
    return lane == first


def stacked(block, heads, first, count):
    zero = jnp.zeros_like(block)
    return jnp.concatenate(
        [jnp.where(head_mask(heads, first + t), block, zero) for t in range(count)], axis=0
    )


def unstacked(total, product, heads, first, count, rows):
    for t in range(count):
        part = product[t * rows : (t + 1) * rows]
        total = total + jnp.where(head_mask(heads, first + t), part, 0.0)
    return total


def attn_fwd_kernel(
    mols, groups, heads, rows, slots, scale,
    len_ref, q_ref, k_ref, v_ref, pair_ref, pout_ref, p_ref, o_ref,
):
    count = min(heads, max(1, 256 // rows))
    for mol in range(mols):
        length = len_ref[pl.program_id(0) * mols + mol]
        key_at = lax.broadcasted_iota(jnp.int32, (1, 1, slots), 2)
        mask = jnp.where(key_at < length, 0.0, MASKED)
        for group in range(groups):
            lanes = slice(group * LANES, (group + 1) * LANES)
            q = q_ref[mol * rows : (mol + 1) * rows, lanes]
            k = k_ref[mol * slots : (mol + 1) * slots, lanes]
            v = v_ref[mol * slots : (mol + 1) * slots, lanes]
            total = jnp.zeros((rows, LANES), F32)
            for first in range(0, heads, count):
                at = slice(group * heads + first, group * heads + first + count)
                s = dot_nt(stacked(q, heads, first, count), k)
                s = s.reshape(count, rows, slots) * scale + pair_ref[mol, at].astype(F32)
                pout_ref[mol, at] = s.astype(BF)
                s = s + mask
                e = jnp.exp(s - jnp.max(s, axis=-1, keepdims=True))
                p = (e * (1.0 / jnp.sum(e, axis=-1, keepdims=True))).astype(BF)
                p_ref[mol, at] = p
                pv = dot_nn(p.reshape(count * rows, slots), v)
                total = unstacked(total, pv, heads, first, count, rows)
            o_ref[mol * rows : (mol + 1) * rows, lanes] = total


def attn_bwd_kernel(
    mols, groups, heads, rows, slots, scale,
    q_ref, k_ref, v_ref, do_ref, dd_ref, p_ref, dpo_ref, dl_ref, dq_ref, dk_ref, dv_ref,
):
    count = min(heads, max(1, 256 // rows))
    for group in range(groups):
        lanes = slice(group * LANES, (group + 1) * LANES)
        dk_all = []
        dv_all = []
        for mol in range(mols):
            rs = slice(mol * rows, (mol + 1) * rows)
            ks = slice(mol * slots, (mol + 1) * slots)
            q = q_ref[rs, lanes]
            do = do_ref[rs, lanes]
            dd = dd_ref[rs, lanes]
            k = k_ref[ks, lanes]
            v = v_ref[ks, lanes]
            v_aug = jnp.concatenate([v, jnp.ones_like(v)], axis=1)
            total = jnp.zeros((rows, LANES), F32)
            dk = jnp.zeros((LANES, slots), F32)
            dv = jnp.zeros((LANES, slots), F32)
            for first in range(0, heads, count):
                at = slice(group * heads + first, group * heads + first + count)
                do_s = stacked(do, heads, first, count)
                t = dot_nt(
                    jnp.concatenate([do_s, stacked(dd, heads, first, count)], axis=1), v_aug
                )
                p = p_ref[mol, at]
                dl = p.astype(F32) * t.reshape(count, rows, slots) + dpo_ref[mol, at].astype(F32)
                dl = dl.astype(BF)
                dl_ref[mol, at] = dl
                dl = dl.reshape(count * rows, slots)
                total = unstacked(total, dot_nn(dl, k), heads, first, count, rows)
                dk = dk + dot_tn(stacked(q, heads, first, count), dl)
                dv = dv + dot_tn(do_s, p.reshape(count * rows, slots))
            dq_ref[rs, lanes] = (total * scale).astype(BF)
            dk_all.append((dk * scale).astype(BF))
            dv_all.append(dv.astype(BF))
        dk_ref[lanes, :] = jnp.concatenate(dk_all, axis=1)
        dv_ref[lanes, :] = jnp.concatenate(dv_all, axis=1)


def shard_rows(ref, lead, value, chunks, mine):
    size = value.shape[0] // chunks
    for chunk in range(chunks):
        at = pl.multiple_of((chunk ^ mine) * size, size)
        ref[lead, pl.ds(at, size), :] = value[chunk * size : (chunk + 1) * size].astype(ref.dtype)


def dense_kernel(
    tiles, chunks,
    ids, x_ref, ob, om, os, dyb, dym, dys, wo, wu, wd, gain, shift,
    yb, ym, ys, dh_ref, do_ref, dd_ref, go_ref, gs_ref, up_send, down_send, up_keep, down_keep,
    o_s, dy_s, h_s, a2_s, xhat_s, inv_s, y_s, da_s,
):
    step = pl.program_id(0)

    @pl.when(step == 0)
    def _():
        o_s[...] = jnp.concatenate([ob[...], om[...], os[...]], axis=0)
        dy_s[...] = jnp.concatenate([dyb[...], dym[...], dys[...]], axis=0)
        hidden = x_ref[...].astype(F32) + dot_nn(o_s[...].astype(BF), wo[...])
        xhat, inv = normalize(hidden)
        h_s[...] = hidden
        xhat_s[...] = xhat
        inv_s[...] = jnp.broadcast_to(inv, inv_s.shape)
        a2_s[...] = (xhat * gain[...] + shift[...]).astype(BF)
        y_s[...] = hidden
        da_s[...] = jnp.zeros_like(da_s)

    a2 = a2_s[...]
    dy = dy_s[...]
    u = dot_nn(a2, wu[...])
    u2 = u * u
    th = jnp.tanh(GELU_C * (u + GELU_A * u * u2))
    half = 0.5 * (1.0 + th)
    g = (u * half).astype(BF)
    slope = half + 0.5 * u * (1.0 - th * th) * (GELU_C * (1.0 + 3.0 * GELU_A * u2))
    y_s[...] += dot_nn(g, wd[...])
    grad_down = dot_tn(g, dy)
    du = (dot_nt(dy, wd[...]) * slope).astype(BF)
    grad_up = dot_tn(a2, du)
    da_s[...] += dot_nt(du, wu[...])

    @pl.when(step < tiles // 2)
    def _():
        shard_rows(up_send, 0, grad_up, chunks, ids[1])
        shard_rows(down_send, 0, grad_down, chunks, ids[2])

    @pl.when(step >= tiles // 2)
    def _():
        shard_rows(up_keep, 0, grad_up, chunks, ids[1])
        shard_rows(down_keep, 0, grad_down, chunks, ids[2])

    @pl.when(step == tiles - 1)
    def _():
        y = y_s[...].astype(BF)
        nb, nm = yb.shape[0], ym.shape[0]
        yb[...] = y[:nb]
        ym[...] = y[nb : nb + nm]
        ys[...] = y[nb + nm :]
        da = da_s[...]
        xhat = xhat_s[...]
        gs_ref[0:1, :] = jnp.sum(da * xhat, axis=0, keepdims=True)
        gs_ref[1:2, :] = jnp.sum(da, axis=0, keepdims=True)
        dh = dy.astype(F32) + norm_back(da, gain[...], xhat, inv_s[:, 0:1])
        dh_ref[...] = dh
        dh = dh.astype(BF)
        o = o_s[...]
        go_ref[...] = dot_tn(o.astype(BF), dh).astype(BF)
        do = dot_nt(dh, wo[...]).astype(BF)
        do_ref[...] = do
        dd_ref[...] = (-(do.astype(F32) * o)).astype(BF)


def back_kernel(
    layout, chunks,
    ids, dqb, dqm, dqs, dkb, dkm, dks, dvb, dvm, dvs,
    ab, am, as_, hb, hm, hs, wq, wk, wv, go_ref,
    own_ref, keep_ref, send_ref, gs_ref, w_send, w_keep, da_s,
):
    me = ids[3]
    core = ids[0]
    dq = jnp.concatenate([dqb[...], dqm[...], dqs[...]], axis=0)
    daq = dot_nt(dq, wq[...])
    grads = []
    gain_sum = jnp.zeros((1, daq.shape[1]), F32)
    shift_sum = jnp.sum(daq, axis=0, keepdims=True)
    gk = jnp.zeros((wk.shape[1], wk.shape[0]), F32)
    gv = jnp.zeros_like(gk)
    a_own = []
    h_own = []
    base = 0
    for (start, mols, rows, slots), dk, dv, a, h in zip(
        layout, (dkb, dkm, dks), (dvb, dvm, dvs), (ab, am, as_), (hb, hm, hs)
    ):
        size = mols * slots
        da = lax.dot_general(
            dk[...], wk[...], (((0,), (1,)), ((), ())), preferred_element_type=F32
        ) + lax.dot_general(
            dv[...], wv[...], (((0,), (1,)), ((), ())), preferred_element_type=F32
        )
        gk = gk + dot_nn(dk[...], a[...])
        gv = gv + dot_nn(dv[...], a[...])
        gain_sum = gain_sum + jnp.sum(da * h[...].astype(F32), axis=0, keepdims=True)
        shift_sum = shift_sum + jnp.sum(da, axis=0, keepdims=True)
        da_s[base : base + size, :] = da
        for mol in range(mols):
            at = pl.multiple_of(mol * slots + me * rows, rows)
            a_own.append(a[pl.ds(at, rows), :])
            h_own.append(h[pl.ds(at, rows), :])
        base += size
    a_own = jnp.concatenate(a_own, axis=0)
    h_own = jnp.concatenate(h_own, axis=0)
    gq = dot_tn(a_own, dq)
    gain_sum = gain_sum + jnp.sum(daq * h_own.astype(F32), axis=0, keepdims=True)
    gs_ref[0:1, :] = gain_sum
    gs_ref[1:2, :] = shift_sum
    for piece in range(4):
        base = 0
        for start, mols, rows, slots in layout:
            for mol in range(mols):
                at = pl.multiple_of(base + mol * slots + (me ^ piece) * rows, rows)
                value = da_s[pl.ds(at, rows), :]
                to = slice(start + mol * rows, start + (mol + 1) * rows)
                if piece == 0:
                    own_ref[to, :] = value + daq[to]
                elif piece == 2:
                    keep_ref[to, :] = value.astype(BF)
                else:
                    send_ref[piece // 2, to, :] = value.astype(BF)
            base += mols * slots

    @pl.when(core == 0)
    def _():
        shard_rows(w_keep, 0, go_ref[...], chunks, ids[1])
        shard_rows(w_keep, 1, gq, chunks, ids[2])
        shard_rows(w_send, 0, gk, chunks, ids[1])
        shard_rows(w_send, 1, gv, chunks, ids[2])

    @pl.when(core == 1)
    def _():
        shard_rows(w_send, 0, go_ref[...], chunks, ids[1])
        shard_rows(w_send, 1, gq, chunks, ids[2])
        shard_rows(w_keep, 0, gk, chunks, ids[1])
        shard_rows(w_keep, 1, gv, chunks, ids[2])


def last_kernel(x_ref, own, near, far, dh, gain, gb, gm, gs):
    xhat, inv = normalize(x_ref[...].astype(F32))
    da = own[...] + near[...].astype(F32) + far[...].astype(F32)
    grad = (dh[...] + norm_back(da, gain[...], xhat, inv)).astype(BF)
    nb, nm = gb.shape[0], gm.shape[0]
    gb[...] = grad[:nb]
    gm[...] = grad[nb : nb + nm]
    gs[...] = grad[nb + nm :]


def exchange(value, axis, distance, size):
    return lax.ppermute(value, axis, [(i, i ^ distance) for i in range(size)])


def add_low(first, *others):
    total = first.astype(F32)
    for other in others:
        total = total + other.astype(F32)
    return total.astype(BF)


def reduce_shards(tile, order, sizes):
    part = tile.reshape(tile.shape[0], 16, tile.shape[1] // 16, tile.shape[2])
    for axis, bit in order:
        half = part.shape[1] // 2
        part = add_low(part[:, :half], exchange(part[:, half:], axis, bit, sizes[axis]))
    quarter = part.shape[1] // 4
    piece = [part[:, k * quarter : (k + 1) * quarter] for k in range(4)]
    part = add_low(
        piece[0], *[exchange(piece[k], "dp", 2 * k, sizes["dp"]) for k in range(1, 4)]
    )
    distance = 8
    while distance < sizes["dp"]:
        part = add_low(part, exchange(part, "dp", distance, sizes["dp"]))
        distance *= 2
    return part


def gather_shards(part, order, sizes):
    part = jnp.concatenate(
        [part] + [exchange(part, "dp", 2 * k, sizes["dp"]) for k in range(1, 4)], axis=1
    )
    for axis, bit in reversed(order):
        part = jnp.concatenate([part, exchange(part, axis, bit, sizes[axis])], axis=1)
    return part.reshape(part.shape[0], part.shape[1] * part.shape[2], part.shape[3])


def all_sum(value, sizes):
    for axis in ("rows", "dp"):
        distance = 1
        while distance < sizes[axis]:
            value = value + exchange(value, axis, distance, sizes[axis])
            distance *= 2
    return value


ORDER_A = (("dp", 1), ("rows", 2))
ORDER_B = (("rows", 2), ("dp", 1))


def full(shape):
    return pl.BlockSpec(shape, lambda *_: (0,) * len(shape))


def params(limit_mib):
    return pltpu.CompilerParams(vmem_limit_bytes=limit_mib * MIB)


def shards(sizes, *args):
    atoms, pairs, lengths = args[0:3], args[3:6], args[6:9]
    wq, wk, wv, wo, wu, wd = args[9:15]
    gain_one, shift_one, gain_two, shift_two = (v.reshape(1, -1) for v in args[15:19])
    dys, dpos = args[19:22], args[22:25]
    width = atoms[0].shape[-1]
    hidden_units = wu.shape[1]
    head_count = pairs[0].shape[2]
    heads = head_count * LANES // width
    scale = float((width // head_count) ** -0.5)
    groups = width // LANES
    chunks = 16

    rows_at = lax.axis_index("rows")
    dp_at = lax.axis_index("dp")
    core, y = rows_at % 2, rows_at // 2
    xa, z = dp_at % 2, (dp_at // 2) % 4
    ids = jnp.stack(
        [core, xa * 8 + y * 4 + z, y * 8 + xa * 4 + z, rows_at, core ^ 1]
    ).astype(jnp.int32)

    layout = []
    start = 0
    for a in atoms:
        mols, rows = a.shape[0] * a.shape[1], a.shape[2]
        layout.append((start, mols, rows, rows * sizes["rows"]))
        start += mols * rows
    layout = tuple(layout)
    local = start

    x = jnp.concatenate([a.reshape(-1, width) for a in atoms], axis=0)
    dy = [d.reshape(-1, width) for d in dys]
    pair = [p.reshape((-1,) + p.shape[2:]) for p in pairs]
    dpo = [p.reshape((-1,) + p.shape[2:]) for p in dpos]
    lens = [n.reshape(-1) for n in lengths]

    x1 = exchange(x, "rows", 1, sizes["rows"])
    x2 = exchange(x, "rows", 2, sizes["rows"])
    x3 = exchange(x2, "rows", 1, sizes["rows"])

    smem = pl.BlockSpec(memory_space=pltpu.SMEM)
    vmem = pl.BlockSpec(memory_space=pltpu.VMEM)
    bucket_rows = [mols * slots for _, mols, _, slots in layout]
    front_shapes = [jax.ShapeDtypeStruct((local, width), BF)]
    for size in bucket_rows:
        front_shapes += [jax.ShapeDtypeStruct((size, width), BF)] * 4
    front = pl.pallas_call(
        functools.partial(front_kernel, layout),
        out_shape=front_shapes,
        in_specs=[smem] + [vmem] * 9,
        out_specs=[vmem] * len(front_shapes),
        compiler_params=params(40),
        name="front",
    )(ids[3:4], x, x1, x2, x3, wq, wk, wv, gain_one, shift_one)
    q = front[0]
    ks, vs, a1s, xhats = (front[1 + kind :: 4] for kind in range(4))

    def blocking(bucket):
        start, mols, rows, slots = layout[bucket]
        per = max(1, 128 // slots)
        per_groups = 1 if slots >= 256 else groups
        grid = (mols // per, groups // per_groups)
        lanes = per_groups * LANES
        offset = start // (per * rows)
        row_spec = pl.BlockSpec((per * rows, lanes), lambda m, g: (offset + m, g))
        out_spec = pl.BlockSpec((per * rows, lanes), lambda m, g: (m, g))
        key_spec = pl.BlockSpec((per * slots, lanes), lambda m, g: (m, g))
        key_t_spec = pl.BlockSpec((lanes, per * slots), lambda m, g: (g, m))
        pair_spec = pl.BlockSpec(
            (per, per_groups * heads, rows, slots), lambda m, g: (m, g, 0, 0)
        )
        args = (per, per_groups, heads, rows, slots, scale)
        return args, grid, row_spec, out_spec, key_spec, key_t_spec, pair_spec

    pair_out, probs, outs = [], [], []
    for bucket in range(3):
        start, mols, rows, slots = layout[bucket]
        static, grid, row_spec, out_spec, key_spec, _, pair_spec = blocking(bucket)
        shape = pair[bucket].shape
        res = pl.pallas_call(
            functools.partial(attn_fwd_kernel, *static),
            grid=grid,
            out_shape=[
                jax.ShapeDtypeStruct(shape, BF),
                jax.ShapeDtypeStruct(shape, BF),
                jax.ShapeDtypeStruct((mols * rows, width), F32),
            ],
            in_specs=[smem, row_spec, key_spec, key_spec, pair_spec],
            out_specs=[pair_spec, pair_spec, out_spec],
            compiler_params=params(32),
            name=f"attend{bucket}",
        )(lens[bucket], q, ks[bucket], vs[bucket], pair[bucket])
        pair_out.append(res[0])
        probs.append(res[1])
        outs.append(res[2])

    tiles = 4
    tile = hidden_units // tiles
    half = tiles // 2

    def tile_at(t, ids):
        return (t + half * ids[4]) % tiles

    def whole(shape):
        return pl.BlockSpec(shape, lambda t, ids: (0,) * len(shape))

    send_spec = pl.BlockSpec((1, tile, width), lambda t, ids: (jnp.minimum(t, half - 1), 0, 0))
    keep_spec = pl.BlockSpec((1, tile, width), lambda t, ids: (jnp.maximum(t - half, 0), 0, 0))
    half_shape = jax.ShapeDtypeStruct((half, tile, width), BF)
    local_shape = (local, width)
    dense = pl.pallas_call(
        functools.partial(dense_kernel, tiles, chunks),
        grid_spec=pltpu.PrefetchScalarGridSpec(
            num_scalar_prefetch=1,
            grid=(tiles,),
            in_specs=[whole(local_shape)]
            + [whole(o.shape) for o in outs]
            + [whole(d.shape) for d in dy]
            + [
                whole(wo.shape),
                pl.BlockSpec((width, tile), lambda t, ids: (0, tile_at(t, ids))),
                pl.BlockSpec((tile, width), lambda t, ids: (tile_at(t, ids), 0)),
                whole((1, width)),
                whole((1, width)),
            ],
            out_specs=[whole(d.shape) for d in dy]
            + [whole(local_shape)] * 3
            + [whole(wo.shape), whole((8, width)), send_spec, send_spec, keep_spec, keep_spec],
            scratch_shapes=[
                pltpu.VMEM(local_shape, F32),
                pltpu.VMEM(local_shape, BF),
                pltpu.VMEM(local_shape, F32),
                pltpu.VMEM(local_shape, BF),
                pltpu.VMEM(local_shape, F32),
                pltpu.VMEM((local, LANES), F32),
                pltpu.VMEM(local_shape, F32),
                pltpu.VMEM(local_shape, F32),
            ],
        ),
        out_shape=[jax.ShapeDtypeStruct(d.shape, BF) for d in dy]
        + [
            jax.ShapeDtypeStruct(local_shape, F32),
            jax.ShapeDtypeStruct(local_shape, BF),
            jax.ShapeDtypeStruct(local_shape, BF),
            jax.ShapeDtypeStruct(wo.shape, BF),
            jax.ShapeDtypeStruct((8, width), F32),
            half_shape,
            half_shape,
            half_shape,
            half_shape,
        ],
        compiler_params=params(56),
        name="dense",
    )(ids, x, *outs, *dy, wo, wu, wd, gain_two, shift_two)
    atoms_out = dense[0:3]
    dh, do, dd, go, gs_two, up_send, down_send, up_keep, down_keep = dense[3:]

    up = add_low(up_keep, exchange(up_send, "rows", 1, sizes["rows"]))
    down = add_low(down_keep, exchange(down_send, "rows", 1, sizes["rows"]))
    up = reduce_shards(up, ORDER_A, sizes)
    down = reduce_shards(down, ORDER_B, sizes)
    up = gather_shards(up, ORDER_A, sizes)
    down = gather_shards(down, ORDER_B, sizes)
    up_other = exchange(up, "rows", 1, sizes["rows"])
    down_other = exchange(down, "rows", 1, sizes["rows"])

    grad_pair, dqs, dks, dvs = [], [], [], []
    for bucket in range(3):
        start, mols, rows, slots = layout[bucket]
        static, grid, row_spec, out_spec, key_spec, key_t_spec, pair_spec = blocking(bucket)
        res = pl.pallas_call(
            functools.partial(attn_bwd_kernel, *static),
            grid=grid,
            out_shape=[
                jax.ShapeDtypeStruct(pair[bucket].shape, BF),
                jax.ShapeDtypeStruct((mols * rows, width), BF),
                jax.ShapeDtypeStruct((width, mols * slots), BF),
                jax.ShapeDtypeStruct((width, mols * slots), BF),
            ],
            in_specs=[row_spec, key_spec, key_spec, row_spec, row_spec, pair_spec, pair_spec],
            out_specs=[pair_spec, out_spec, key_t_spec, key_t_spec],
            compiler_params=params(32),
            name=f"attend_back{bucket}",
        )(q, ks[bucket], vs[bucket], do, dd, probs[bucket], dpo[bucket])
        grad_pair.append(res[0])
        dqs.append(res[1])
        dks.append(res[2])
        dvs.append(res[3])

    pair_tiles = jax.ShapeDtypeStruct((2, width, width), BF)
    own, keep, send, gs_one, w_send, w_keep = pl.pallas_call(
        functools.partial(back_kernel, layout, chunks),
        out_shape=[
            jax.ShapeDtypeStruct(local_shape, F32),
            jax.ShapeDtypeStruct(local_shape, BF),
            jax.ShapeDtypeStruct((2,) + local_shape, BF),
            jax.ShapeDtypeStruct((8, width), F32),
            pair_tiles,
            pair_tiles,
        ],
        in_specs=[smem] + [vmem] * 19,
        out_specs=[vmem] * 6,
        scratch_shapes=[pltpu.VMEM((sum(bucket_rows), width), F32)],
        compiler_params=params(56),
        name="back",
    )(ids, *dqs, *dks, *dvs, *a1s, *xhats, wq, wk, wv, go)

    near = exchange(send, "rows", 1, sizes["rows"])
    far = exchange(add_low(keep, near[1]), "rows", 2, sizes["rows"])
    grad_atoms = pl.pallas_call(
        last_kernel,
        out_shape=[jax.ShapeDtypeStruct(d.shape, BF) for d in dy],
        in_specs=[vmem] * 6,
        out_specs=[vmem] * 3,
        compiler_params=params(32),
        name="last",
    )(x, own, near[0], far, dh, gain_one)

    rest = add_low(w_keep, exchange(w_send, "rows", 1, sizes["rows"]))
    first = gather_shards(reduce_shards(rest[0:1], ORDER_A, sizes), ORDER_A, sizes)
    second = gather_shards(reduce_shards(rest[1:2], ORDER_B, sizes), ORDER_B, sizes)
    first_other = exchange(first, "rows", 1, sizes["rows"])
    second_other = exchange(second, "rows", 1, sizes["rows"])

    gs = jnp.concatenate([gs_one[0:2], gs_two[0:2], jnp.zeros((4, width), F32)], axis=0)
    gs = all_sum(gs, sizes)

    def ordered(ref, mine):
        size = ref.shape[1] // chunks
        return [
            ref[0, pl.ds(pl.multiple_of((c ^ mine) * size, size), size), :].astype(F32)
            for c in range(chunks)
        ]

    def finish_ff(ids, up_m, up_o, down_m, down_o, gu, gd):
        own_tile = (pl.program_id(0) // half) == ids[0]

        @pl.when(own_tile)
        def _():
            gu[...] = jnp.concatenate(ordered(up_m, ids[1]), axis=0)
            gd[...] = jnp.concatenate(ordered(down_m, ids[2]), axis=0)

        @pl.when(jnp.logical_not(own_tile))
        def _():
            gu[...] = jnp.concatenate(ordered(up_o, ids[1]), axis=0)
            gd[...] = jnp.concatenate(ordered(down_o, ids[2]), axis=0)

    half_spec = pl.BlockSpec((1, tile, width), lambda t, ids: (t % half, 0, 0))
    grad_up, grad_down = pl.pallas_call(
        finish_ff,
        grid_spec=pltpu.PrefetchScalarGridSpec(
            num_scalar_prefetch=1,
            grid=(tiles,),
            in_specs=[half_spec] * 4,
            out_specs=[
                pl.BlockSpec((width, tile), lambda t, ids: (0, t)),
                pl.BlockSpec((tile, width), lambda t, ids: (t, 0)),
            ],
        ),
        out_shape=[
            jax.ShapeDtypeStruct(wu.shape, F32),
            jax.ShapeDtypeStruct(wd.shape, F32),
        ],
        compiler_params=params(32),
        name="finish_ff",
    )(ids, up, up_other, down, down_other)

    def finish_rest(ids, first_m, first_o, second_m, second_o, go_out, gq_out, gk_out, gv_out):
        def put(zero_first, zero_second, one_first, one_second):
            go_out[...] = jnp.concatenate(ordered(zero_first, ids[1]), axis=0)
            gq_out[...] = jnp.concatenate(ordered(zero_second, ids[2]), axis=0)
            gk_out[...] = jnp.concatenate(ordered(one_first, ids[1]), axis=0).T
            gv_out[...] = jnp.concatenate(ordered(one_second, ids[2]), axis=0).T

        @pl.when(ids[0] == 0)
        def _():
            put(first_m, second_m, first_o, second_o)

        @pl.when(ids[0] == 1)
        def _():
            put(first_o, second_o, first_m, second_m)

    go, gq, gk, gv = pl.pallas_call(
        finish_rest,
        out_shape=[jax.ShapeDtypeStruct(wo.shape, F32)] * 4,
        in_specs=[smem] + [vmem] * 4,
        out_specs=[vmem] * 4,
        compiler_params=params(32),
        name="finish_rest",
    )(ids, first, first_other, second, second_other)

    return (
        *[v.reshape(a.shape) for v, a in zip(atoms_out, atoms)],
        *[v.reshape(a.shape) for v, a in zip(pair_out, pairs)],
        *[v.reshape(a.shape) for v, a in zip(grad_atoms, atoms)],
        *[v.reshape(a.shape) for v, a in zip(grad_pair, pairs)],
        gq,
        gk,
        gv,
        go,
        grad_up,
        grad_down,
        gs[0],
        gs[1],
        gs[2],
        gs[3],
    )


def solution(mesh):
    atom = P(None, "dp", "rows", None)
    pair = P(None, "dp", None, "rows", None)
    length = P(None, "dp")
    in_specs = (
        (atom,) * 3 + (pair,) * 3 + (length,) * 3 + (P(),) * 10 + (atom,) * 3 + (pair,) * 3
    )
    out_specs = (atom,) * 3 + (pair,) * 3 + (atom,) * 3 + (pair,) * 3 + (P(),) * 10
    body = functools.partial(shards, dict(mesh.shape))
    return jax.shard_map(
        body, mesh=mesh, in_specs=in_specs, out_specs=out_specs, check_vma=False
    )
```

```python
import functools

import jax
import jax.numpy as jnp
from jax import lax
from jax.experimental import pallas as pl
from jax.experimental.pallas import tpu as pltpu
from jax.sharding import PartitionSpec as P

EPSILON = 1e-05
MASKED = -1e30
BF = jnp.bfloat16
F32 = jnp.float32
LANES = 128
GELU_C = 0.7978845608028654
GELU_A = 0.044715
MIB = 1 << 20
CHUNKS = 4
LIMIT = 58


def dot_nn(a, b):
    return lax.dot_general(a, b, (((1,), (0,)), ((), ())), preferred_element_type=F32)


def dot_nt(a, b):
    return lax.dot_general(a, b, (((1,), (1,)), ((), ())), preferred_element_type=F32)


def dot_tn(a, b):
    return lax.dot_general(a, b, (((0,), (0,)), ((), ())), preferred_element_type=F32)


def normalize(x):
    centred = x - jnp.mean(x, axis=-1, keepdims=True)
    spread = jnp.mean(centred * centred, axis=-1, keepdims=True)
    inv = lax.rsqrt(spread + EPSILON)
    return centred * inv, inv


def norm_back(grad, gain, xhat, inv):
    g = grad * gain
    return inv * (
        g
        - jnp.mean(g, axis=-1, keepdims=True)
        - xhat * jnp.mean(g * xhat, axis=-1, keepdims=True)
    )


def front_kernel(pieces, copied, *refs):
    me_ref = refs[0]
    xs = refs[1 : 1 + pieces]
    wq, wk, wv, gain, shift = refs[1 + pieces : 6 + pieces]
    outs = refs[6 + pieces + copied :]
    step = pl.program_id(0)
    for piece in range(pieces):

        @pl.when(step == piece)
        def _(piece=piece):
            xhat, _ = normalize(xs[piece][...].astype(F32))
            a1 = (xhat * gain[...] + shift[...]).astype(BF)
            outs[0][0] = dot_nn(a1, wk[...]).astype(BF)
            outs[1][0] = dot_nn(a1, wv[...]).astype(BF)
            outs[2][0] = a1
            outs[3][0] = xhat.astype(BF)
            if not copied and piece == 0:
                outs[4][...] = dot_nn(a1, wq[...]).astype(BF)


def head_mask(heads, first):
    lane = lax.broadcasted_iota(jnp.int32, (1, LANES), 1) // (LANES // heads)
    return lane == first


def stacked(block, heads, first, count):
    zero = jnp.zeros_like(block)
    return jnp.concatenate(
        [jnp.where(head_mask(heads, first + t), block, zero) for t in range(count)], axis=0
    )


def unstacked(total, product, heads, first, count, rows):
    for t in range(count):
        part = product[t * rows : (t + 1) * rows]
        total = total + jnp.where(head_mask(heads, first + t), part, 0.0)
    return total


def key_rows(ref, start, rows, lanes):
    return jnp.concatenate(
        [ref[r, start : start + rows, lanes] for r in range(ref.shape[0])], axis=0
    )


def attn_fwd_kernel(layout, groups, heads, scale, *refs):
    lens, (q_ref, k_ref, v_ref), pairs = refs[0:3], refs[3:6], refs[6:9]
    pouts, ps, o_ref = refs[9:12], refs[12:15], refs[15]
    for (start, mols, rows, slots), len_ref, pair_ref, pout_ref, p_ref in zip(
        layout, lens, pairs, pouts, ps
    ):
        count = min(heads, max(1, 512 // rows))
        for mol in range(mols):
            length = len_ref[pl.program_id(0) * mols + mol]
            key_at = lax.broadcasted_iota(jnp.int32, (1, 1, slots), 2)
            mask = jnp.where(key_at < length, 0.0, MASKED)
            at_row = start + mol * rows
            for group in range(groups):
                lanes = slice(group * LANES, (group + 1) * LANES)
                q = q_ref[at_row : at_row + rows, lanes]
                k = key_rows(k_ref, at_row, rows, lanes)
                v = key_rows(v_ref, at_row, rows, lanes)
                total = jnp.zeros((rows, LANES), F32)
                for first in range(0, heads, count):
                    at = slice(group * heads + first, group * heads + first + count)
                    s = dot_nt(stacked(q, heads, first, count), k)
                    s = s.reshape(count, rows, slots) * scale + pair_ref[mol, at].astype(F32)
                    pout_ref[mol, at] = s.astype(BF)
                    s = s + mask
                    e = jnp.exp(s - jnp.max(s, axis=-1, keepdims=True))
                    p = (e * (1.0 / jnp.sum(e, axis=-1, keepdims=True))).astype(BF)
                    p_ref[mol, at] = p
                    pv = dot_nn(p.reshape(count * rows, slots), v)
                    total = unstacked(total, pv, heads, first, count, rows)
                o_ref[at_row : at_row + rows, lanes] = total


def attn_bwd_kernel(layout, groups, heads, scale, *refs):
    count_of = len(layout)
    q_ref, do_ref, dd_ref, k_ref, v_ref = refs[0:5]
    ps, dpos = refs[5 : 5 + count_of], refs[5 + count_of : 5 + 2 * count_of]
    dls = refs[5 + 2 * count_of : 5 + 3 * count_of]
    dq_ref, dk_ref, dv_ref = refs[5 + 3 * count_of :]
    ranks = k_ref.shape[0]
    origin = layout[0][0]
    for (start, mols, rows, slots), p_ref, dpo_ref, dl_ref in zip(layout, ps, dpos, dls):
        count = min(heads, max(1, 1024 // rows))
        base = (start - origin) * ranks
        for group in range(groups):
            lanes = slice(group * LANES, (group + 1) * LANES)
            dk_all = []
            dv_all = []
            for mol in range(mols):
                at_row = start + mol * rows
                rs = slice(at_row, at_row + rows)
                q = q_ref[rs, lanes]
                do = do_ref[rs, lanes]
                dd = dd_ref[rs, lanes]
                k = key_rows(k_ref, at_row, rows, lanes)
                v = key_rows(v_ref, at_row, rows, lanes)
                v_aug = jnp.concatenate([v, jnp.ones_like(v)], axis=1)
                total = jnp.zeros((rows, LANES), F32)
                dk = jnp.zeros((LANES, slots), F32)
                dv = jnp.zeros((LANES, slots), F32)
                for first in range(0, heads, count):
                    at = slice(group * heads + first, group * heads + first + count)
                    do_s = stacked(do, heads, first, count)
                    t = dot_nt(
                        jnp.concatenate([do_s, stacked(dd, heads, first, count)], axis=1), v_aug
                    )
                    p = p_ref[mol, at]
                    dl = p.astype(F32) * t.reshape(count, rows, slots)
                    dl = (dl + dpo_ref[mol, at].astype(F32)).astype(BF)
                    dl_ref[mol, at] = dl
                    dl = dl.reshape(count * rows, slots)
                    total = unstacked(total, dot_nn(dl, k), heads, first, count, rows)
                    dk = dk + dot_tn(stacked(q, heads, first, count), dl)
                    dv = dv + dot_tn(do_s, p.reshape(count * rows, slots))
                to = slice(at_row - origin, at_row - origin + rows)
                dq_ref[to, lanes] = (total * scale).astype(BF)
                dk_all.append((dk * scale).astype(BF))
                dv_all.append(dv.astype(BF))
            dk_ref[lanes, base : base + mols * slots] = jnp.concatenate(dk_all, axis=1)
            dv_ref[lanes, base : base + mols * slots] = jnp.concatenate(dv_all, axis=1)


def back_kernel(layout, share, parts, ids, *refs):
    dqs, dks, dvs = (refs[i * parts : (i + 1) * parts] for i in range(3))
    a_ref, h_ref, wq, wk, wv, gs_two = refs[3 * parts : 3 * parts + 6]
    own_ref, keep_ref, send_ref, w_send, w_keep = refs[3 * parts + 6 : 3 * parts + 11]
    gq_ref, gk_ref, gv_ref, gs_ref, da_s = refs[3 * parts + 11 :]
    step = pl.program_id(0)
    me = ids[3]
    ranks = a_ref.shape[0]

    @pl.when(step == 0)
    def _():
        for ref in (gq_ref, gk_ref, gv_ref, gs_ref):
            ref[...] = jnp.zeros_like(ref)

    def molecules(ref):
        return jnp.concatenate(
            [
                key_rows(ref, start + mol * rows, rows, slice(None))
                for start, mols, rows, slots in layout
                for mol in range(mols)
            ],
            axis=0,
        )

    dq = jnp.concatenate([ref[...] for ref in dqs], axis=0)
    dk = jnp.concatenate([ref[...] for ref in dks], axis=1)
    dv = jnp.concatenate([ref[...] for ref in dvs], axis=1)
    a1 = molecules(a_ref)
    gk_ref[...] += dot_nn(dk, a1)
    gv_ref[...] += dot_nn(dv, a1)
    gq_ref[...] += dot_tn(a_ref[me], dq)
    daq = dot_nt(dq, wq[...])
    across = (((0,), (1,)), ((), ()))
    da = lax.dot_general(dk, wk[...], across, preferred_element_type=F32) + lax.dot_general(
        dv, wv[...], across, preferred_element_type=F32
    )
    da_s[...] = da
    gs_ref[0:1, :] += jnp.sum(da * molecules(h_ref).astype(F32), axis=0, keepdims=True) + jnp.sum(
        daq * h_ref[me].astype(F32), axis=0, keepdims=True
    )
    gs_ref[1:2, :] += jnp.sum(da, axis=0, keepdims=True) + jnp.sum(daq, axis=0, keepdims=True)
    for piece in range(ranks):
        for start, mols, rows, slots in layout:
            for mol in range(mols):
                at = pl.multiple_of(start * ranks + mol * slots + (me ^ piece) * rows, rows)
                value = da_s[pl.ds(at, rows), :]
                to = slice(start + mol * rows, start + (mol + 1) * rows)
                if piece == 0:
                    own_ref[to, :] = value + daq[to]
                elif piece == 2:
                    keep_ref[to, :] = value.astype(BF)
                else:
                    send_ref[piece // 2, to, :] = value.astype(BF)

    @pl.when(step == pl.num_programs(0) - 1)
    def _():
        width = gq_ref.shape[1]
        size = width // CHUNKS
        half = width // 2
        gains = jnp.concatenate(
            [gs_ref[0:2, :], gs_two[0:2, :], jnp.zeros((12, width), F32)], axis=0
        ).astype(BF)
        for value in (0, 1):

            @pl.when(ids[0] == value)
            def _(value=value):
                for ref, owner, mine in ((w_keep, value, ids[1]), (w_send, 1 - value, ids[2])):
                    shard_rows(ref, (gk_ref if owner else gq_ref)[...], 0, share, mine)
                    gv = gv_ref[owner * half : (owner + 1) * half, :]
                    shard_rows(ref, gv, size, share, mine)

        w_keep[CHUNKS * share :, :] = gains
        w_send[CHUNKS * share :, :] = gains


def shard_rows(ref, value, at, rows, mine):
    size = value.shape[0] // CHUNKS
    for chunk in range(CHUNKS):
        to = pl.multiple_of((chunk ^ mine) * rows + at, 16)
        ref[pl.ds(to, size), :] = value[chunk * size : (chunk + 1) * size].astype(ref.dtype)


def store_by_bucket(refs, value):
    row = 0
    for micro in range(refs[0].shape[0]):
        for ref in refs:
            ref[micro] = value[row : row + ref.shape[1]]
            row += ref.shape[1]


def store_tile(send_ref, keep_ref, value, step, at, half_tiles, rows, ids):
    size = value.shape[0] // CHUNKS

    @pl.when(step < half_tiles)
    def _():
        shard_rows(send_ref, value, (2 * step + at) * size, rows, ids[2])

    @pl.when(step >= half_tiles)
    def _():
        shard_rows(keep_ref, value, (2 * (step - half_tiles) + at) * size, rows, ids[1])


def dense_kernel(
    tiles, rows, ids, x_ref, o_ref, dy_ref, wo, wu, wd, gain, shift,
    yb, ym, ys, dh_ref, do_ref, dd_ref, gs_ref, send_ref, keep_ref,
    a2_s, y_s, xhat_s, inv_s, da_s,
):
    step = pl.program_id(0)
    half_tiles = tiles // 2

    @pl.when(step == 0)
    def _():
        hidden = x_ref[...].astype(F32) + dot_nn(o_ref[...].astype(BF), wo[...])
        xhat, inv = normalize(hidden)
        y_s[...] = hidden
        xhat_s[...] = xhat
        inv_s[...] = jnp.broadcast_to(inv, inv_s.shape)
        a2_s[...] = (xhat * gain[...] + shift[...]).astype(BF)
        da_s[...] = jnp.zeros_like(da_s)

    dy = dy_ref[...]
    u = dot_nn(a2_s[...], wu[...])
    u2 = u * u
    th = jnp.tanh(GELU_C * (u + GELU_A * u * u2))
    half = 0.5 * (1.0 + th)
    g = (u * half).astype(BF)
    slope = half + 0.5 * u * (1.0 - th * th) * (GELU_C * (1.0 + 3.0 * GELU_A * u2))
    y_s[...] += dot_nn(g, wd[...])
    store_tile(send_ref, keep_ref, dot_tn(g, dy), step, 1, half_tiles, rows, ids)
    du = (dot_nt(dy, wd[...]) * slope).astype(BF)
    store_tile(send_ref, keep_ref, dot_tn(a2_s[...], du), step, 0, half_tiles, rows, ids)
    da_s[...] += dot_nt(du, wu[...])

    @pl.when(step == tiles - 1)
    def _():
        store_by_bucket((yb, ym, ys), y_s[...].astype(BF))
        da = da_s[...]
        xhat = xhat_s[...]
        gs_ref[0:1, :] = jnp.sum(da * xhat, axis=0, keepdims=True)
        gs_ref[1:2, :] = jnp.sum(da, axis=0, keepdims=True)
        dh = dy.astype(F32) + norm_back(da, gain[...], xhat, inv_s[:, 0:1])
        dh_ref[...] = dh
        dh = dh.astype(BF)
        o = o_ref[...]
        do = dot_nt(dh, wo[...]).astype(BF)
        do_ref[...] = do
        dd_ref[...] = (-(do.astype(F32) * o)).astype(BF)
        da_s[...] = dot_tn(o.astype(BF), dh)
        width = da.shape[1]
        part = width // 2
        for ref, core, mine in ((send_ref, ids[4], ids[2]), (keep_ref, ids[0], ids[1])):
            value = da_s[pl.ds(pl.multiple_of(core * part, part), part), :]
            shard_rows(ref, value, 2 * half_tiles * (width // CHUNKS), rows, mine)


def last_kernel(parts, x_ref, dh, gain, *refs):
    grads = []
    row = 0
    for part in range(parts):
        own, near, far = refs[3 * part : 3 * part + 3]
        at = slice(row, row + own.shape[0])
        row += own.shape[0]
        xhat, inv = normalize(x_ref[at, :].astype(F32))
        da = own[...] + near[0].astype(F32) + far[...].astype(F32)
        grads.append((dh[at, :] + norm_back(da, gain[...], xhat, inv)).astype(BF))
    store_by_bucket(refs[3 * parts :], jnp.concatenate(grads, axis=0))


def exchange(value, axis, distance, size):
    return lax.ppermute(value, axis, [(i, i ^ distance) for i in range(size)])


def add_low(first, *others):
    total = first.astype(F32)
    for other in others:
        total = total + other.astype(F32)
    return total.astype(BF)


def stage_permutes(sizes):
    rows = sizes["rows"]
    x, y, z_near, z_far = rows, 2, 2 * rows, 4 * rows
    pairs = [(x, y), (y, x), (z_near, z_far), (z_far, z_near)]
    extra = 8
    while extra < sizes["dp"]:
        pairs.append((extra * rows, extra * rows))
        extra *= 2
    total = rows * sizes["dp"]
    return [[(i, i ^ pair[i % 2]) for i in range(total)] for pair in pairs]


def send_all(value, perm):
    return lax.ppermute(value, ("dp", "rows"), perm)


def after(value, *others):
    return lax.optimization_barrier((value,) + others)[0]


class SumOverAll:
    def __init__(self, keep, send, tail, sizes):
        self.stages = stage_permutes(sizes)
        self.swap = functools.partial(exchange, axis="rows", distance=1, size=sizes["rows"])
        self.tail = tail
        self.block = (keep.shape[0] - tail) // CHUNKS
        self.size = CHUNKS * self.block
        self.keep = keep
        self.send = send

    def cut(self, value, start, stop):
        if not self.tail:
            return value[start:stop]
        return jnp.concatenate([value[start:stop], value[self.size :]], axis=0)

    def split(self, got):
        half = self.size // 2
        self.send = add_low(self.cut(self.keep, half, self.size), self.cut(got, half, self.size))
        self.keep = add_low(self.cut(self.keep, 0, half), self.cut(got, 0, half))
        self.size = half
        return self.send

    def reduce(self):
        got = yield self.send, self.swap
        for stage in self.stages[:2]:
            got = yield self.split(got), functools.partial(send_all, perm=stage)
        part = add_low(self.keep, got)
        for stage in self.stages[2:4]:
            got = yield part, functools.partial(send_all, perm=stage)
            part = add_low(part, got)
        for stage in self.stages[4:]:
            part = add_low(part, send_all(part, stage))
        block = part[: self.block]
        got = yield block, functools.partial(send_all, perm=self.stages[1])
        low = jnp.concatenate([block, got], axis=0)
        got = yield low, functools.partial(send_all, perm=self.stages[0])
        mine = jnp.concatenate([low, got, part[self.block :]], axis=0)
        other = yield mine, self.swap
        self.result = (mine, other)
        yield None, None

    def begin(self):
        self.run = self.reduce()
        return self.step(None)

    def step(self, got, *deps):
        self.operand, move = self.run.send(got)
        return None if move is None else move(after(self.operand, *deps))


def cost(micros):
    return pl.CostEstimate(flops=0, bytes_accessed=int(micros * 0.8e6), transcendentals=0)


def params():
    return pltpu.CompilerParams(vmem_limit_bytes=LIMIT * MIB)


def shards(sizes, *args):
    atoms, pairs, lengths = args[0:3], args[3:6], args[6:9]
    wq, wk, wv, wo, wu, wd = args[9:15]
    gain_one, shift_one, gain_two, shift_two = (v.reshape(1, -1) for v in args[15:19])
    dys, dpos = args[19:22], args[22:25]
    width = atoms[0].shape[-1]
    micros = atoms[0].shape[0]
    hidden_units = wu.shape[1]
    head_count = pairs[0].shape[2]
    heads = head_count * LANES // width
    scale = float((width // head_count) ** -0.5)
    groups = width // LANES
    ranks = sizes["rows"]

    rows_at = lax.axis_index("rows")
    core, y = rows_at % 2, rows_at // 2
    xa = lax.axis_index("dp") % 2
    order = (xa * 2 + y, y * 2 + xa)
    mine = jnp.where(core == 0, order[0], order[1])
    other = jnp.where(core == 0, order[1], order[0])
    ids = jnp.stack([core, mine, other, rows_at, core ^ 1]).astype(jnp.int32)

    layout = []
    start = 0
    for a in atoms:
        layout.append((start, a.shape[1], a.shape[2], a.shape[2] * ranks))
        start += a.shape[1] * a.shape[2]
    layout = tuple(layout)
    micro_rows = start
    local = micros * micro_rows

    def by_micro(arrays):
        return jnp.concatenate(
            [a.reshape(micros, -1, width) for a in arrays], axis=1
        ).reshape(local, width)

    x = by_micro(atoms)
    dy = by_micro(dys)
    pair = [p.reshape((-1,) + p.shape[2:]) for p in pairs]
    dpo = [p.reshape((-1,) + p.shape[2:]) for p in dpos]
    lens = [n.reshape(-1) for n in lengths]

    near_rows = functools.partial(exchange, axis="rows", distance=1, size=ranks)
    far_rows = functools.partial(exchange, axis="rows", distance=2, size=ranks)
    x1 = near_rows(x)
    x2 = far_rows(x)

    smem = pl.BlockSpec(memory_space=pltpu.SMEM)
    anywhere = pl.BlockSpec(memory_space=pl.ANY)

    def whole(shape):
        return pl.BlockSpec(tuple(shape), lambda *_: (0,) * len(shape))

    def call(kernel, name, micros, grid, operands, in_specs, outs, out_specs, scratch=(), **kw):
        return pl.pallas_call(
            kernel,
            grid_spec=pltpu.PrefetchScalarGridSpec(
                num_scalar_prefetch=1,
                grid=grid,
                in_specs=in_specs,
                out_specs=out_specs,
                scratch_shapes=list(scratch),
            ),
            out_shape=[jax.ShapeDtypeStruct(tuple(shape), kind) for shape, kind in outs],
            compiler_params=params(),
            cost_estimate=cost(micros),
            name=name,
            **kw,
        )(ids, *operands)

    gathered = (ranks, local, width)
    weights = [wq, wk, wv, gain_one, shift_one]

    def front(name, pieces, first, old):
        piece_spec = pl.BlockSpec((1, local, width), lambda t, ids: (ids[3] ^ (first + t), 0, 0))
        outs = [(gathered, BF)] * 4
        out_specs = [piece_spec] * 4
        if not old:
            outs = outs + [((local, width), BF)]
            out_specs = out_specs + [whole((local, width))]
        operands = list(pieces) + weights
        return call(
            functools.partial(front_kernel, len(pieces), len(old)),
            name,
            4,
            (len(pieces),),
            operands + list(old),
            [whole(v.shape) for v in operands] + [anywhere] * len(old),
            outs,
            out_specs,
            input_output_aliases={1 + len(operands) + i: i for i in range(len(old))},
        )

    *early, q = front("front_near", (x, x1), 0, [])
    x2 = after(x2, q)
    x3 = near_rows(x2)
    ks, vs, a1s, xhats = front("front_far", (x2, x3), 2, early)

    row_spec = pl.BlockSpec((micro_rows, width), lambda m, ids: (m, 0))
    rank_spec = pl.BlockSpec((ranks, micro_rows, width), lambda m, ids: (0, m, 0))
    pair_specs = [
        pl.BlockSpec((p.shape[0] // micros,) + p.shape[1:], lambda m, ids: (m, 0, 0, 0))
        for p in pair
    ]
    pair_outs = [(p.shape, BF) for p in pair]
    *res, o = call(
        lambda ids, *refs: attn_fwd_kernel(layout, groups, heads, scale, *refs),
        "attend",
        18,
        (micros,),
        [*lens, q, ks, vs, *pair],
        [smem] * 3 + [row_spec, rank_spec, rank_spec] + pair_specs,
        pair_outs * 2 + [((local, width), F32)],
        pair_specs * 2 + [row_spec],
    )
    pair_out, probs = res[0:3], res[3:6]

    tiles = 4
    tile = hidden_units // tiles
    half = tiles // 2

    def tile_at(t, ids):
        return (t + half * ids[4]) % tiles

    up_spec = pl.BlockSpec((width, tile), lambda t, ids: (0, tile_at(t, ids)))
    down_spec = pl.BlockSpec((tile, width), lambda t, ids: (tile_at(t, ids), 0))
    local_shape = (local, width)
    flat = whole(local_shape)
    ff_rows = (2 * half * tile + width // 2) // CHUNKS
    ff_shape = (CHUNKS * ff_rows, width)
    atom_outs = [((micros, a.shape[1] * a.shape[2], width), BF) for a in atoms]
    atom_specs = [whole(shape) for shape, _ in atom_outs]
    *atoms_out, dh, do, dd, gs_two, ff_send, ff_keep = call(
        functools.partial(dense_kernel, tiles, ff_rows),
        "dense",
        16,
        (tiles,),
        [x, o, dy, wo, wu, wd, gain_two, shift_two],
        [flat, flat, flat, whole(wo.shape), up_spec, down_spec] + [whole((1, width))] * 2,
        atom_outs
        + [(local_shape, F32), (local_shape, BF), (local_shape, BF), ((8, width), F32)]
        + [(ff_shape, BF)] * 2,
        atom_specs + [flat, flat, flat, whole((8, width)), whole(ff_shape), whole(ff_shape)],
        [
            pltpu.VMEM(local_shape, BF),
            pltpu.VMEM(local_shape, F32),
            pltpu.VMEM(local_shape, F32),
            pltpu.VMEM((local, LANES), F32),
            pltpu.VMEM(local_shape, F32),
        ],
    )
    ff = SumOverAll(ff_keep, ff_send, 0, sizes)
    moving = ff.step(ff.begin())
    do = after(do, ff.operand)

    dls = []
    dqs, dks, dvs = [], [], []
    for name, buckets in (("attend_back_big", (0,)), ("attend_back_rest", (1, 2))):
        here = tuple(layout[b] for b in buckets)
        rows_here = sum(mols * rows for _, mols, rows, _ in here)
        specs = [pair_specs[b] for b in buckets]
        key_spec = pl.BlockSpec((width, rows_here * ranks), lambda m, ids: (0, m))
        key_out = ((width, micros * rows_here * ranks), BF)
        res = call(
            lambda ids, *refs, here=here: attn_bwd_kernel(here, groups, heads, scale, *refs),
            name,
            15,
            (micros,),
            [q, do, dd, ks, vs] + [probs[b] for b in buckets] + [dpo[b] for b in buckets],
            [row_spec] * 3 + [rank_spec] * 2 + specs * 2,
            [pair_outs[b] for b in buckets]
            + [((micros * rows_here, width), BF), key_out, key_out],
            specs
            + [pl.BlockSpec((rows_here, width), lambda m, ids: (m, 0)), key_spec, key_spec],
        )
        dls += res[: len(buckets)]
        for values, value in zip((dqs, dks, dvs), res[len(buckets) :]):
            values.append(value)
        moving = ff.step(after(moving, dqs[-1]))
        if len(dqs) == 1:
            do = after(do, ff.operand)
        else:
            dqs[-1] = after(dqs[-1], ff.operand)

    share = (width + width // 2) // CHUNKS
    w_shape = (CHUNKS * share + 16, width)
    operands = [*dqs, *dks, *dvs, a1s, xhats, wq, wk, wv, gs_two]
    own, keep, send, w_send, w_keep = call(
        functools.partial(back_kernel, layout, share, len(dqs)),
        "back",
        9,
        (micros,),
        operands,
        [pl.BlockSpec((v.shape[0] // micros, width), lambda m, ids: (m, 0)) for v in dqs]
        + [pl.BlockSpec((width, v.shape[1] // micros), lambda m, ids: (0, m)) for v in dks + dvs]
        + [rank_spec] * 2
        + [whole(v.shape) for v in operands[-4:]],
        [
            (local_shape, F32),
            (local_shape, BF),
            ((2,) + local_shape, BF),
            (w_shape, BF),
            (w_shape, BF),
        ],
        [
            row_spec,
            row_spec,
            pl.BlockSpec((2, micro_rows, width), lambda m, ids: (0, m, 0)),
            whole(w_shape),
            whole(w_shape),
        ],
        [
            pltpu.VMEM((width, width), F32),
            pltpu.VMEM((width, width), F32),
            pltpu.VMEM((width, width), F32),
            pltpu.VMEM((8, width), F32),
            pltpu.VMEM((ranks * micro_rows, width), F32),
        ],
    )
    moving = ff.step(after(moving, w_send))
    w_send = after(w_send, ff.operand)
    w_sum = SumOverAll(w_keep, w_send, 16, sizes)
    w = w_sum.begin()
    near = near_rows(after(send, ff.operand))
    w = w_sum.step(w)
    near = after(near, w_sum.operand)
    far = far_rows(add_low(keep, near[1]))
    w = w_sum.step(w)
    moving = ff.step(after(moving, w_sum.operand))
    w = w_sum.step(w)
    w = w_sum.step(w)
    moving = ff.step(after(moving, w_sum.operand))
    w = w_sum.step(w)
    w = w_sum.step(w)
    fars = [(own, near, after(far, w_sum.operand))]
    last_args = [x, dh, gain_one] + [v for triple in fars for v in triple]
    grad_atoms = call(
        lambda ids, *refs: last_kernel(len(fars), *refs),
        "last",
        2,
        (1,),
        last_args,
        [whole(v.shape) for v in last_args],
        atom_outs,
        atom_specs,
    )
    moving = ff.step(after(moving, grad_atoms[0]))
    ff.step(moving)

    def ordered(ref, at, size, rows, mine):
        return jnp.concatenate(
            [
                ref[pl.ds(pl.multiple_of((c ^ mine) * rows + at, 16), size), :].astype(F32)
                for c in range(CHUNKS)
            ],
            axis=0,
        )

    def finish_ff(ids, mine_ref, other_ref, gu, gd, go):
        step = pl.program_id(0)
        own_tile = (step // half) == ids[0]
        size = width // CHUNKS
        at = (step % half) * 2 * size

        def put(ref, mine):
            gu[...] = ordered(ref, at, size, ff_rows, mine)
            gd[...] = ordered(ref, at + size, size, ff_rows, mine)

            @pl.when(step % half == 0)
            def _():
                go[...] = ordered(ref, 2 * half * size, size // 2, ff_rows, mine)

        pl.when(own_tile)(lambda: put(mine_ref, ids[1]))
        pl.when(jnp.logical_not(own_tile))(lambda: put(other_ref, ids[2]))

    grad_up, grad_down, go = call(
        finish_ff,
        "finish_ff",
        6,
        (tiles,),
        list(ff.result),
        [whole(ff_shape)] * 2,
        [(wu.shape, F32), (wd.shape, F32), (wo.shape, F32)],
        [
            pl.BlockSpec((width, tile), lambda t, ids: (0, t)),
            pl.BlockSpec((tile, width), lambda t, ids: (t, 0)),
            pl.BlockSpec((width // 2, width), lambda t, ids: (t // half, 0)),
        ],
    )
    w = w_sum.step(after(w, grad_down))
    w_sum.step(w)

    def finish_rest(ids, mine_ref, other_ref, gq_out, gk_out, gv_out, gs_out):
        size = width // CHUNKS

        def put(zero, zero_at, one, one_at):
            gq_out[...] = ordered(zero, 0, size, share, zero_at)
            gk_out[...] = ordered(one, 0, size, share, one_at).T
            gv_out[:, : width // 2] = ordered(zero, size, size // 2, share, zero_at).T
            gv_out[:, width // 2 :] = ordered(one, size, size // 2, share, one_at).T
            gs_out[...] = zero[CHUNKS * share :, :].astype(F32)

        pl.when(ids[0] == 0)(lambda: put(mine_ref, ids[1], other_ref, ids[2]))
        pl.when(ids[0] == 1)(lambda: put(other_ref, ids[2], mine_ref, ids[1]))

    gq, gk, gv, gs = call(
        finish_rest,
        "finish_rest",
        3,
        (1,),
        list(w_sum.result),
        [whole(w_shape)] * 2,
        [(wq.shape, F32)] * 3 + [((16, width), F32)],
        [whole(wq.shape)] * 3 + [whole((16, width))],
    )

    return (
        *[v.reshape(a.shape) for v, a in zip(atoms_out, atoms)],
        *[v.reshape(a.shape) for v, a in zip(pair_out, pairs)],
        *[v.reshape(a.shape) for v, a in zip(grad_atoms, atoms)],
        *[v.reshape(a.shape) for v, a in zip(dls, pairs)],
        gq,
        gk,
        gv,
        go,
        grad_up,
        grad_down,
        gs[0],
        gs[1],
        gs[2],
        gs[3],
    )


def solution(mesh):
    atom = P(None, "dp", "rows", None)
    pair = P(None, "dp", None, "rows", None)
    length = P(None, "dp")
    in_specs = (
        (atom,) * 3 + (pair,) * 3 + (length,) * 3 + (P(),) * 10 + (atom,) * 3 + (pair,) * 3
    )
    out_specs = (atom,) * 3 + (pair,) * 3 + (atom,) * 3 + (pair,) * 3 + (P(),) * 10
    body = functools.partial(shards, dict(mesh.shape))
    return jax.shard_map(
        body, mesh=mesh, in_specs=in_specs, out_specs=out_specs, check_vma=False
    )
```

```python
import functools

import jax
import jax.numpy as jnp
from jax import lax
from jax.experimental import pallas as pl
from jax.experimental.pallas import tpu as pltpu
from jax.sharding import PartitionSpec as P

EPSILON = 1e-05
MASKED = -1e30
BF = jnp.bfloat16
F32 = jnp.float32
LANES = 128
GELU_C = 0.7978845608028654
GELU_A = 0.044715
MIB = 1 << 20
CHUNKS = 4
LIMIT = 60


def dot_nn(a, b):
    return lax.dot_general(a, b, (((1,), (0,)), ((), ())), preferred_element_type=F32)


def dot_nt(a, b):
    return lax.dot_general(a, b, (((1,), (1,)), ((), ())), preferred_element_type=F32)


def dot_tn(a, b):
    return lax.dot_general(a, b, (((0,), (0,)), ((), ())), preferred_element_type=F32)


def normalize(x):
    centred = x - jnp.mean(x, axis=-1, keepdims=True)
    spread = jnp.mean(centred * centred, axis=-1, keepdims=True)
    inv = lax.rsqrt(spread + EPSILON)
    return centred * inv, inv


def norm_back(grad, gain, xhat, inv):
    g = grad * gain
    return inv * (
        g
        - jnp.mean(g, axis=-1, keepdims=True)
        - xhat * jnp.mean(g * xhat, axis=-1, keepdims=True)
    )


def front_kernel(ids, x0, x1, wq, wk, wv, gain, shift, q_out, *outs):
    for piece, x_ref in enumerate((x0, x1)):

        @pl.when(pl.program_id(0) == piece)
        def _(piece=piece, x_ref=x_ref):
            a1 = front_rows(x_ref[...], gain, shift, wk, wv, [out.at[0] for out in outs])
            if piece == 0:
                q_out[...] = dot_nn(a1, wq[...]).astype(BF)


def front_rows(x, gain, shift, wk, wv, outs):
    xhat, _ = normalize(x.astype(F32))
    a1 = (xhat * gain[...] + shift[...]).astype(BF)
    outs[0][...] = dot_nn(a1, wk[...]).astype(BF)
    outs[1][...] = dot_nn(a1, wv[...]).astype(BF)
    outs[2][...] = a1
    outs[3][...] = xhat.astype(BF)
    return a1


def head_mask(heads, first):
    lane = lax.broadcasted_iota(jnp.int32, (1, LANES), 1) // (LANES // heads)
    return lane == first


def stacked(block, heads, first, count):
    zero = jnp.zeros_like(block)
    return jnp.concatenate(
        [jnp.where(head_mask(heads, first + t), block, zero) for t in range(count)], axis=0
    )


def unstacked(total, product, heads, first, count, rows):
    for t in range(count):
        part = product[t * rows : (t + 1) * rows]
        total = total + jnp.where(head_mask(heads, first + t), part, 0.0)
    return total


def key_rows(ref, me, start, rows, lanes):
    return jnp.concatenate(
        [ref[me ^ r, start : start + rows, lanes] for r in range(ref.shape[0])], axis=0
    )


def attn_fwd_kernel(layout, groups, heads, scale, ids, *refs):
    lens, q_ref, far_xs, weights, pairs = refs[0:3], refs[3], refs[4:6], refs[6:10], refs[10:13]
    k_near, v_near = refs[13:15]
    pouts, ps, o_ref, fronts, (k_ref, v_ref) = (
        refs[17:20], refs[20:23], refs[23], refs[24:28], refs[28:30]
    )
    wk, wv, gain, shift = weights
    me = ids[3]
    near = k_near.shape[0]
    for i in range(near):
        k_ref[i] = k_near[i]
        v_ref[i] = v_near[i]
    for i, x_ref in enumerate(far_xs):
        front_rows(x_ref[...], gain, shift, wk, wv, [out.at[i] for out in fronts])
        k_ref[near + i] = fronts[0][i]
        v_ref[near + i] = fronts[1][i]
    for (start, mols, rows, slots), len_ref, pair_ref, pout_ref, p_ref in zip(
        layout, lens, pairs, pouts, ps
    ):
        count = min(heads, max(1, 512 // rows))
        for mol in range(mols):
            length = len_ref[pl.program_id(0) * mols + mol]
            key_at = lax.broadcasted_iota(jnp.int32, (1, 1, slots), 2)
            mask = jnp.where(key_at < length, 0.0, MASKED)
            at_row = start + mol * rows
            for group in range(groups):
                lanes = slice(group * LANES, (group + 1) * LANES)
                q = q_ref[at_row : at_row + rows, lanes]
                k = key_rows(k_ref, me, at_row, rows, lanes)
                v = key_rows(v_ref, me, at_row, rows, lanes)
                total = jnp.zeros((rows, LANES), F32)
                for first in range(0, heads, count):
                    at = slice(group * heads + first, group * heads + first + count)
                    s = dot_nt(stacked(q, heads, first, count), k)
                    s = s.reshape(count, rows, slots) * scale + pair_ref[mol, at].astype(F32)
                    pout_ref[mol, at] = s.astype(BF)
                    s = s + mask
                    e = jnp.exp(s - jnp.max(s, axis=-1, keepdims=True))
                    p = (e * (1.0 / jnp.sum(e, axis=-1, keepdims=True))).astype(BF)
                    p_ref[mol, at] = p
                    pv = dot_nn(p.reshape(count * rows, slots), v)
                    total = unstacked(total, pv, heads, first, count, rows)
                o_ref[at_row : at_row + rows, lanes] = total


def attn_bwd_kernel(layout, groups, heads, scale, ids, *refs):
    me = ids[3]
    count_of = len(layout)
    q_ref, do_ref, dd_ref, k_ref, v_ref = refs[0:5]
    ps, dpos = refs[5 : 5 + count_of], refs[5 + count_of : 5 + 2 * count_of]
    dls = refs[5 + 2 * count_of : 5 + 3 * count_of]
    dq_ref, dk_ref, dv_ref = refs[5 + 3 * count_of :]
    ranks = k_ref.shape[0]
    origin = layout[0][0]
    for (start, mols, rows, slots), p_ref, dpo_ref, dl_ref in zip(layout, ps, dpos, dls):
        count = min(heads, max(1, 1024 // rows))
        base = (start - origin) * ranks
        for group in range(groups):
            lanes = slice(group * LANES, (group + 1) * LANES)
            dk_all = []
            dv_all = []
            for mol in range(mols):
                at_row = start - origin + mol * rows
                rs = slice(at_row, at_row + rows)
                q = q_ref[rs, lanes]
                do = do_ref[rs, lanes]
                dd = dd_ref[rs, lanes]
                k = key_rows(k_ref, me, at_row, rows, lanes)
                v = key_rows(v_ref, me, at_row, rows, lanes)
                v_aug = jnp.concatenate([v, jnp.ones_like(v)], axis=1)
                total = jnp.zeros((rows, LANES), F32)
                dk = jnp.zeros((LANES, slots), F32)
                dv = jnp.zeros((LANES, slots), F32)
                for first in range(0, heads, count):
                    at = slice(group * heads + first, group * heads + first + count)
                    do_s = stacked(do, heads, first, count)
                    t = dot_nt(
                        jnp.concatenate([do_s, stacked(dd, heads, first, count)], axis=1), v_aug
                    )
                    p = p_ref[mol, at]
                    dl = p.astype(F32) * t.reshape(count, rows, slots)
                    dl = (dl + dpo_ref[mol, at].astype(F32)).astype(BF)
                    dl_ref[mol, at] = dl
                    dl = dl.reshape(count * rows, slots)
                    total = unstacked(total, dot_nn(dl, k), heads, first, count, rows)
                    dk = dk + dot_tn(stacked(q, heads, first, count), dl)
                    dv = dv + dot_tn(do_s, p.reshape(count * rows, slots))
                dq_ref[rs, lanes] = (total * scale).astype(BF)
                dk_all.append((dk * scale).astype(BF))
                dv_all.append(dv.astype(BF))
            dk_ref[lanes, base : base + mols * slots] = jnp.concatenate(dk_all, axis=1)
            dv_ref[lanes, base : base + mols * slots] = jnp.concatenate(dv_all, axis=1)


def back_kernel(layout, share, parts, ids, *refs):
    dqs, dks, dvs = (refs[i * parts : (i + 1) * parts] for i in range(3))
    a_ref, h_ref, wq, wk, wv, gs_two = refs[3 * parts : 3 * parts + 6]
    own_ref, keep_ref, send_ref, w_send, w_keep = refs[3 * parts + 6 : 3 * parts + 11]
    gq_ref, gk_ref, gv_ref, gs_ref, da_s = refs[3 * parts + 11 :]
    step = pl.program_id(0)
    me = ids[3]
    ranks = a_ref.shape[0]

    @pl.when(step == 0)
    def _():
        for ref in (gq_ref, gk_ref, gv_ref, gs_ref):
            ref[...] = jnp.zeros_like(ref)

    def molecules(ref):
        return jnp.concatenate(
            [
                key_rows(ref, me, start + mol * rows, rows, slice(None))
                for start, mols, rows, slots in layout
                for mol in range(mols)
            ],
            axis=0,
        )

    dq = jnp.concatenate([ref[...] for ref in dqs], axis=0)
    dk = jnp.concatenate([ref[...] for ref in dks], axis=1)
    dv = jnp.concatenate([ref[...] for ref in dvs], axis=1)
    a1 = molecules(a_ref)
    gk_ref[...] += dot_nn(dk, a1)
    gv_ref[...] += dot_nn(dv, a1)
    gq_ref[...] += dot_tn(a_ref[0], dq)
    daq = dot_nt(dq, wq[...])
    across = (((0,), (1,)), ((), ()))
    da = lax.dot_general(dk, wk[...], across, preferred_element_type=F32) + lax.dot_general(
        dv, wv[...], across, preferred_element_type=F32
    )
    da_s[...] = da
    gs_ref[0:1, :] += jnp.sum(da * molecules(h_ref).astype(F32), axis=0, keepdims=True) + jnp.sum(
        daq * h_ref[0].astype(F32), axis=0, keepdims=True
    )
    gs_ref[1:2, :] += jnp.sum(da, axis=0, keepdims=True) + jnp.sum(daq, axis=0, keepdims=True)
    for piece in range(ranks):
        for start, mols, rows, slots in layout:
            for mol in range(mols):
                at = pl.multiple_of(start * ranks + mol * slots + (me ^ piece) * rows, rows)
                value = da_s[pl.ds(at, rows), :]
                to = slice(start + mol * rows, start + (mol + 1) * rows)
                if piece == 0:
                    own_ref[to, :] = value + daq[to]
                elif piece == 2:
                    keep_ref[to, :] = value.astype(BF)
                else:
                    send_ref[piece // 2, to, :] = value.astype(BF)

    @pl.when(step == pl.num_programs(0) - 1)
    def _():
        width = gq_ref.shape[1]
        size = width // CHUNKS
        half = width // 2
        gains = jnp.concatenate(
            [gs_ref[0:2, :], gs_two[0:2, :], jnp.zeros((12, width), F32)], axis=0
        ).astype(BF)
        for value in (0, 1):

            @pl.when(ids[0] == value)
            def _(value=value):
                for ref, owner, mine in ((w_keep, value, ids[1]), (w_send, 1 - value, ids[2])):
                    shard_rows(ref, (gk_ref if owner else gq_ref)[...], 0, share, mine)
                    gv = gv_ref[owner * half : (owner + 1) * half, :]
                    shard_rows(ref, gv, size, share, mine)

        w_keep[CHUNKS * share :, :] = gains
        w_send[CHUNKS * share :, :] = gains


def shard_rows(ref, value, at, rows, mine):
    size = value.shape[0] // CHUNKS
    for chunk in range(CHUNKS):
        to = pl.multiple_of((chunk ^ mine) * rows + at, 16)
        ref[pl.ds(to, size), :] = value[chunk * size : (chunk + 1) * size].astype(ref.dtype)


def store_by_bucket(refs, value):
    row = 0
    for micro in range(refs[0].shape[0]):
        for ref in refs:
            ref[micro] = value[row : row + ref.shape[1]]
            row += ref.shape[1]


def store_tile(send_ref, keep_ref, value, step, at, half_tiles, rows, ids):
    size = value.shape[0] // CHUNKS

    @pl.when(step < half_tiles)
    def _():
        shard_rows(send_ref, value, (2 * step + at) * size, rows, ids[2])

    @pl.when(step >= half_tiles)
    def _():
        shard_rows(keep_ref, value, (2 * (step - half_tiles) + at) * size, rows, ids[1])


def dense_kernel(
    tiles, rows, ids, x_ref, o_ref, dy_ref, wo, wu, wd, gain, shift,
    yb, ym, ys, dh_ref, do_ref, dd_ref, gs_ref, send_ref, keep_ref,
    a2_s, y_s, xhat_s, inv_s, da_s,
):
    step = pl.program_id(0)
    half_tiles = tiles // 2

    @pl.when(step == 0)
    def _():
        hidden = x_ref[...].astype(F32) + dot_nn(o_ref[...].astype(BF), wo[...])
        xhat, inv = normalize(hidden)
        y_s[...] = hidden
        xhat_s[...] = xhat
        inv_s[...] = jnp.broadcast_to(inv, inv_s.shape)
        a2_s[...] = (xhat * gain[...] + shift[...]).astype(BF)
        da_s[...] = jnp.zeros_like(da_s)

    dy = dy_ref[...]
    u = dot_nn(a2_s[...], wu[...])
    u2 = u * u
    th = jnp.tanh(GELU_C * (u + GELU_A * u * u2))
    half = 0.5 * (1.0 + th)
    g = (u * half).astype(BF)
    slope = half + 0.5 * u * (1.0 - th * th) * (GELU_C * (1.0 + 3.0 * GELU_A * u2))
    y_s[...] += dot_nn(g, wd[...])
    store_tile(send_ref, keep_ref, dot_tn(g, dy), step, 1, half_tiles, rows, ids)
    du = (dot_nt(dy, wd[...]) * slope).astype(BF)
    store_tile(send_ref, keep_ref, dot_tn(a2_s[...], du), step, 0, half_tiles, rows, ids)
    da_s[...] += dot_nt(du, wu[...])

    @pl.when(step == tiles - 1)
    def _():
        store_by_bucket((yb, ym, ys), y_s[...].astype(BF))
        da = da_s[...]
        xhat = xhat_s[...]
        gs_ref[0:1, :] = jnp.sum(da * xhat, axis=0, keepdims=True)
        gs_ref[1:2, :] = jnp.sum(da, axis=0, keepdims=True)
        dh = dy.astype(F32) + norm_back(da, gain[...], xhat, inv_s[:, 0:1])
        dh_ref[...] = dh
        dh = dh.astype(BF)
        o = o_ref[...]
        do = dot_nt(dh, wo[...]).astype(BF)
        do_ref[...] = do
        dd_ref[...] = (-(do.astype(F32) * o)).astype(BF)
        da_s[...] = dot_tn(o.astype(BF), dh)
        width = da.shape[1]
        part = width // 2
        for ref, core, mine in ((send_ref, ids[4], ids[2]), (keep_ref, ids[0], ids[1])):
            value = da_s[pl.ds(pl.multiple_of(core * part, part), part), :]
            shard_rows(ref, value, 2 * half_tiles * (width // CHUNKS), rows, mine)


def last_kernel(parts, x_ref, dh, gain, *refs):
    grads = []
    row = 0
    for part in range(parts):
        own, near, far = refs[3 * part : 3 * part + 3]
        at = slice(row, row + own.shape[0])
        row += own.shape[0]
        xhat, inv = normalize(x_ref[at, :].astype(F32))
        da = own[...] + near[0].astype(F32) + far[...].astype(F32)
        grads.append((dh[at, :] + norm_back(da, gain[...], xhat, inv)).astype(BF))
    store_by_bucket(refs[3 * parts :], jnp.concatenate(grads, axis=0))


def exchange(value, axis, distance, size):
    return lax.ppermute(value, axis, [(i, i ^ distance) for i in range(size)])


def add_low(first, *others):
    total = first.astype(F32)
    for other in others:
        total = total + other.astype(F32)
    return total.astype(BF)


def stage_permutes(sizes):
    rows = sizes["rows"]
    x, y, z_near, z_far = rows, 2, 2 * rows, 4 * rows
    pairs = [(x, y), (y, x), (z_near, z_far), (z_far, z_near)]
    extra = 8
    while extra < sizes["dp"]:
        pairs.append((extra * rows, extra * rows))
        extra *= 2
    total = rows * sizes["dp"]
    return [[(i, i ^ pair[i % 2]) for i in range(total)] for pair in pairs]


def send_all(value, perm):
    return lax.ppermute(value, ("dp", "rows"), perm)


def after(value, *others):
    return lax.optimization_barrier((value,) + others)[0]


def after_all(values, *others):
    return list(lax.optimization_barrier((*values, *others)))[: len(values)]


class SumOverAll:
    def __init__(self, keep, send, tail, sizes):
        self.stages = stage_permutes(sizes)
        self.swap = functools.partial(exchange, axis="rows", distance=1, size=sizes["rows"])
        self.tail = tail
        self.block = (keep.shape[0] - tail) // CHUNKS
        self.size = CHUNKS * self.block
        self.terms = [keep]
        self.send = send

    def cut(self, value, start, stop):
        if not self.tail:
            return value[start:stop]
        return jnp.concatenate([value[start:stop], value[value.shape[0] - self.tail :]], axis=0)

    def split(self, got):
        self.terms.append(got)
        half = self.size // 2
        send = add_low(*[self.cut(v, half, self.size) for v in self.terms])
        self.size = half
        return send

    def reduce(self):
        got = yield self.send, self.swap
        for stage in self.stages[:2]:
            got = yield self.split(got), functools.partial(send_all, perm=stage)
        part = add_low(*[self.cut(v, 0, self.size) for v in self.terms + [got]])
        for stage in self.stages[2:4]:
            got = yield part, functools.partial(send_all, perm=stage)
            part = add_low(part, got)
        for stage in self.stages[4:]:
            part = add_low(part, send_all(part, stage))
        block = part[: self.block]
        self.own = [part]
        self.other = [self.swap(part)]
        second = yield block, functools.partial(send_all, perm=self.stages[1])
        self.own.append(second)
        self.other.append(self.swap(second))
        low = jnp.concatenate([block, second], axis=0)
        high = yield low, functools.partial(send_all, perm=self.stages[0])
        self.own.append(high)
        got = yield high, self.swap
        self.other.append(got)
        yield None, None

    def begin(self):
        self.run = self.reduce()
        return self.step(None)

    def step(self, got, *deps):
        self.operand, move = self.run.send(got)
        return None if move is None else move(after(self.operand, *deps))


def cost(micros):
    return pl.CostEstimate(flops=0, bytes_accessed=int(micros * 0.8e6), transcendentals=0)


def params():
    return pltpu.CompilerParams(vmem_limit_bytes=LIMIT * MIB)


def shards(sizes, *args):
    atoms, pairs, lengths = args[0:3], args[3:6], args[6:9]
    wq, wk, wv, wo, wu, wd = args[9:15]
    gain_one, shift_one, gain_two, shift_two = (v.reshape(1, -1) for v in args[15:19])
    dys, dpos = args[19:22], args[22:25]
    width = atoms[0].shape[-1]
    micros = atoms[0].shape[0]
    hidden_units = wu.shape[1]
    head_count = pairs[0].shape[2]
    heads = head_count * LANES // width
    scale = float((width // head_count) ** -0.5)
    groups = width // LANES
    ranks = sizes["rows"]

    rows_at = lax.axis_index("rows")
    core, y = rows_at % 2, rows_at // 2
    xa = lax.axis_index("dp") % 2
    order = (xa * 2 + y, y * 2 + xa)
    mine = jnp.where(core == 0, order[0], order[1])
    other = jnp.where(core == 0, order[1], order[0])
    ids = jnp.stack([core, mine, other, rows_at, core ^ 1]).astype(jnp.int32)

    layout = []
    start = 0
    for a in atoms:
        layout.append((start, a.shape[1], a.shape[2], a.shape[2] * ranks))
        start += a.shape[1] * a.shape[2]
    layout = tuple(layout)
    micro_rows = start
    local = micros * micro_rows

    def by_micro(arrays):
        return jnp.concatenate(
            [a.reshape(micros, -1, width) for a in arrays], axis=1
        ).reshape(local, width)

    x = by_micro(atoms)
    dy = by_micro(dys)
    pair = [p.reshape((-1,) + p.shape[2:]) for p in pairs]
    dpo = [p.reshape((-1,) + p.shape[2:]) for p in dpos]
    lens = [n.reshape(-1) for n in lengths]

    near_rows = functools.partial(exchange, axis="rows", distance=1, size=ranks)
    far_rows = functools.partial(exchange, axis="rows", distance=2, size=ranks)
    x2 = far_rows(x)
    x1 = near_rows(x)

    smem = pl.BlockSpec(memory_space=pltpu.SMEM)
    anywhere = pl.BlockSpec(memory_space=pl.ANY)

    def whole(shape):
        return pl.BlockSpec(tuple(shape), lambda *_: (0,) * len(shape))

    def call(kernel, name, micros, grid, operands, in_specs, outs, out_specs, scratch=(), **kw):
        return pl.pallas_call(
            kernel,
            grid_spec=pltpu.PrefetchScalarGridSpec(
                num_scalar_prefetch=1,
                grid=grid,
                in_specs=in_specs,
                out_specs=out_specs,
                scratch_shapes=list(scratch),
            ),
            out_shape=[jax.ShapeDtypeStruct(tuple(shape), kind) for shape, kind in outs],
            compiler_params=params(),
            cost_estimate=cost(micros),
            name=name,
            **kw,
        )(ids, *operands)

    near = 2
    gathered = ((ranks, local, width), BF)
    operands = [x, x1, wq, wk, wv, gain_one, shift_one]
    q, *fronts = call(
        front_kernel,
        "front",
        4,
        (near,),
        operands,
        [whole(v.shape) for v in operands],
        [((local, width), BF)] + [gathered] * 4,
        [whole((local, width))] + [pl.BlockSpec((1, local, width), lambda t, ids: (t, 0, 0))] * 4,
    )
    x2 = after(x2, q, dy, *lens)
    x3 = near_rows(x2)

    row_spec = pl.BlockSpec((micro_rows, width), lambda m, ids: (m, 0))
    rank_spec = pl.BlockSpec((ranks, micro_rows, width), lambda m, ids: (0, m, 0))
    pair_specs = [
        pl.BlockSpec((p.shape[0] // micros,) + p.shape[1:], lambda m, ids: (m, 0, 0, 0))
        for p in pair
    ]
    pair_outs = [(p.shape, BF) for p in pair]
    near_spec = pl.BlockSpec((near, micro_rows, width), lambda m, ids: (0, m, 0))
    far_spec = pl.BlockSpec((ranks - near, micro_rows, width), lambda m, ids: (1, m, 0))
    operands = [*lens, q, x2, x3, wk, wv, gain_one, shift_one, *pair, *fronts]
    res = call(
        functools.partial(attn_fwd_kernel, layout, groups, heads, scale),
        "attend",
        18,
        (micros,),
        operands,
        [smem] * 3
        + [row_spec] * 3
        + [whole(v.shape) for v in operands[6:10]]
        + pair_specs
        + [near_spec] * 2
        + [anywhere] * 2,
        pair_outs * 2 + [((local, width), F32)] + [gathered] * 4,
        pair_specs * 2 + [row_spec] + [far_spec] * 4,
        [pltpu.VMEM((ranks, micro_rows, width), BF)] * 2,
        input_output_aliases={14 + i: 7 + i for i in range(4)},
    )
    o = res[6]
    ks, vs, a1s, xhats = res[7:11]
    pair_out, probs = res[0:3], res[3:6]

    tiles = 4
    tile = hidden_units // tiles
    half = tiles // 2

    def tile_at(t, ids):
        return (t + half * ids[4]) % tiles

    up_spec = pl.BlockSpec((width, tile), lambda t, ids: (0, tile_at(t, ids)))
    down_spec = pl.BlockSpec((tile, width), lambda t, ids: (tile_at(t, ids), 0))
    local_shape = (local, width)
    flat = whole(local_shape)
    ff_rows = (2 * half * tile + width // 2) // CHUNKS
    ff_shape = (CHUNKS * ff_rows, width)
    atom_outs = [((micros, a.shape[1] * a.shape[2], width), BF) for a in atoms]
    atom_specs = [whole(shape) for shape, _ in atom_outs]
    *atoms_out, dh, do, dd, gs_two, ff_send, ff_keep = call(
        functools.partial(dense_kernel, tiles, ff_rows),
        "dense",
        16,
        (tiles,),
        [x, o, dy, wo, wu, wd, gain_two, shift_two],
        [flat, flat, flat, whole(wo.shape), up_spec, down_spec] + [whole((1, width))] * 2,
        atom_outs
        + [(local_shape, F32), (local_shape, BF), (local_shape, BF), ((8, width), F32)]
        + [(ff_shape, BF)] * 2,
        atom_specs + [flat, flat, flat, whole((8, width)), whole(ff_shape), whole(ff_shape)],
        [
            pltpu.VMEM(local_shape, BF),
            pltpu.VMEM(local_shape, F32),
            pltpu.VMEM(local_shape, F32),
            pltpu.VMEM((local, LANES), F32),
            pltpu.VMEM(local_shape, F32),
        ],
    )
    ff = SumOverAll(ff_keep, ff_send, 0, sizes)
    moving = ff.step(ff.begin())
    do = after(do, ff.operand)

    dls = []
    dqs, dks, dvs = [], [], []
    for name, buckets in (("attend_back_big", (0,)), ("attend_back_rest", (1, 2))):
        here = tuple(layout[b] for b in buckets)
        rows_here = sum(mols * rows for _, mols, rows, _ in here)
        specs = [pair_specs[b] for b in buckets]
        per, at = micro_rows // rows_here, here[0][0] // rows_here
        rows_spec = pl.BlockSpec(
            (rows_here, width), lambda m, ids, per=per, at=at: (m * per + at, 0)
        )
        ranks_spec = pl.BlockSpec(
            (ranks, rows_here, width), lambda m, ids, per=per, at=at: (0, m * per + at, 0)
        )
        key_spec = pl.BlockSpec((width, rows_here * ranks), lambda m, ids: (0, m))
        key_out = ((width, micros * rows_here * ranks), BF)
        res = call(
            functools.partial(attn_bwd_kernel, here, groups, heads, scale),
            name,
            15,
            (micros,),
            [q, do, dd, ks, vs] + [probs[b] for b in buckets] + [dpo[b] for b in buckets],
            [rows_spec] * 3 + [ranks_spec] * 2 + specs * 2,
            [pair_outs[b] for b in buckets]
            + [((micros * rows_here, width), BF), key_out, key_out],
            specs
            + [pl.BlockSpec((rows_here, width), lambda m, ids: (m, 0)), key_spec, key_spec],
        )
        dls += res[: len(buckets)]
        for values, value in zip((dqs, dks, dvs), res[len(buckets) :]):
            values.append(value)
        moving = ff.step(after(moving, dqs[-1]))
        if len(dqs) == 1:
            do = after(do, ff.operand)
        else:
            dqs[-1] = after(dqs[-1], ff.operand)

    share = (width + width // 2) // CHUNKS
    w_shape = (CHUNKS * share + 16, width)
    operands = [*dqs, *dks, *dvs, a1s, xhats, wq, wk, wv, gs_two]
    own, keep, send, w_send, w_keep = call(
        functools.partial(back_kernel, layout, share, len(dqs)),
        "back",
        9,
        (micros,),
        operands,
        [pl.BlockSpec((v.shape[0] // micros, width), lambda m, ids: (m, 0)) for v in dqs]
        + [pl.BlockSpec((width, v.shape[1] // micros), lambda m, ids: (0, m)) for v in dks + dvs]
        + [rank_spec] * 2
        + [whole(v.shape) for v in operands[-4:]],
        [
            (local_shape, F32),
            (local_shape, BF),
            ((2,) + local_shape, BF),
            (w_shape, BF),
            (w_shape, BF),
        ],
        [
            row_spec,
            row_spec,
            pl.BlockSpec((2, micro_rows, width), lambda m, ids: (0, m, 0)),
            whole(w_shape),
            whole(w_shape),
        ],
        [
            pltpu.VMEM((width, width), F32),
            pltpu.VMEM((width, width), F32),
            pltpu.VMEM((width, width), F32),
            pltpu.VMEM((8, width), F32),
            pltpu.VMEM((ranks * micro_rows, width), F32),
        ],
    )
    moving = ff.step(after(moving, w_send))
    ff_outs = [
        ((CHUNKS, width // CHUNKS, hidden_units), F32),
        ((2, half, CHUNKS, tile // CHUNKS, width), F32),
        ((2, CHUNKS, width // 2 // CHUNKS, width), F32),
    ]

    def finish_ff(name, own, other, first, offsets, old):
        def place(h, j, ids):
            core = jnp.where(h == 0, ids[0], ids[4])
            mine = jnp.where(h == 0, ids[1], ids[2])
            return core, (first + j) ^ mine

        def up_at(h, j, ids):
            core, chunk = place(h, j, ids)
            return chunk, 0, core

        def down_at(h, j, ids):
            core, chunk = place(h, j, ids)
            return core, 0, chunk, 0, 0

        def out_at(h, j, ids):
            core, chunk = place(h, j, ids)
            return core, chunk, 0, 0

        def kernel(ids, *refs):
            gu, gd, go = refs[-3:]
            size = width // CHUNKS
            for h in range(2):
                for j in range(2):

                    @pl.when((pl.program_id(0) == h) & (pl.program_id(1) == j))
                    def _(ref=refs[len(own) * h + j % len(own)], at=offsets[j]):
                        for t in range(half):
                            row = at + 2 * t * size
                            columns = slice(t * tile, (t + 1) * tile)
                            gu[0, :, columns] = ref[row : row + size, :].astype(F32)
                            gd[0, t, 0] = ref[row + size : row + 2 * size, :].astype(F32)
                        row = at + 2 * half * size
                        go[0, 0] = ref[row : row + size // 2, :].astype(F32)

        operands = [*own, *other]
        return call(
            kernel,
            name,
            4,
            (2, 2),
            operands + list(old),
            [whole(v.shape) for v in operands] + [anywhere] * len(old),
            ff_outs,
            [
                pl.BlockSpec((1, width // CHUNKS, half * tile), up_at),
                pl.BlockSpec((1, half, 1, tile // CHUNKS, width), down_at),
                pl.BlockSpec((1, 1, width // 2 // CHUNKS, width), out_at),
            ],
            input_output_aliases={1 + len(operands) + i: i for i in range(len(old))},
        )

    near_da = near_rows(after(send, ff.operand))
    w_sum = SumOverAll(w_keep, after(w_send, ff.operand), 16, sizes)
    w = w_sum.begin()
    far = add_low(keep, near_da[1])
    w = w_sum.step(after(w, far))
    far = far_rows(far)
    w = w_sum.step(w)
    far = after(far, w_sum.operand)
    w = w_sum.step(after(w, far))
    moving = ff.step(after(moving, w_sum.operand))
    last_args = [x, dh, gain_one, own, near_da, after(far, ff.operand)]
    grad_atoms = call(
        lambda ids, *refs: last_kernel(1, *refs),
        "last",
        2,
        (1,),
        last_args,
        [whole(v.shape) for v in last_args],
        atom_outs,
        atom_specs,
    )
    w = w_sum.step(after(w, grad_atoms[0]))
    moving = ff.step(after(moving, w_sum.operand))
    w = w_sum.step(after(w, ff.operand))
    grads = finish_ff(
        "finish_ff_early", ff.own, after_all(ff.other, w_sum.operand), 0, (0, 0), []
    )
    w = w_sum.step(after(w, *grads))
    moving = ff.step(after(moving, w_sum.operand))
    ff.step(moving)
    grad_up, grad_down, go = finish_ff(
        "finish_ff", ff.own[2:], ff.other[2:], 2, (0, ff_rows), grads
    )

    def ordered(pieces, at, size, rows, mine):
        blocks = []
        for chunk in range(CHUNKS):
            place = chunk ^ mine
            start = at + (rows if place == 3 else 0)
            blocks.append(pieces[min(place, 2)][pl.ds(start, size), :])
        return jnp.concatenate(blocks, axis=0)

    def for_each_order(mine, put):
        for value in range(CHUNKS):
            pl.when(mine == value)(lambda value=value: put(value))

    w = w_sum.step(after(w, grad_down))
    w_sum.step(w)

    def finish_rest(ids, *refs):
        own_refs, other_refs = refs[0:3], refs[3:6]
        gq_out, gk_out, gv_out = refs[6:9]
        gains = refs[9:13]
        size = width // CHUNKS

        def put_zero(refs, mine):
            gq_out[...] = ordered(refs, 0, size, share, mine).astype(F32)
            gv_out[:, : width // 2] = ordered(refs, size, size // 2, share, mine).T.astype(F32)

        def put_gains(ref):
            rows = ref[share : share + 16, :].astype(F32)
            for at, out in enumerate(gains):
                out[...] = rows[at]

        def put_one(refs, mine):
            gk_out[...] = ordered(refs, 0, size, share, mine).T.astype(F32)
            gv_out[:, width // 2 :] = ordered(refs, size, size // 2, share, mine).T.astype(F32)

        @pl.when(ids[0] == 0)
        def _():
            for_each_order(ids[1], functools.partial(put_zero, own_refs))
            for_each_order(ids[2], functools.partial(put_one, other_refs))
            put_gains(own_refs[0])

        @pl.when(ids[0] == 1)
        def _():
            for_each_order(ids[2], functools.partial(put_zero, other_refs))
            for_each_order(ids[1], functools.partial(put_one, own_refs))
            put_gains(other_refs[0])

    pieces = w_sum.own + w_sum.other
    gq, gk, gv, *gs = call(
        finish_rest,
        "finish_rest",
        3,
        (1,),
        pieces,
        [whole(v.shape) for v in pieces],
        [(wq.shape, F32)] * 3 + [((width,), F32)] * 4,
        [whole(wq.shape)] * 3 + [whole((width,))] * 4,
    )

    return (
        *[v.reshape(a.shape) for v, a in zip(atoms_out, atoms)],
        *[v.reshape(a.shape) for v, a in zip(pair_out, pairs)],
        *[v.reshape(a.shape) for v, a in zip(grad_atoms, atoms)],
        *[v.reshape(a.shape) for v, a in zip(dls, pairs)],
        gq,
        gk,
        gv,
        go.reshape(wo.shape),
        grad_up.reshape(wu.shape),
        grad_down.reshape(wd.shape),
        *gs,
    )


def solution(mesh):
    atom = P(None, "dp", "rows", None)
    pair = P(None, "dp", None, "rows", None)
    length = P(None, "dp")
    in_specs = (
        (atom,) * 3 + (pair,) * 3 + (length,) * 3 + (P(),) * 10 + (atom,) * 3 + (pair,) * 3
    )
    out_specs = (atom,) * 3 + (pair,) * 3 + (atom,) * 3 + (pair,) * 3 + (P(),) * 10
    body = functools.partial(shards, dict(mesh.shape))
    return jax.shard_map(
        body, mesh=mesh, in_specs=in_specs, out_specs=out_specs, check_vma=False
    )
```

```python
import functools

import jax
import jax.numpy as jnp
from jax import lax
from jax.experimental import pallas as pl
from jax.experimental.pallas import tpu as pltpu
from jax.sharding import PartitionSpec as P

EPSILON = 1e-05
MASKED = -1e30
BF = jnp.bfloat16
F32 = jnp.float32
LANES = 128
GELU_C = 0.7978845608028654
GELU_A = 0.044715
MIB = 1 << 20
CHUNKS = 4
LIMIT = 60


def dot_nn(a, b):
    return lax.dot_general(a, b, (((1,), (0,)), ((), ())), preferred_element_type=F32)


def dot_nt(a, b):
    return lax.dot_general(a, b, (((1,), (1,)), ((), ())), preferred_element_type=F32)


def dot_tn(a, b):
    return lax.dot_general(a, b, (((0,), (0,)), ((), ())), preferred_element_type=F32)


def normalize(x):
    centred = x - jnp.mean(x, axis=-1, keepdims=True)
    spread = jnp.mean(centred * centred, axis=-1, keepdims=True)
    inv = lax.rsqrt(spread + EPSILON)
    return centred * inv, inv


def norm_back(grad, gain, xhat, inv):
    g = grad * gain
    return inv * (
        g
        - jnp.mean(g, axis=-1, keepdims=True)
        - xhat * jnp.mean(g * xhat, axis=-1, keepdims=True)
    )


def front_kernel(ids, x0, x1, wq, wk, wv, gain, shift, q_out, *outs):
    for piece, x_ref in enumerate((x0, x1)):

        @pl.when(pl.program_id(0) == piece)
        def _(piece=piece, x_ref=x_ref):
            a1 = front_rows(x_ref[...], gain, shift, wk, wv, [out.at[0] for out in outs])
            if piece == 0:
                q_out[...] = dot_nn(a1, wq[...]).astype(BF)


def front_rows(x, gain, shift, wk, wv, outs):
    xhat, _ = normalize(x.astype(F32))
    a1 = (xhat * gain[...] + shift[...]).astype(BF)
    outs[0][...] = dot_nn(a1, wk[...]).astype(BF)
    outs[1][...] = dot_nn(a1, wv[...]).astype(BF)
    outs[2][...] = a1
    outs[3][...] = xhat.astype(BF)
    return a1


def head_mask(heads, first):
    lane = lax.broadcasted_iota(jnp.int32, (1, LANES), 1) // (LANES // heads)
    return lane == first


def stacked(block, heads, first, count):
    zero = jnp.zeros_like(block)
    return jnp.concatenate(
        [jnp.where(head_mask(heads, first + t), block, zero) for t in range(count)], axis=0
    )


def unstacked(total, product, heads, first, count, rows):
    for t in range(count):
        part = product[t * rows : (t + 1) * rows]
        total = total + jnp.where(head_mask(heads, first + t), part, 0.0)
    return total


def key_rows(ref, me, start, rows, lanes):
    return jnp.concatenate(
        [ref[me ^ r, start : start + rows, lanes] for r in range(ref.shape[0])], axis=0
    )


def attn_fwd_kernel(layout, groups, heads, scale, ids, *refs):
    lens, q_ref, far_xs, weights, pairs = refs[0:3], refs[3], refs[4:6], refs[6:10], refs[10:13]
    k_near, v_near = refs[13:15]
    pouts, ps, o_ref, fronts, (k_ref, v_ref) = (
        refs[17:20], refs[20:23], refs[23], refs[24:28], refs[28:30]
    )
    wk, wv, gain, shift = weights
    me = ids[3]
    near = k_near.shape[0]
    for i in range(near):
        k_ref[i] = k_near[i]
        v_ref[i] = v_near[i]
    for i, x_ref in enumerate(far_xs):
        front_rows(x_ref[...], gain, shift, wk, wv, [out.at[i] for out in fronts])
        k_ref[near + i] = fronts[0][i]
        v_ref[near + i] = fronts[1][i]
    for (start, mols, rows, slots), len_ref, pair_ref, pout_ref, p_ref in zip(
        layout, lens, pairs, pouts, ps
    ):
        count = min(heads, max(1, 512 // rows))
        for mol in range(mols):
            length = len_ref[pl.program_id(0) * mols + mol]
            key_at = lax.broadcasted_iota(jnp.int32, (1, 1, slots), 2)
            mask = jnp.where(key_at < length, 0.0, MASKED)
            at_row = start + mol * rows
            for group in range(groups):
                lanes = slice(group * LANES, (group + 1) * LANES)
                q = q_ref[at_row : at_row + rows, lanes]
                k = key_rows(k_ref, me, at_row, rows, lanes)
                v = key_rows(v_ref, me, at_row, rows, lanes)
                total = jnp.zeros((rows, LANES), F32)
                for first in range(0, heads, count):
                    at = slice(group * heads + first, group * heads + first + count)
                    s = dot_nt(stacked(q, heads, first, count), k)
                    s = s.reshape(count, rows, slots) * scale + pair_ref[mol, at].astype(F32)
                    pout_ref[mol, at] = s.astype(BF)
                    s = s + mask
                    e = jnp.exp(s - jnp.max(s, axis=-1, keepdims=True))
                    p = (e * (1.0 / jnp.sum(e, axis=-1, keepdims=True))).astype(BF)
                    p_ref[mol, at] = p
                    pv = dot_nn(p.reshape(count * rows, slots), v)
                    total = unstacked(total, pv, heads, first, count, rows)
                o_ref[at_row : at_row + rows, lanes] = total


def attn_bwd_kernel(layout, groups, heads, scale, ids, *refs):
    me = ids[3]
    count_of = len(layout)
    q_ref, do_ref, dd_ref, k_ref, v_ref = refs[0:5]
    ps, dpos = refs[5 : 5 + count_of], refs[5 + count_of : 5 + 2 * count_of]
    dls = refs[5 + 2 * count_of : 5 + 3 * count_of]
    dq_ref, dk_ref, dv_ref = refs[5 + 3 * count_of :]
    ranks = k_ref.shape[0]
    origin = layout[0][0]
    for (start, mols, rows, slots), p_ref, dpo_ref, dl_ref in zip(layout, ps, dpos, dls):
        count = min(heads, max(1, 1024 // rows))
        base = (start - origin) * ranks
        for group in range(groups):
            lanes = slice(group * LANES, (group + 1) * LANES)
            dk_all = []
            dv_all = []
            for mol in range(mols):
                at_row = start - origin + mol * rows
                rs = slice(at_row, at_row + rows)
                q = q_ref[rs, lanes]
                do = do_ref[rs, lanes]
                dd = dd_ref[rs, lanes]
                k = key_rows(k_ref, me, at_row, rows, lanes)
                v = key_rows(v_ref, me, at_row, rows, lanes)
                v_aug = jnp.concatenate([v, jnp.ones_like(v)], axis=1)
                total = jnp.zeros((rows, LANES), F32)
                dk = jnp.zeros((LANES, slots), F32)
                dv = jnp.zeros((LANES, slots), F32)
                for first in range(0, heads, count):
                    at = slice(group * heads + first, group * heads + first + count)
                    do_s = stacked(do, heads, first, count)
                    t = dot_nt(
                        jnp.concatenate([do_s, stacked(dd, heads, first, count)], axis=1), v_aug
                    )
                    p = p_ref[mol, at]
                    dl = p.astype(F32) * t.reshape(count, rows, slots)
                    dl = (dl + dpo_ref[mol, at].astype(F32)).astype(BF)
                    dl_ref[mol, at] = dl
                    dl = dl.reshape(count * rows, slots)
                    total = unstacked(total, dot_nn(dl, k), heads, first, count, rows)
                    dk = dk + dot_tn(stacked(q, heads, first, count), dl)
                    dv = dv + dot_tn(do_s, p.reshape(count * rows, slots))
                dq_ref[rs, lanes] = (total * scale).astype(BF)
                dk_all.append((dk * scale).astype(BF))
                dv_all.append(dv.astype(BF))
            dk_ref[lanes, base : base + mols * slots] = jnp.concatenate(dk_all, axis=1)
            dv_ref[lanes, base : base + mols * slots] = jnp.concatenate(dv_all, axis=1)


def back_kernel(layout, share, parts, ids, *refs):
    dqs, dks, dvs = (refs[i * parts : (i + 1) * parts] for i in range(3))
    a_ref, h_ref, wq, wk, wv, gs_two = refs[3 * parts : 3 * parts + 6]
    own_ref, keep_ref, send_ref, w_send, w_keep = refs[3 * parts + 6 : 3 * parts + 11]
    gq_ref, gk_ref, gv_ref, gs_ref, da_s = refs[3 * parts + 11 :]
    step = pl.program_id(0)
    me = ids[3]
    ranks = a_ref.shape[0]

    @pl.when(step == 0)
    def _():
        for ref in (gq_ref, gk_ref, gv_ref, gs_ref):
            ref[...] = jnp.zeros_like(ref)

    def molecules(ref):
        return jnp.concatenate(
            [
                key_rows(ref, me, start + mol * rows, rows, slice(None))
                for start, mols, rows, slots in layout
                for mol in range(mols)
            ],
            axis=0,
        )

    dq = jnp.concatenate([ref[...] for ref in dqs], axis=0)
    dk = jnp.concatenate([ref[...] for ref in dks], axis=1)
    dv = jnp.concatenate([ref[...] for ref in dvs], axis=1)
    a1 = molecules(a_ref)
    gk_ref[...] += dot_nn(dk, a1)
    gv_ref[...] += dot_nn(dv, a1)
    gq_ref[...] += dot_tn(a_ref[0], dq)
    daq = dot_nt(dq, wq[...])
    across = (((0,), (1,)), ((), ()))
    da = lax.dot_general(dk, wk[...], across, preferred_element_type=F32) + lax.dot_general(
        dv, wv[...], across, preferred_element_type=F32
    )
    da_s[...] = da
    gs_ref[0:1, :] += jnp.sum(da * molecules(h_ref).astype(F32), axis=0, keepdims=True) + jnp.sum(
        daq * h_ref[0].astype(F32), axis=0, keepdims=True
    )
    gs_ref[1:2, :] += jnp.sum(da, axis=0, keepdims=True) + jnp.sum(daq, axis=0, keepdims=True)
    for piece in range(ranks):
        for start, mols, rows, slots in layout:
            for mol in range(mols):
                at = pl.multiple_of(start * ranks + mol * slots + (me ^ piece) * rows, rows)
                value = da_s[pl.ds(at, rows), :]
                to = slice(start + mol * rows, start + (mol + 1) * rows)
                if piece == 0:
                    own_ref[to, :] = value + daq[to]
                elif piece == 2:
                    keep_ref[to, :] = value.astype(BF)
                else:
                    send_ref[piece // 2, to, :] = value.astype(BF)

    @pl.when(step == pl.num_programs(0) - 1)
    def _():
        width = gq_ref.shape[1]
        size = width // CHUNKS
        half = width // 2
        gains = jnp.concatenate(
            [gs_ref[0:2, :], gs_two[0:2, :], jnp.zeros((12, width), F32)], axis=0
        ).astype(BF)
        for value in (0, 1):

            @pl.when(ids[0] == value)
            def _(value=value):
                for ref, owner, mine in ((w_keep, value, ids[1]), (w_send, 1 - value, ids[2])):
                    shard_rows(ref, (gk_ref if owner else gq_ref)[...], 0, share, mine)
                    gv = gv_ref[owner * half : (owner + 1) * half, :]
                    shard_rows(ref, gv, size, share, mine)

        w_keep[CHUNKS * share :, :] = gains
        w_send[CHUNKS * share :, :] = gains


def shard_rows(ref, value, at, rows, mine):
    size = value.shape[0] // CHUNKS
    if isinstance(ref, tuple):
        for chunk in range(CHUNKS):
            place = chunk ^ mine
            to = pl.multiple_of((place % 2) * rows + at, 16)
            for half, part in enumerate(ref):

                @pl.when(place // 2 == half)
                def _(part=part, to=to, chunk=chunk):
                    block = value[chunk * size : (chunk + 1) * size]
                    part[pl.ds(to, size), :] = block.astype(part.dtype)

        return
    for chunk in range(CHUNKS):
        to = pl.multiple_of((chunk ^ mine) * rows + at, 16)
        ref[pl.ds(to, size), :] = value[chunk * size : (chunk + 1) * size].astype(ref.dtype)


def store_by_bucket(refs, value):
    row = 0
    for micro in range(refs[0].shape[0]):
        for ref in refs:
            ref[micro] = value[row : row + ref.shape[1]]
            row += ref.shape[1]


def store_tile(send_ref, keep_ref, value, step, at, half_tiles, rows, ids):
    size = value.shape[0] // CHUNKS

    @pl.when(step < half_tiles)
    def _():
        shard_rows(send_ref, value, (2 * step + at) * size, rows, ids[2])

    @pl.when(step >= half_tiles)
    def _():
        shard_rows(keep_ref, value, (2 * (step - half_tiles) + at) * size, rows, ids[1])


def dense_kernel(
    tiles, rows, ids, x_ref, o_ref, dy_ref, wo, wu, wd, gain, shift,
    yb, ym, ys, dh_ref, do_ref, dd_ref, gs_ref, send_low, send_high, keep_ref,
    a2_s, a2t_s, y_s, xhat_s, inv_s, da_s,
):
    step = pl.program_id(0)
    half_tiles = tiles // 2
    send_ref = (send_low, send_high)

    @pl.when(step == 0)
    def _():
        hidden = x_ref[...].astype(F32) + dot_nn(o_ref[...].astype(BF), wo[...])
        xhat, inv = normalize(hidden)
        y_s[...] = hidden
        xhat_s[...] = xhat
        inv_s[...] = jnp.broadcast_to(inv, inv_s.shape)
        a2 = (xhat * gain[...] + shift[...]).astype(BF)
        a2_s[...] = a2
        a2t_s[...] = a2.T
        da_s[...] = jnp.zeros_like(da_s)

    dy = dy_ref[...]
    u = dot_nn(a2_s[...], wu[...])
    u2 = u * u
    th = jnp.tanh(u * (GELU_C + (GELU_C * GELU_A) * u2))
    half = 0.5 + 0.5 * th
    g = u * half
    slope = half + g * (1.0 - th) * (GELU_C + (3.0 * GELU_C * GELU_A) * u2)
    g = g.astype(BF)
    y_s[...] += dot_nn(g, wd[...])
    store_tile(send_ref, keep_ref, dot_tn(g, dy), step, 1, half_tiles, rows, ids)
    du = (dot_nt(dy, wd[...]) * slope).astype(BF)
    store_tile(send_ref, keep_ref, dot_nn(a2t_s[...], du), step, 0, half_tiles, rows, ids)
    da_s[...] += dot_nt(du, wu[...])

    @pl.when(step == tiles - 1)
    def _():
        store_by_bucket((yb, ym, ys), y_s[...].astype(BF))
        da = da_s[...]
        xhat = xhat_s[...]
        gs_ref[0:1, :] = jnp.sum(da * xhat, axis=0, keepdims=True)
        gs_ref[1:2, :] = jnp.sum(da, axis=0, keepdims=True)
        dh = dy.astype(F32) + norm_back(da, gain[...], xhat, inv_s[:, 0:1])
        dh_ref[...] = dh
        dh = dh.astype(BF)
        o = o_ref[...]
        do = dot_nt(dh, wo[...]).astype(BF)
        do_ref[...] = do
        dd_ref[...] = (-(do.astype(F32) * o)).astype(BF)
        da_s[...] = dot_tn(o.astype(BF), dh)
        width = da.shape[1]
        part = width // 2
        for ref, core, mine in ((send_ref, ids[4], ids[2]), (keep_ref, ids[0], ids[1])):
            value = da_s[pl.ds(pl.multiple_of(core * part, part), part), :]
            shard_rows(ref, value, 2 * half_tiles * (width // CHUNKS), rows, mine)


def last_kernel(parts, x_ref, dh, gain, *refs):
    grads = []
    row = 0
    for part in range(parts):
        own, near, far = refs[3 * part : 3 * part + 3]
        at = slice(row, row + own.shape[0])
        row += own.shape[0]
        xhat, inv = normalize(x_ref[at, :].astype(F32))
        da = own[...] + near[0].astype(F32) + far[...].astype(F32)
        grads.append((dh[at, :] + norm_back(da, gain[...], xhat, inv)).astype(BF))
    store_by_bucket(refs[3 * parts :], jnp.concatenate(grads, axis=0))


def exchange(value, axis, distance, size):
    return lax.ppermute(value, axis, [(i, i ^ distance) for i in range(size)])


def add_low(first, *others):
    total = first.astype(F32)
    for other in others:
        total = total + other.astype(F32)
    return total.astype(BF)


def stage_permutes(sizes):
    rows = sizes["rows"]
    x, y, z_near, z_far = rows, 2, 2 * rows, 4 * rows
    pairs = [(x, y), (y, x), (z_near, z_far), (z_far, z_near)]
    extra = 8
    while extra < sizes["dp"]:
        pairs.append((extra * rows, extra * rows))
        extra *= 2
    total = rows * sizes["dp"]
    return [[(i, i ^ pair[i % 2]) for i in range(total)] for pair in pairs]


def send_all(value, perm):
    return lax.ppermute(value, ("dp", "rows"), perm)


def after(value, *others):
    return lax.optimization_barrier((value,) + others)[0]


def after_all(values, *others):
    return list(lax.optimization_barrier((*values, *others)))[: len(values)]


class SumOverAll:
    def __init__(self, keep, send, tail, sizes):
        self.stages = stage_permutes(sizes)
        self.swap = functools.partial(exchange, axis="rows", distance=1, size=sizes["rows"])
        self.tail = tail
        self.block = (keep.shape[0] - tail) // CHUNKS
        self.size = CHUNKS * self.block
        self.terms = [keep]
        self.send = send

    def cut(self, value, start, stop):
        if not self.tail:
            return value[start:stop]
        return jnp.concatenate([value[start:stop], value[value.shape[0] - self.tail :]], axis=0)

    def split(self, got):
        self.terms.append(got)
        half = self.size // 2
        send = add_low(*[self.cut(v, half, self.size) for v in self.terms])
        self.size = half
        return send

    def reduce(self):
        if isinstance(self.send, tuple):
            half = self.size // 2
            low = self.swap(self.send[0])
            high = yield self.send[1], self.swap
            first = add_low(self.terms[0][half:], high)
            self.size = half
            got = yield first, functools.partial(send_all, perm=self.stages[0])
            self.terms.append(low)
        else:
            got = yield self.send, self.swap
            got = yield self.split(got), functools.partial(send_all, perm=self.stages[0])
        got = yield self.split(got), functools.partial(send_all, perm=self.stages[1])
        part = add_low(*[self.cut(v, 0, self.size) for v in self.terms + [got]])
        for stage in self.stages[2:4]:
            got = yield part, functools.partial(send_all, perm=stage)
            part = add_low(part, got)
        for stage in self.stages[4:]:
            part = add_low(part, send_all(part, stage))
        block = part[: self.block]
        self.own = [part]
        self.other = [self.swap(part)]
        second = yield block, functools.partial(send_all, perm=self.stages[1])
        self.own.append(second)
        self.other.append(self.swap(second))
        low = jnp.concatenate([block, second], axis=0)
        high = yield low, functools.partial(send_all, perm=self.stages[0])
        self.own.append(high)
        got = yield high, self.swap
        self.other.append(got)
        yield None, None

    def begin(self):
        self.run = self.reduce()
        return self.step(None)

    def step(self, got, *deps):
        self.operand, move = self.run.send(got)
        return None if move is None else move(after(self.operand, *deps))


def cost(micros):
    return pl.CostEstimate(flops=0, bytes_accessed=int(micros * 0.8e6), transcendentals=0)


def params():
    return pltpu.CompilerParams(vmem_limit_bytes=LIMIT * MIB)


def shards(sizes, *args):
    atoms, pairs, lengths = args[0:3], args[3:6], args[6:9]
    wq, wk, wv, wo, wu, wd = args[9:15]
    gain_one, shift_one, gain_two, shift_two = (v.reshape(1, -1) for v in args[15:19])
    dys, dpos = args[19:22], args[22:25]
    width = atoms[0].shape[-1]
    micros = atoms[0].shape[0]
    hidden_units = wu.shape[1]
    head_count = pairs[0].shape[2]
    heads = head_count * LANES // width
    scale = float((width // head_count) ** -0.5)
    groups = width // LANES
    ranks = sizes["rows"]

    rows_at = lax.axis_index("rows")
    core, y = rows_at % 2, rows_at // 2
    xa = lax.axis_index("dp") % 2
    order = (xa * 2 + y, y * 2 + xa)
    mine = jnp.where(core == 0, order[0], order[1])
    other = jnp.where(core == 0, order[1], order[0])
    ids = jnp.stack([core, mine, other, rows_at, core ^ 1]).astype(jnp.int32)

    layout = []
    start = 0
    for a in atoms:
        layout.append((start, a.shape[1], a.shape[2], a.shape[2] * ranks))
        start += a.shape[1] * a.shape[2]
    layout = tuple(layout)
    micro_rows = start
    local = micros * micro_rows

    def by_micro(arrays):
        return jnp.concatenate(
            [a.reshape(micros, -1, width) for a in arrays], axis=1
        ).reshape(local, width)

    x = by_micro(atoms)
    dy = by_micro(dys)
    pair = [p.reshape((-1,) + p.shape[2:]) for p in pairs]
    dpo = [p.reshape((-1,) + p.shape[2:]) for p in dpos]
    lens = [n.reshape(-1) for n in lengths]

    near_rows = functools.partial(exchange, axis="rows", distance=1, size=ranks)
    far_rows = functools.partial(exchange, axis="rows", distance=2, size=ranks)
    x2 = far_rows(x)
    x1 = near_rows(x)

    smem = pl.BlockSpec(memory_space=pltpu.SMEM)
    anywhere = pl.BlockSpec(memory_space=pl.ANY)

    def whole(shape):
        return pl.BlockSpec(tuple(shape), lambda *_: (0,) * len(shape))

    def call(kernel, name, micros, grid, operands, in_specs, outs, out_specs, scratch=(), **kw):
        return pl.pallas_call(
            kernel,
            grid_spec=pltpu.PrefetchScalarGridSpec(
                num_scalar_prefetch=1,
                grid=grid,
                in_specs=in_specs,
                out_specs=out_specs,
                scratch_shapes=list(scratch),
            ),
            out_shape=[jax.ShapeDtypeStruct(tuple(shape), kind) for shape, kind in outs],
            compiler_params=params(),
            cost_estimate=cost(micros),
            name=name,
            **kw,
        )(ids, *operands)

    near = 2
    gathered = ((ranks, local, width), BF)
    operands = [x, x1, wq, wk, wv, gain_one, shift_one]
    q, *fronts = call(
        front_kernel,
        "front",
        4,
        (near,),
        operands,
        [whole(v.shape) for v in operands],
        [((local, width), BF)] + [gathered] * 4,
        [whole((local, width))] + [pl.BlockSpec((1, local, width), lambda t, ids: (t, 0, 0))] * 4,
    )
    x2 = after(x2, q, dy, *lens)
    x3 = near_rows(x2)

    row_spec = pl.BlockSpec((micro_rows, width), lambda m, ids: (m, 0))
    rank_spec = pl.BlockSpec((ranks, micro_rows, width), lambda m, ids: (0, m, 0))
    pair_specs = [
        pl.BlockSpec((p.shape[0] // micros,) + p.shape[1:], lambda m, ids: (m, 0, 0, 0))
        for p in pair
    ]
    pair_outs = [(p.shape, BF) for p in pair]
    near_spec = pl.BlockSpec((near, micro_rows, width), lambda m, ids: (0, m, 0))
    far_spec = pl.BlockSpec((ranks - near, micro_rows, width), lambda m, ids: (1, m, 0))
    operands = [*lens, q, x2, x3, wk, wv, gain_one, shift_one, *pair, *fronts]
    res = call(
        functools.partial(attn_fwd_kernel, layout, groups, heads, scale),
        "attend",
        18,
        (micros,),
        operands,
        [smem] * 3
        + [row_spec] * 3
        + [whole(v.shape) for v in operands[6:10]]
        + pair_specs
        + [near_spec] * 2
        + [anywhere] * 2,
        pair_outs * 2 + [((local, width), F32)] + [gathered] * 4,
        pair_specs * 2 + [row_spec] + [far_spec] * 4,
        [pltpu.VMEM((ranks, micro_rows, width), BF)] * 2,
        input_output_aliases={14 + i: 7 + i for i in range(4)},
    )
    o = res[6]
    ks, vs, a1s, xhats = res[7:11]
    pair_out, probs = res[0:3], res[3:6]

    tiles = 4
    tile = hidden_units // tiles
    half = tiles // 2

    def tile_at(t, ids):
        return (t + half * ids[4]) % tiles

    up_spec = pl.BlockSpec((width, tile), lambda t, ids: (0, tile_at(t, ids)))
    down_spec = pl.BlockSpec((tile, width), lambda t, ids: (tile_at(t, ids), 0))
    local_shape = (local, width)
    flat = whole(local_shape)
    ff_rows = (2 * half * tile + width // 2) // CHUNKS
    ff_shape = (CHUNKS * ff_rows, width)
    ff_half = (CHUNKS // 2 * ff_rows, width)
    atom_outs = [((micros, a.shape[1] * a.shape[2], width), BF) for a in atoms]
    atom_specs = [whole(shape) for shape, _ in atom_outs]
    *atoms_out, dh, do, dd, gs_two, ff_low, ff_high, ff_keep = call(
        functools.partial(dense_kernel, tiles, ff_rows),
        "dense",
        16,
        (tiles,),
        [x, o, dy, wo, wu, wd, gain_two, shift_two],
        [flat, flat, flat, whole(wo.shape), up_spec, down_spec] + [whole((1, width))] * 2,
        atom_outs
        + [(local_shape, F32), (local_shape, BF), (local_shape, BF), ((8, width), F32)]
        + [(ff_half, BF), (ff_half, BF), (ff_shape, BF)],
        atom_specs
        + [flat, flat, flat, whole((8, width)), whole(ff_half), whole(ff_half), whole(ff_shape)],
        [
            pltpu.VMEM(local_shape, BF),
            pltpu.VMEM((width, local), BF),
            pltpu.VMEM(local_shape, F32),
            pltpu.VMEM(local_shape, F32),
            pltpu.VMEM((local, LANES), F32),
            pltpu.VMEM(local_shape, F32),
        ],
    )
    ff = SumOverAll(ff_keep, (ff_low, ff_high), 0, sizes)
    moving = ff.step(ff.begin())
    do = after(do, ff.operand)

    dls = []
    dqs, dks, dvs = [], [], []
    for name, buckets in (("attend_back_big", (0,)), ("attend_back_rest", (1, 2))):
        here = tuple(layout[b] for b in buckets)
        rows_here = sum(mols * rows for _, mols, rows, _ in here)
        specs = [pair_specs[b] for b in buckets]
        per, at = micro_rows // rows_here, here[0][0] // rows_here
        rows_spec = pl.BlockSpec(
            (rows_here, width), lambda m, ids, per=per, at=at: (m * per + at, 0)
        )
        ranks_spec = pl.BlockSpec(
            (ranks, rows_here, width), lambda m, ids, per=per, at=at: (0, m * per + at, 0)
        )
        key_spec = pl.BlockSpec((width, rows_here * ranks), lambda m, ids: (0, m))
        key_out = ((width, micros * rows_here * ranks), BF)
        res = call(
            functools.partial(attn_bwd_kernel, here, groups, heads, scale),
            name,
            15,
            (micros,),
            [q, do, dd, ks, vs] + [probs[b] for b in buckets] + [dpo[b] for b in buckets],
            [rows_spec] * 3 + [ranks_spec] * 2 + specs * 2,
            [pair_outs[b] for b in buckets]
            + [((micros * rows_here, width), BF), key_out, key_out],
            specs
            + [pl.BlockSpec((rows_here, width), lambda m, ids: (m, 0)), key_spec, key_spec],
        )
        dls += res[: len(buckets)]
        for values, value in zip((dqs, dks, dvs), res[len(buckets) :]):
            values.append(value)
        moving = ff.step(after(moving, dqs[-1]))
        if len(dqs) == 1:
            do = after(do, ff.operand)
        else:
            dqs[-1] = after(dqs[-1], ff.operand)

    share = (width + width // 2) // CHUNKS
    w_shape = (CHUNKS * share + 16, width)
    operands = [*dqs, *dks, *dvs, a1s, xhats, wq, wk, wv, gs_two]
    own, keep, send, w_send, w_keep = call(
        functools.partial(back_kernel, layout, share, len(dqs)),
        "back",
        9,
        (micros,),
        operands,
        [pl.BlockSpec((v.shape[0] // micros, width), lambda m, ids: (m, 0)) for v in dqs]
        + [pl.BlockSpec((width, v.shape[1] // micros), lambda m, ids: (0, m)) for v in dks + dvs]
        + [rank_spec] * 2
        + [whole(v.shape) for v in operands[-4:]],
        [
            (local_shape, F32),
            (local_shape, BF),
            ((2,) + local_shape, BF),
            (w_shape, BF),
            (w_shape, BF),
        ],
        [
            row_spec,
            row_spec,
            pl.BlockSpec((2, micro_rows, width), lambda m, ids: (0, m, 0)),
            whole(w_shape),
            whole(w_shape),
        ],
        [
            pltpu.VMEM((width, width), F32),
            pltpu.VMEM((width, width), F32),
            pltpu.VMEM((width, width), F32),
            pltpu.VMEM((8, width), F32),
            pltpu.VMEM((ranks * micro_rows, width), F32),
        ],
    )
    moving = ff.step(after(moving, w_send))
    ff_outs = [
        ((CHUNKS, width // CHUNKS, hidden_units), F32),
        ((2, half, CHUNKS, tile // CHUNKS, width), F32),
        ((2, CHUNKS, width // 2 // CHUNKS, width), F32),
    ]

    def finish_ff(name, own, other, first, offsets, old):
        def place(h, j, ids):
            core = jnp.where(h == 0, ids[0], ids[4])
            mine = jnp.where(h == 0, ids[1], ids[2])
            return core, (first + j) ^ mine

        def up_at(h, j, ids):
            core, chunk = place(h, j, ids)
            return chunk, 0, core

        def down_at(h, j, ids):
            core, chunk = place(h, j, ids)
            return core, 0, chunk, 0, 0

        def out_at(h, j, ids):
            core, chunk = place(h, j, ids)
            return core, chunk, 0, 0

        def kernel(ids, *refs):
            gu, gd, go = refs[-3:]
            size = width // CHUNKS
            for h in range(2):
                for j in range(2):

                    @pl.when((pl.program_id(0) == h) & (pl.program_id(1) == j))
                    def _(ref=refs[len(own) * h + j % len(own)], at=offsets[j]):
                        for t in range(half):
                            row = at + 2 * t * size
                            columns = slice(t * tile, (t + 1) * tile)
                            gu[0, :, columns] = ref[row : row + size, :].astype(F32)
                            gd[0, t, 0] = ref[row + size : row + 2 * size, :].astype(F32)
                        row = at + 2 * half * size
                        go[0, 0] = ref[row : row + size // 2, :].astype(F32)

        operands = [*own, *other]
        return call(
            kernel,
            name,
            4,
            (2, 2),
            operands + list(old),
            [whole(v.shape) for v in operands] + [anywhere] * len(old),
            ff_outs,
            [
                pl.BlockSpec((1, width // CHUNKS, half * tile), up_at),
                pl.BlockSpec((1, half, 1, tile // CHUNKS, width), down_at),
                pl.BlockSpec((1, 1, width // 2 // CHUNKS, width), out_at),
            ],
            input_output_aliases={1 + len(operands) + i: i for i in range(len(old))},
        )

    near_da = near_rows(after(send, ff.operand))
    w_sum = SumOverAll(w_keep, after(w_send, ff.operand), 16, sizes)
    w = w_sum.begin()
    far = add_low(keep, near_da[1])
    w = w_sum.step(after(w, far))
    far = far_rows(far)
    w = w_sum.step(w)
    far = after(far, w_sum.operand)
    w = w_sum.step(after(w, far))
    moving = ff.step(after(moving, w_sum.operand))
    last_args = [x, dh, gain_one, own, near_da, after(far, ff.operand)]
    grad_atoms = call(
        lambda ids, *refs: last_kernel(1, *refs),
        "last",
        2,
        (1,),
        last_args,
        [whole(v.shape) for v in last_args],
        atom_outs,
        atom_specs,
    )
    w = w_sum.step(after(w, grad_atoms[0]))
    moving = ff.step(after(moving, w_sum.operand))
    w = w_sum.step(after(w, ff.operand))
    grads = finish_ff(
        "finish_ff_early", ff.own, after_all(ff.other, w_sum.operand), 0, (0, 0), []
    )
    w = w_sum.step(after(w, *grads))
    moving = ff.step(after(moving, w_sum.operand))
    ff.step(moving)
    grad_up, grad_down, go = finish_ff(
        "finish_ff", ff.own[2:], ff.other[2:], 2, (0, ff_rows), grads
    )

    def ordered(pieces, at, size, rows, mine):
        blocks = []
        for chunk in range(CHUNKS):
            place = chunk ^ mine
            start = at + (rows if place == 3 else 0)
            blocks.append(pieces[min(place, 2)][pl.ds(start, size), :])
        return jnp.concatenate(blocks, axis=0)

    def for_each_order(mine, put):
        for value in range(CHUNKS):
            pl.when(mine == value)(lambda value=value: put(value))

    w = w_sum.step(after(w, grad_down))
    w_sum.step(w)

    def finish_rest(ids, *refs):
        own_refs, other_refs = refs[0:3], refs[3:6]
        gq_out, gk_out, gv_out = refs[6:9]
        gains = refs[9:13]
        size = width // CHUNKS

        def put_zero(refs, mine):
            gq_out[...] = ordered(refs, 0, size, share, mine).astype(F32)
            gv_out[:, : width // 2] = ordered(refs, size, size // 2, share, mine).T.astype(F32)

        def put_gains(ref):
            rows = ref[share : share + 16, :].astype(F32)
            for at, out in enumerate(gains):
                out[...] = rows[at]

        def put_one(refs, mine):
            gk_out[...] = ordered(refs, 0, size, share, mine).T.astype(F32)
            gv_out[:, width // 2 :] = ordered(refs, size, size // 2, share, mine).T.astype(F32)

        @pl.when(ids[0] == 0)
        def _():
            for_each_order(ids[1], functools.partial(put_zero, own_refs))
            for_each_order(ids[2], functools.partial(put_one, other_refs))
            put_gains(own_refs[0])

        @pl.when(ids[0] == 1)
        def _():
            for_each_order(ids[2], functools.partial(put_zero, other_refs))
            for_each_order(ids[1], functools.partial(put_one, own_refs))
            put_gains(other_refs[0])

    pieces = w_sum.own + w_sum.other
    gq, gk, gv, *gs = call(
        finish_rest,
        "finish_rest",
        3,
        (1,),
        pieces,
        [whole(v.shape) for v in pieces],
        [(wq.shape, F32)] * 3 + [((width,), F32)] * 4,
        [whole(wq.shape)] * 3 + [whole((width,))] * 4,
    )

    return (
        *[v.reshape(a.shape) for v, a in zip(atoms_out, atoms)],
        *[v.reshape(a.shape) for v, a in zip(pair_out, pairs)],
        *[v.reshape(a.shape) for v, a in zip(grad_atoms, atoms)],
        *[v.reshape(a.shape) for v, a in zip(dls, pairs)],
        gq,
        gk,
        gv,
        go.reshape(wo.shape),
        grad_up.reshape(wu.shape),
        grad_down.reshape(wd.shape),
        *gs,
    )


def solution(mesh):
    atom = P(None, "dp", "rows", None)
    pair = P(None, "dp", None, "rows", None)
    length = P(None, "dp")
    in_specs = (
        (atom,) * 3 + (pair,) * 3 + (length,) * 3 + (P(),) * 10 + (atom,) * 3 + (pair,) * 3
    )
    out_specs = (atom,) * 3 + (pair,) * 3 + (atom,) * 3 + (pair,) * 3 + (P(),) * 10
    body = functools.partial(shards, dict(mesh.shape))
    return jax.shard_map(
        body, mesh=mesh, in_specs=in_specs, out_specs=out_specs, check_vma=False
    )
```

```python
import functools

import jax
import jax.numpy as jnp
from jax import lax
from jax.experimental import pallas as pl
from jax.experimental.pallas import tpu as pltpu
from jax.sharding import PartitionSpec as P

EPSILON = 1e-05
MASKED = -1e30
BF = jnp.bfloat16
F32 = jnp.float32
LANES = 128
GELU_C = 0.7978845608028654
GELU_A = 0.044715
MIB = 1 << 20
CHUNKS = 4
LIMIT = 60


def dot_nn(a, b):
    return lax.dot_general(a, b, (((1,), (0,)), ((), ())), preferred_element_type=F32)


def dot_nt(a, b):
    return lax.dot_general(a, b, (((1,), (1,)), ((), ())), preferred_element_type=F32)


def dot_tn(a, b):
    return lax.dot_general(a, b, (((0,), (0,)), ((), ())), preferred_element_type=F32)


def normalize(x):
    centred = x - jnp.mean(x, axis=-1, keepdims=True)
    spread = jnp.mean(centred * centred, axis=-1, keepdims=True)
    inv = lax.rsqrt(spread + EPSILON)
    return centred * inv, inv


def norm_back(grad, gain, xhat, inv):
    g = grad * gain
    return inv * (
        g
        - jnp.mean(g, axis=-1, keepdims=True)
        - xhat * jnp.mean(g * xhat, axis=-1, keepdims=True)
    )


def front_kernel(ids, x0, x1, wq, wk, wv, gain, shift, q_out, *outs):
    for piece, x_ref in enumerate((x0, x1)):

        @pl.when(pl.program_id(0) == piece)
        def _(piece=piece, x_ref=x_ref):
            a1 = front_rows(x_ref[...], gain, shift, wk, wv, [out.at[0] for out in outs])
            if piece == 0:
                q_out[...] = dot_nn(a1, wq[...]).astype(BF)


def front_rows(x, gain, shift, wk, wv, outs):
    xhat, _ = normalize(x.astype(F32))
    a1 = (xhat * gain[...] + shift[...]).astype(BF)
    outs[0][...] = dot_nn(a1, wk[...]).astype(BF)
    outs[1][...] = dot_nn(a1, wv[...]).astype(BF)
    outs[2][...] = a1
    outs[3][...] = xhat.astype(BF)
    return a1


def head_mask(heads, first):
    lane = lax.broadcasted_iota(jnp.int32, (1, LANES), 1) // (LANES // heads)
    return lane == first


def stacked(block, heads, first, count):
    zero = jnp.zeros_like(block)
    return jnp.concatenate(
        [jnp.where(head_mask(heads, first + t), block, zero) for t in range(count)], axis=0
    )


def unstacked(total, product, heads, first, count, rows):
    for t in range(count):
        part = product[t * rows : (t + 1) * rows]
        total = total + jnp.where(head_mask(heads, first + t), part, 0.0)
    return total


def key_rows(ref, me, start, rows, lanes):
    return jnp.concatenate(
        [ref[me ^ r, start : start + rows, lanes] for r in range(ref.shape[0])], axis=0
    )


def attn_fwd_kernel(layout, groups, heads, scale, ids, *refs):
    lens, q_ref, far_xs, weights, pairs = refs[0:3], refs[3], refs[4:6], refs[6:10], refs[10:13]
    k_near, v_near = refs[13:15]
    pouts, ps, o_ref, fronts, (k_ref, v_ref) = (
        refs[17:20], refs[20:23], refs[23], refs[24:28], refs[28:30]
    )
    wk, wv, gain, shift = weights
    me = ids[3]
    near = k_near.shape[0]
    for i in range(near):
        k_ref[i] = k_near[i]
        v_ref[i] = v_near[i]
    for i, x_ref in enumerate(far_xs):
        front_rows(x_ref[...], gain, shift, wk, wv, [out.at[i] for out in fronts])
        k_ref[near + i] = fronts[0][i]
        v_ref[near + i] = fronts[1][i]
    for (start, mols, rows, slots), len_ref, pair_ref, pout_ref, p_ref in zip(
        layout, lens, pairs, pouts, ps
    ):
        count = min(heads, max(1, 512 // rows))
        for mol in range(mols):
            length = len_ref[pl.program_id(0) * mols + mol]
            key_at = lax.broadcasted_iota(jnp.int32, (1, 1, slots), 2)
            mask = jnp.where(key_at < length, 0.0, MASKED)
            at_row = start + mol * rows
            for group in range(groups):
                lanes = slice(group * LANES, (group + 1) * LANES)
                q = q_ref[at_row : at_row + rows, lanes]
                k = key_rows(k_ref, me, at_row, rows, lanes)
                v = key_rows(v_ref, me, at_row, rows, lanes)
                total = jnp.zeros((rows, LANES), F32)
                for first in range(0, heads, count):
                    at = slice(group * heads + first, group * heads + first + count)
                    s = dot_nt(stacked(q, heads, first, count), k)
                    s = s.reshape(count, rows, slots) * scale + pair_ref[mol, at].astype(F32)
                    pout_ref[mol, at] = s.astype(BF)
                    s = s + mask
                    e = jnp.exp(s - jnp.max(s, axis=-1, keepdims=True))
                    p = (e * (1.0 / jnp.sum(e, axis=-1, keepdims=True))).astype(BF)
                    p_ref[mol, at] = p
                    pv = dot_nn(p.reshape(count * rows, slots), v)
                    total = unstacked(total, pv, heads, first, count, rows)
                o_ref[at_row : at_row + rows, lanes] = total


def attn_bwd_kernel(layout, groups, heads, scale, ids, *refs):
    me = ids[3]
    count_of = len(layout)
    q_ref, do_ref, dd_ref, k_ref, v_ref = refs[0:5]
    ps, dpos = refs[5 : 5 + count_of], refs[5 + count_of : 5 + 2 * count_of]
    dls = refs[5 + 2 * count_of : 5 + 3 * count_of]
    dq_ref, dk_ref, dv_ref = refs[5 + 3 * count_of :]
    ranks = k_ref.shape[0]
    origin = layout[0][0]
    for (start, mols, rows, slots), p_ref, dpo_ref, dl_ref in zip(layout, ps, dpos, dls):
        count = min(heads, max(1, 1024 // rows))
        base = (start - origin) * ranks
        for group in range(groups):
            lanes = slice(group * LANES, (group + 1) * LANES)
            dk_all = []
            dv_all = []
            for mol in range(mols):
                at_row = start - origin + mol * rows
                rs = slice(at_row, at_row + rows)
                q = q_ref[rs, lanes]
                do = do_ref[rs, lanes]
                dd = dd_ref[rs, lanes]
                k = key_rows(k_ref, me, at_row, rows, lanes)
                v = key_rows(v_ref, me, at_row, rows, lanes)
                v_aug = jnp.concatenate([v, jnp.ones_like(v)], axis=1)
                total = jnp.zeros((rows, LANES), F32)
                dk = jnp.zeros((LANES, slots), F32)
                dv = jnp.zeros((LANES, slots), F32)
                for first in range(0, heads, count):
                    at = slice(group * heads + first, group * heads + first + count)
                    do_s = stacked(do, heads, first, count)
                    t = dot_nt(
                        jnp.concatenate([do_s, stacked(dd, heads, first, count)], axis=1), v_aug
                    )
                    p = p_ref[mol, at]
                    dl = p.astype(F32) * t.reshape(count, rows, slots)
                    dl = (dl + dpo_ref[mol, at].astype(F32)).astype(BF)
                    dl_ref[mol, at] = dl
                    dl = dl.reshape(count * rows, slots)
                    total = unstacked(total, dot_nn(dl, k), heads, first, count, rows)
                    dk = dk + dot_tn(stacked(q, heads, first, count), dl)
                    dv = dv + dot_tn(do_s, p.reshape(count * rows, slots))
                dq_ref[rs, lanes] = (total * scale).astype(BF)
                dk_all.append((dk * scale).astype(BF))
                dv_all.append(dv.astype(BF))
            dk_ref[lanes, base : base + mols * slots] = jnp.concatenate(dk_all, axis=1)
            dv_ref[lanes, base : base + mols * slots] = jnp.concatenate(dv_all, axis=1)


def back_kernel(layout, share, parts, ids, *refs):
    dqs, dks, dvs = (refs[i * parts : (i + 1) * parts] for i in range(3))
    a_ref, h_ref, wq, wk, wv, gs_two = refs[3 * parts : 3 * parts + 6]
    own_ref, keep_ref, send_ref, w_send, w_keep = refs[3 * parts + 6 : 3 * parts + 11]
    gq_ref, gk_ref, gv_ref, gs_ref, da_s = refs[3 * parts + 11 :]
    step = pl.program_id(0)
    me = ids[3]
    ranks = a_ref.shape[0]

    @pl.when(step == 0)
    def _():
        for ref in (gq_ref, gk_ref, gv_ref, gs_ref):
            ref[...] = jnp.zeros_like(ref)

    def molecules(ref):
        return jnp.concatenate(
            [
                key_rows(ref, me, start + mol * rows, rows, slice(None))
                for start, mols, rows, slots in layout
                for mol in range(mols)
            ],
            axis=0,
        )

    dq = jnp.concatenate([ref[...] for ref in dqs], axis=0)
    dk = jnp.concatenate([ref[...] for ref in dks], axis=1)
    dv = jnp.concatenate([ref[...] for ref in dvs], axis=1)
    a1 = molecules(a_ref)
    gk_ref[...] += dot_nn(dk, a1)
    gv_ref[...] += dot_nn(dv, a1)
    gq_ref[...] += dot_tn(a_ref[0], dq)
    daq = dot_nt(dq, wq[...])
    across = (((0,), (1,)), ((), ()))
    da = lax.dot_general(dk, wk[...], across, preferred_element_type=F32) + lax.dot_general(
        dv, wv[...], across, preferred_element_type=F32
    )
    da_s[...] = da
    gs_ref[0:1, :] += jnp.sum(da * molecules(h_ref).astype(F32), axis=0, keepdims=True) + jnp.sum(
        daq * h_ref[0].astype(F32), axis=0, keepdims=True
    )
    gs_ref[1:2, :] += jnp.sum(da, axis=0, keepdims=True) + jnp.sum(daq, axis=0, keepdims=True)
    for piece in range(ranks):
        for start, mols, rows, slots in layout:
            for mol in range(mols):
                at = pl.multiple_of(start * ranks + mol * slots + (me ^ piece) * rows, rows)
                value = da_s[pl.ds(at, rows), :]
                to = slice(start + mol * rows, start + (mol + 1) * rows)
                if piece == 0:
                    own_ref[to, :] = value + daq[to]
                elif piece == 2:
                    keep_ref[to, :] = value.astype(BF)
                else:
                    send_ref[piece // 2, to, :] = value.astype(BF)

    @pl.when(step == pl.num_programs(0) - 1)
    def _():
        width = gq_ref.shape[1]
        size = width // CHUNKS
        half = width // 2
        gains = jnp.concatenate(
            [gs_ref[0:2, :], gs_two[0:2, :], jnp.zeros((12, width), F32)], axis=0
        ).astype(BF)
        for value in (0, 1):

            @pl.when(ids[0] == value)
            def _(value=value):
                for ref, owner, mine in ((w_keep, value, ids[1]), (w_send, 1 - value, ids[2])):
                    shard_rows(ref, (gk_ref if owner else gq_ref)[...], 0, share, mine)
                    gv = gv_ref[owner * half : (owner + 1) * half, :]
                    shard_rows(ref, gv, size, share, mine)

        w_keep[CHUNKS * share :, :] = gains
        w_send[CHUNKS * share :, :] = gains


def shard_rows(ref, value, at, rows, mine):
    size = value.shape[0] // CHUNKS
    if isinstance(ref, tuple):
        for chunk in range(CHUNKS):
            place = chunk ^ mine
            to = pl.multiple_of((place % 2) * rows + at, 16)
            for half, part in enumerate(ref):

                @pl.when(place // 2 == half)
                def _(part=part, to=to, chunk=chunk):
                    block = value[chunk * size : (chunk + 1) * size]
                    part[pl.ds(to, size), :] = block.astype(part.dtype)

        return
    for chunk in range(CHUNKS):
        to = pl.multiple_of((chunk ^ mine) * rows + at, 16)
        ref[pl.ds(to, size), :] = value[chunk * size : (chunk + 1) * size].astype(ref.dtype)


def store_by_bucket(refs, value):
    row = 0
    for micro in range(refs[0].shape[0]):
        for ref in refs:
            ref[micro] = value[row : row + ref.shape[1]]
            row += ref.shape[1]


def store_tile(send_ref, keep_ref, value, step, at, half_tiles, rows, ids):
    size = value.shape[0] // CHUNKS

    @pl.when(step < half_tiles)
    def _():
        shard_rows(send_ref, value, (2 * step + at) * size, rows, ids[2])

    @pl.when(step >= half_tiles)
    def _():
        shard_rows(keep_ref, value, (2 * (step - half_tiles) + at) * size, rows, ids[1])


def dense_kernel(
    tiles, rows, ids, x_ref, o_ref, dy_ref, wo, wu, wd, gain, shift,
    yb, ym, ys, dh_ref, do_ref, dd_ref, gs_ref, send_low, send_high, keep_ref,
    a2_s, a2t_s, y_s, xhat_s, inv_s, da_s,
):
    step = pl.program_id(0)
    half_tiles = tiles // 2
    send_ref = (send_low, send_high)

    @pl.when(step == 0)
    def _():
        hidden = x_ref[...].astype(F32) + dot_nn(o_ref[...].astype(BF), wo[...])
        xhat, inv = normalize(hidden)
        y_s[...] = hidden
        xhat_s[...] = xhat
        inv_s[...] = jnp.broadcast_to(inv, inv_s.shape)
        a2 = (xhat * gain[...] + shift[...]).astype(BF)
        a2_s[...] = a2
        a2t_s[...] = a2.T
        da_s[...] = jnp.zeros_like(da_s)

    dy = dy_ref[...]
    u = dot_nn(a2_s[...], wu[...])
    u2 = u * u
    th = jnp.tanh(u * (GELU_C + (GELU_C * GELU_A) * u2))
    half = 0.5 + 0.5 * th
    g = u * half
    slope = half + g * (1.0 - th) * (GELU_C + (3.0 * GELU_C * GELU_A) * u2)
    g = g.astype(BF)
    y_s[...] += dot_nn(g, wd[...])
    store_tile(send_ref, keep_ref, dot_tn(g, dy), step, 1, half_tiles, rows, ids)
    du = (dot_nt(dy, wd[...]) * slope).astype(BF)
    store_tile(send_ref, keep_ref, dot_nn(a2t_s[...], du), step, 0, half_tiles, rows, ids)
    da_s[...] += dot_nt(du, wu[...])

    @pl.when(step == tiles - 1)
    def _():
        store_by_bucket((yb, ym, ys), y_s[...].astype(BF))
        da = da_s[...]
        xhat = xhat_s[...]
        gs_ref[0:1, :] = jnp.sum(da * xhat, axis=0, keepdims=True)
        gs_ref[1:2, :] = jnp.sum(da, axis=0, keepdims=True)
        dh = dy.astype(F32) + norm_back(da, gain[...], xhat, inv_s[:, 0:1])
        dh_ref[...] = dh
        dh = dh.astype(BF)
        o = o_ref[...]
        do = dot_nt(dh, wo[...]).astype(BF)
        do_ref[...] = do
        dd_ref[...] = (-(do.astype(F32) * o)).astype(BF)
        da_s[...] = dot_tn(o.astype(BF), dh)
        width = da.shape[1]
        part = width // 2
        for ref, core, mine in ((send_ref, ids[4], ids[2]), (keep_ref, ids[0], ids[1])):
            value = da_s[pl.ds(pl.multiple_of(core * part, part), part), :]
            shard_rows(ref, value, 2 * half_tiles * (width // CHUNKS), rows, mine)


def last_kernel(parts, x_ref, dh, gain, *refs):
    grads = []
    row = 0
    for part in range(parts):
        own, near, far = refs[3 * part : 3 * part + 3]
        at = slice(row, row + own.shape[0])
        row += own.shape[0]
        xhat, inv = normalize(x_ref[at, :].astype(F32))
        da = own[...] + near[0].astype(F32) + far[...].astype(F32)
        grads.append((dh[at, :] + norm_back(da, gain[...], xhat, inv)).astype(BF))
    store_by_bucket(refs[3 * parts :], jnp.concatenate(grads, axis=0))


def exchange(value, axis, distance, size):
    return lax.ppermute(value, axis, [(i, i ^ distance) for i in range(size)])


def add_low(first, *others):
    total = first.astype(F32)
    for other in others:
        total = total + other.astype(F32)
    return total.astype(BF)


def stage_permutes(sizes):
    rows = sizes["rows"]
    x, y, z_near, z_far = rows, 2, 2 * rows, 4 * rows
    pairs = [(x, y), (y, x), (z_near, z_far), (z_far, z_near)]
    extra = 8
    while extra < sizes["dp"]:
        pairs.append((extra * rows, extra * rows))
        extra *= 2
    total = rows * sizes["dp"]
    return [[(i, i ^ pair[i % 2]) for i in range(total)] for pair in pairs]


def send_all(value, perm):
    return lax.ppermute(value, ("dp", "rows"), perm)


def after(value, *others):
    return lax.optimization_barrier((value,) + others)[0]


def after_all(values, *others):
    return list(lax.optimization_barrier((*values, *others)))[: len(values)]


class SumOverAll:
    def __init__(self, keep, send, tail, sizes):
        self.stages = stage_permutes(sizes)
        self.swap = functools.partial(exchange, axis="rows", distance=1, size=sizes["rows"])
        self.tail = tail
        self.block = (keep.shape[0] - tail) // CHUNKS
        self.size = CHUNKS * self.block
        self.terms = [keep]
        self.send = send

    def cut(self, value, start, stop):
        if not self.tail:
            return value[start:stop]
        return jnp.concatenate([value[start:stop], value[value.shape[0] - self.tail :]], axis=0)

    def split(self, got):
        self.terms.append(got)
        half = self.size // 2
        send = add_low(*[self.cut(v, half, self.size) for v in self.terms])
        self.size = half
        return send

    def reduce(self):
        if isinstance(self.send, tuple):
            half = self.size // 2
            low = self.swap(self.send[0])
            high = yield self.send[1], self.swap
            first = add_low(self.terms[0][half:], high)
            self.size = half
            got = yield first, functools.partial(send_all, perm=self.stages[0])
            self.terms.append(low)
        else:
            got = yield self.send, self.swap
            got = yield self.split(got), functools.partial(send_all, perm=self.stages[0])
        got = yield self.split(got), functools.partial(send_all, perm=self.stages[1])
        part = add_low(*[self.cut(v, 0, self.size) for v in self.terms + [got]])
        for stage in self.stages[2:4]:
            got = yield part, functools.partial(send_all, perm=stage)
            part = add_low(part, got)
        for stage in self.stages[4:]:
            part = add_low(part, send_all(part, stage))
        block = part[: self.block]
        self.own = [part]
        self.other = [self.swap(part)]
        second = yield block, functools.partial(send_all, perm=self.stages[1])
        self.own.append(second)
        self.other.append(self.swap(second))
        low = jnp.concatenate([block, second], axis=0)
        high = yield low, functools.partial(send_all, perm=self.stages[0])
        self.own.append(high)
        got = yield high, self.swap
        self.other.append(got)
        yield None, None

    def begin(self):
        self.run = self.reduce()
        return self.step(None)

    def step(self, got, *deps):
        self.operand, move = self.run.send(got)
        return None if move is None else move(after(self.operand, *deps))


def cost(micros):
    return pl.CostEstimate(flops=0, bytes_accessed=int(micros * 0.8e6), transcendentals=0)


def params():
    return pltpu.CompilerParams(vmem_limit_bytes=LIMIT * MIB)


def shards(sizes, *args):
    atoms, pairs, lengths = args[0:3], args[3:6], args[6:9]
    wq, wk, wv, wo, wu, wd = args[9:15]
    gain_one, shift_one, gain_two, shift_two = (v.reshape(1, -1) for v in args[15:19])
    dys, dpos = args[19:22], args[22:25]
    width = atoms[0].shape[-1]
    micros = atoms[0].shape[0]
    hidden_units = wu.shape[1]
    head_count = pairs[0].shape[2]
    heads = head_count * LANES // width
    scale = float((width // head_count) ** -0.5)
    groups = width // LANES
    ranks = sizes["rows"]

    rows_at = lax.axis_index("rows")
    core, y = rows_at % 2, rows_at // 2
    xa = lax.axis_index("dp") % 2
    order = (xa * 2 + y, y * 2 + xa)
    mine = jnp.where(core == 0, order[0], order[1])
    other = jnp.where(core == 0, order[1], order[0])
    ids = jnp.stack([core, mine, other, rows_at, core ^ 1]).astype(jnp.int32)

    layout = []
    start = 0
    for a in atoms:
        layout.append((start, a.shape[1], a.shape[2], a.shape[2] * ranks))
        start += a.shape[1] * a.shape[2]
    layout = tuple(layout)
    micro_rows = start
    local = micros * micro_rows

    def by_micro(arrays):
        return jnp.concatenate(
            [a.reshape(micros, -1, width) for a in arrays], axis=1
        ).reshape(local, width)

    x = by_micro(atoms)
    dy = by_micro(dys)
    pair = [p.reshape((-1,) + p.shape[2:]) for p in pairs]
    dpo = [p.reshape((-1,) + p.shape[2:]) for p in dpos]
    lens = [n.reshape(-1) for n in lengths]

    near_rows = functools.partial(exchange, axis="rows", distance=1, size=ranks)
    far_rows = functools.partial(exchange, axis="rows", distance=2, size=ranks)
    x2 = far_rows(x)
    x1 = near_rows(x)

    smem = pl.BlockSpec(memory_space=pltpu.SMEM)
    anywhere = pl.BlockSpec(memory_space=pl.ANY)

    def whole(shape):
        return pl.BlockSpec(tuple(shape), lambda *_: (0,) * len(shape))

    def call(kernel, name, micros, grid, operands, in_specs, outs, out_specs, scratch=(), **kw):
        return pl.pallas_call(
            kernel,
            grid_spec=pltpu.PrefetchScalarGridSpec(
                num_scalar_prefetch=1,
                grid=grid,
                in_specs=in_specs,
                out_specs=out_specs,
                scratch_shapes=list(scratch),
            ),
            out_shape=[jax.ShapeDtypeStruct(tuple(shape), kind) for shape, kind in outs],
            compiler_params=params(),
            cost_estimate=cost(micros),
            name=name,
            **kw,
        )(ids, *operands)

    near = 2
    gathered = ((ranks, local, width), BF)
    operands = [x, x1, wq, wk, wv, gain_one, shift_one]
    q, *fronts = call(
        front_kernel,
        "front",
        4,
        (near,),
        operands,
        [whole(v.shape) for v in operands],
        [((local, width), BF)] + [gathered] * 4,
        [whole((local, width))] + [pl.BlockSpec((1, local, width), lambda t, ids: (t, 0, 0))] * 4,
    )
    x2 = after(x2, q, dy, *lens)
    x3 = near_rows(x2)

    row_spec = pl.BlockSpec((micro_rows, width), lambda m, ids: (m, 0))
    rank_spec = pl.BlockSpec((ranks, micro_rows, width), lambda m, ids: (0, m, 0))
    pair_specs = [
        pl.BlockSpec((p.shape[0] // micros,) + p.shape[1:], lambda m, ids: (m, 0, 0, 0))
        for p in pair
    ]
    pair_outs = [(p.shape, BF) for p in pair]
    near_spec = pl.BlockSpec((near, micro_rows, width), lambda m, ids: (0, m, 0))
    far_spec = pl.BlockSpec((ranks - near, micro_rows, width), lambda m, ids: (1, m, 0))
    operands = [*lens, q, x2, x3, wk, wv, gain_one, shift_one, *pair, *fronts]
    res = call(
        functools.partial(attn_fwd_kernel, layout, groups, heads, scale),
        "attend",
        18,
        (micros,),
        operands,
        [smem] * 3
        + [row_spec] * 3
        + [whole(v.shape) for v in operands[6:10]]
        + pair_specs
        + [near_spec] * 2
        + [anywhere] * 2,
        pair_outs * 2 + [((local, width), F32)] + [gathered] * 4,
        pair_specs * 2 + [row_spec] + [far_spec] * 4,
        [pltpu.VMEM((ranks, micro_rows, width), BF)] * 2,
        input_output_aliases={14 + i: 7 + i for i in range(4)},
    )
    o = res[6]
    ks, vs, a1s, xhats = res[7:11]
    pair_out, probs = res[0:3], res[3:6]

    tiles = 4
    tile = hidden_units // tiles
    half = tiles // 2

    def tile_at(t, ids):
        return (t + half * ids[4]) % tiles

    up_spec = pl.BlockSpec((width, tile), lambda t, ids: (0, tile_at(t, ids)))
    down_spec = pl.BlockSpec((tile, width), lambda t, ids: (tile_at(t, ids), 0))
    local_shape = (local, width)
    flat = whole(local_shape)
    ff_rows = (2 * half * tile + width // 2) // CHUNKS
    ff_shape = (CHUNKS * ff_rows, width)
    ff_half = (CHUNKS // 2 * ff_rows, width)
    atom_outs = [((micros, a.shape[1] * a.shape[2], width), BF) for a in atoms]
    atom_specs = [whole(shape) for shape, _ in atom_outs]
    *atoms_out, dh, do, dd, gs_two, ff_low, ff_high, ff_keep = call(
        functools.partial(dense_kernel, tiles, ff_rows),
        "dense",
        16,
        (tiles,),
        [x, o, dy, wo, wu, wd, gain_two, shift_two],
        [flat, flat, flat, whole(wo.shape), up_spec, down_spec] + [whole((1, width))] * 2,
        atom_outs
        + [(local_shape, F32), (local_shape, BF), (local_shape, BF), ((8, width), F32)]
        + [(ff_half, BF), (ff_half, BF), (ff_shape, BF)],
        atom_specs
        + [flat, flat, flat, whole((8, width)), whole(ff_half), whole(ff_half), whole(ff_shape)],
        [
            pltpu.VMEM(local_shape, BF),
            pltpu.VMEM((width, local), BF),
            pltpu.VMEM(local_shape, F32),
            pltpu.VMEM(local_shape, F32),
            pltpu.VMEM((local, LANES), F32),
            pltpu.VMEM(local_shape, F32),
        ],
    )
    ff = SumOverAll(ff_keep, (ff_low, ff_high), 0, sizes)
    moving = ff.step(ff.begin())
    do = after(do, ff.operand)

    dls = []
    dqs, dks, dvs = [], [], []
    for name, buckets in (("attend_back_big", (0,)), ("attend_back_rest", (1, 2))):
        here = tuple(layout[b] for b in buckets)
        rows_here = sum(mols * rows for _, mols, rows, _ in here)
        specs = [pair_specs[b] for b in buckets]
        per, at = micro_rows // rows_here, here[0][0] // rows_here
        rows_spec = pl.BlockSpec(
            (rows_here, width), lambda m, ids, per=per, at=at: (m * per + at, 0)
        )
        ranks_spec = pl.BlockSpec(
            (ranks, rows_here, width), lambda m, ids, per=per, at=at: (0, m * per + at, 0)
        )
        key_spec = pl.BlockSpec((width, rows_here * ranks), lambda m, ids: (0, m))
        key_out = ((width, micros * rows_here * ranks), BF)
        res = call(
            functools.partial(attn_bwd_kernel, here, groups, heads, scale),
            name,
            15,
            (micros,),
            [q, do, dd, ks, vs] + [probs[b] for b in buckets] + [dpo[b] for b in buckets],
            [rows_spec] * 3 + [ranks_spec] * 2 + specs * 2,
            [pair_outs[b] for b in buckets]
            + [((micros * rows_here, width), BF), key_out, key_out],
            specs
            + [pl.BlockSpec((rows_here, width), lambda m, ids: (m, 0)), key_spec, key_spec],
        )
        dls += res[: len(buckets)]
        for values, value in zip((dqs, dks, dvs), res[len(buckets) :]):
            values.append(value)
        moving = ff.step(after(moving, dqs[-1]))
        if len(dqs) == 1:
            do = after(do, ff.operand)
        else:
            dqs[-1] = after(dqs[-1], ff.operand)

    share = (width + width // 2) // CHUNKS
    w_shape = (CHUNKS * share + 16, width)
    operands = [*dqs, *dks, *dvs, a1s, xhats, wq, wk, wv, gs_two]
    own, keep, send, w_send, w_keep = call(
        functools.partial(back_kernel, layout, share, len(dqs)),
        "back",
        9,
        (micros,),
        operands,
        [pl.BlockSpec((v.shape[0] // micros, width), lambda m, ids: (m, 0)) for v in dqs]
        + [pl.BlockSpec((width, v.shape[1] // micros), lambda m, ids: (0, m)) for v in dks + dvs]
        + [rank_spec] * 2
        + [whole(v.shape) for v in operands[-4:]],
        [
            (local_shape, F32),
            (local_shape, BF),
            ((2,) + local_shape, BF),
            (w_shape, BF),
            (w_shape, BF),
        ],
        [
            row_spec,
            row_spec,
            pl.BlockSpec((2, micro_rows, width), lambda m, ids: (0, m, 0)),
            whole(w_shape),
            whole(w_shape),
        ],
        [
            pltpu.VMEM((width, width), F32),
            pltpu.VMEM((width, width), F32),
            pltpu.VMEM((width, width), F32),
            pltpu.VMEM((8, width), F32),
            pltpu.VMEM((ranks * micro_rows, width), F32),
        ],
    )
    moving = ff.step(after(moving, w_send))
    ff_outs = [
        ((CHUNKS, width // CHUNKS, hidden_units), F32),
        ((2, half, CHUNKS, tile // CHUNKS, width), F32),
        ((2, CHUNKS, width // 2 // CHUNKS, width), F32),
    ]

    def finish_ff(name, own, other, first, offsets, old):
        def place(h, j, ids):
            core = jnp.where(h == 0, ids[0], ids[4])
            mine = jnp.where(h == 0, ids[1], ids[2])
            return core, (first + j) ^ mine

        def up_at(h, j, ids):
            core, chunk = place(h, j, ids)
            return chunk, 0, core

        def down_at(h, j, ids):
            core, chunk = place(h, j, ids)
            return core, 0, chunk, 0, 0

        def out_at(h, j, ids):
            core, chunk = place(h, j, ids)
            return core, chunk, 0, 0

        def kernel(ids, *refs):
            gu, gd, go = refs[-3:]
            size = width // CHUNKS
            for h in range(2):
                for j in range(2):

                    @pl.when((pl.program_id(0) == h) & (pl.program_id(1) == j))
                    def _(ref=refs[len(own) * h + j % len(own)], at=offsets[j]):
                        for t in range(half):
                            row = at + 2 * t * size
                            columns = slice(t * tile, (t + 1) * tile)
                            gu[0, :, columns] = ref[row : row + size, :].astype(F32)
                            gd[0, t, 0] = ref[row + size : row + 2 * size, :].astype(F32)
                        row = at + 2 * half * size
                        go[0, 0] = ref[row : row + size // 2, :].astype(F32)

        operands = [*own, *other]
        return call(
            kernel,
            name,
            4,
            (2, 2),
            operands + list(old),
            [whole(v.shape) for v in operands] + [anywhere] * len(old),
            ff_outs,
            [
                pl.BlockSpec((1, width // CHUNKS, half * tile), up_at),
                pl.BlockSpec((1, half, 1, tile // CHUNKS, width), down_at),
                pl.BlockSpec((1, 1, width // 2 // CHUNKS, width), out_at),
            ],
            input_output_aliases={1 + len(operands) + i: i for i in range(len(old))},
        )

    near_da = near_rows(after(send, ff.operand))
    w_sum = SumOverAll(w_keep, after(w_send, ff.operand), 16, sizes)
    w = w_sum.begin()
    far = add_low(keep, near_da[1])
    w = w_sum.step(after(w, far))
    far = far_rows(far)
    w = w_sum.step(w)
    moving = ff.step(after(moving, w_sum.operand))
    far = after(far, ff.operand)
    w = w_sum.step(after(w, far))
    last_args = [x, dh, gain_one, own, near_da, after(far, ff.operand)]
    grad_atoms = call(
        lambda ids, *refs: last_kernel(1, *refs),
        "last",
        2,
        (1,),
        last_args,
        [whole(v.shape) for v in last_args],
        atom_outs,
        atom_specs,
    )
    w = w_sum.step(after(w, grad_atoms[0]))
    moving = ff.step(after(moving, w_sum.operand))
    w = w_sum.step(after(w, ff.operand))
    grads = finish_ff(
        "finish_ff_early", ff.own, after_all(ff.other, w_sum.operand), 0, (0, 0), []
    )
    w = w_sum.step(after(w, *grads))
    moving = ff.step(after(moving, w_sum.operand))
    ff.step(moving)
    grad_up, grad_down, go = finish_ff(
        "finish_ff", ff.own[2:], ff.other[2:], 2, (0, ff_rows), grads
    )

    def ordered(pieces, at, size, rows, mine):
        blocks = []
        for chunk in range(CHUNKS):
            place = chunk ^ mine
            start = at + (rows if place == 3 else 0)
            blocks.append(pieces[min(place, 2)][pl.ds(start, size), :])
        return jnp.concatenate(blocks, axis=0)

    def for_each_order(mine, put):
        for value in range(CHUNKS):
            pl.when(mine == value)(lambda value=value: put(value))

    w = w_sum.step(after(w, grad_down))
    w_sum.step(w)

    def finish_rest(ids, *refs):
        own_refs, other_refs = refs[0:3], refs[3:6]
        gq_out, gk_out, gv_out = refs[6:9]
        gains = refs[9:13]
        size = width // CHUNKS

        def put_zero(refs, mine):
            gq_out[...] = ordered(refs, 0, size, share, mine).astype(F32)
            gv_out[:, : width // 2] = ordered(refs, size, size // 2, share, mine).T.astype(F32)

        def put_gains(ref):
            rows = ref[share : share + 16, :].astype(F32)
            for at, out in enumerate(gains):
                out[...] = rows[at]

        def put_one(refs, mine):
            gk_out[...] = ordered(refs, 0, size, share, mine).T.astype(F32)
            gv_out[:, width // 2 :] = ordered(refs, size, size // 2, share, mine).T.astype(F32)

        @pl.when(ids[0] == 0)
        def _():
            for_each_order(ids[1], functools.partial(put_zero, own_refs))
            for_each_order(ids[2], functools.partial(put_one, other_refs))
            put_gains(own_refs[0])

        @pl.when(ids[0] == 1)
        def _():
            for_each_order(ids[2], functools.partial(put_zero, other_refs))
            for_each_order(ids[1], functools.partial(put_one, own_refs))
            put_gains(other_refs[0])

    pieces = w_sum.own + w_sum.other
    gq, gk, gv, *gs = call(
        finish_rest,
        "finish_rest",
        3,
        (1,),
        pieces,
        [whole(v.shape) for v in pieces],
        [(wq.shape, F32)] * 3 + [((width,), F32)] * 4,
        [whole(wq.shape)] * 3 + [whole((width,))] * 4,
    )

    return (
        *[v.reshape(a.shape) for v, a in zip(atoms_out, atoms)],
        *[v.reshape(a.shape) for v, a in zip(pair_out, pairs)],
        *[v.reshape(a.shape) for v, a in zip(grad_atoms, atoms)],
        *[v.reshape(a.shape) for v, a in zip(dls, pairs)],
        gq,
        gk,
        gv,
        go.reshape(wo.shape),
        grad_up.reshape(wu.shape),
        grad_down.reshape(wd.shape),
        *gs,
    )


def solution(mesh):
    atom = P(None, "dp", "rows", None)
    pair = P(None, "dp", None, "rows", None)
    length = P(None, "dp")
    in_specs = (
        (atom,) * 3 + (pair,) * 3 + (length,) * 3 + (P(),) * 10 + (atom,) * 3 + (pair,) * 3
    )
    out_specs = (atom,) * 3 + (pair,) * 3 + (atom,) * 3 + (pair,) * 3 + (P(),) * 10
    body = functools.partial(shards, dict(mesh.shape))
    return jax.shard_map(
        body, mesh=mesh, in_specs=in_specs, out_specs=out_specs, check_vma=False
    )
```

```python
import functools

import jax
import jax.numpy as jnp
from jax import lax
from jax.experimental import pallas as pl
from jax.experimental.pallas import tpu as pltpu
from jax.sharding import PartitionSpec as P

EPSILON = 1e-05
MASKED = -1e30
BF = jnp.bfloat16
F32 = jnp.float32
LANES = 128
GELU_C = 0.7978845608028654
GELU_A = 0.044715
MIB = 1 << 20
CHUNKS = 4
LIMIT = 50


def dot_nn(a, b):
    return lax.dot_general(a, b, (((1,), (0,)), ((), ())), preferred_element_type=F32)


def dot_nt(a, b):
    return lax.dot_general(a, b, (((1,), (1,)), ((), ())), preferred_element_type=F32)


def dot_tn(a, b):
    return lax.dot_general(a, b, (((0,), (0,)), ((), ())), preferred_element_type=F32)


def normalize(x):
    centred = x - jnp.mean(x, axis=-1, keepdims=True)
    spread = jnp.mean(centred * centred, axis=-1, keepdims=True)
    inv = lax.rsqrt(spread + EPSILON)
    return centred * inv, inv


def norm_back(grad, gain, xhat, inv):
    g = grad * gain
    return inv * (
        g
        - jnp.mean(g, axis=-1, keepdims=True)
        - xhat * jnp.mean(g * xhat, axis=-1, keepdims=True)
    )


def front_kernel(ids, x0, x1, wq, wk, wv, gain, shift, q_out, *outs):
    for piece, x_ref in enumerate((x0, x1)):

        @pl.when(pl.program_id(0) == piece)
        def _(piece=piece, x_ref=x_ref):
            a1 = front_rows(x_ref[...], gain, shift, wk, wv, [out.at[0] for out in outs])
            if piece == 0:
                q_out[...] = dot_nn(a1, wq[...]).astype(BF)


def front_rows(x, gain, shift, wk, wv, outs):
    xhat, _ = normalize(x.astype(F32))
    a1 = (xhat * gain[...] + shift[...]).astype(BF)
    outs[0][...] = dot_nn(a1, wk[...]).astype(BF)
    outs[1][...] = dot_nn(a1, wv[...]).astype(BF)
    outs[2][...] = a1
    outs[3][...] = xhat.astype(BF)
    return a1


def head_mask(heads, first):
    lane = lax.broadcasted_iota(jnp.int32, (1, LANES), 1) // (LANES // heads)
    return lane == first


def stacked(block, heads, first, count):
    zero = jnp.zeros_like(block)
    return jnp.concatenate(
        [jnp.where(head_mask(heads, first + t), block, zero) for t in range(count)], axis=0
    )


def unstacked(total, product, heads, first, count, rows):
    for t in range(count):
        part = product[t * rows : (t + 1) * rows]
        total = total + jnp.where(head_mask(heads, first + t), part, 0.0)
    return total


def key_rows(ref, me, start, rows, lanes):
    return jnp.concatenate(
        [ref[me ^ r, start : start + rows, lanes] for r in range(ref.shape[0])], axis=0
    )


def attn_fwd_kernel(layout, groups, heads, scale, ids, *refs):
    lens, q_ref, far_xs, weights, pairs = refs[0:3], refs[3], refs[4:6], refs[6:10], refs[10:13]
    k_near, v_near = refs[13:15]
    pouts, ps, o_ref, fronts, (k_ref, v_ref) = (
        refs[17:20], refs[20:23], refs[23], refs[24:28], refs[28:30]
    )
    wk, wv, gain, shift = weights
    me = ids[3]
    near = k_near.shape[0]
    for i in range(near):
        k_ref[i] = k_near[i]
        v_ref[i] = v_near[i]
    for i, x_ref in enumerate(far_xs):
        front_rows(x_ref[...], gain, shift, wk, wv, [out.at[i] for out in fronts])
        k_ref[near + i] = fronts[0][i]
        v_ref[near + i] = fronts[1][i]
    for (start, mols, rows, slots), len_ref, pair_ref, pout_ref, p_ref in zip(
        layout, lens, pairs, pouts, ps
    ):
        count = min(heads, max(1, 512 // rows))
        for mol in range(mols):
            length = len_ref[pl.program_id(0) * mols + mol]
            key_at = lax.broadcasted_iota(jnp.int32, (1, 1, slots), 2)
            mask = jnp.where(key_at < length, 0.0, MASKED)
            at_row = start + mol * rows
            for group in range(groups):
                lanes = slice(group * LANES, (group + 1) * LANES)
                q = q_ref[at_row : at_row + rows, lanes]
                k = key_rows(k_ref, me, at_row, rows, lanes)
                v = key_rows(v_ref, me, at_row, rows, lanes)
                total = jnp.zeros((rows, LANES), F32)
                for first in range(0, heads, count):
                    at = slice(group * heads + first, group * heads + first + count)
                    s = dot_nt(stacked(q, heads, first, count), k)
                    s = s.reshape(count, rows, slots) * scale + pair_ref[mol, at].astype(F32)
                    pout_ref[mol, at] = s.astype(BF)
                    s = s + mask
                    e = jnp.exp(s - jnp.max(s, axis=-1, keepdims=True))
                    p = (e * (1.0 / jnp.sum(e, axis=-1, keepdims=True))).astype(BF)
                    p_ref[mol, at] = p
                    pv = dot_nn(p.reshape(count * rows, slots), v)
                    total = unstacked(total, pv, heads, first, count, rows)
                o_ref[at_row : at_row + rows, lanes] = total


def attn_bwd_kernel(layout, groups, heads, scale, ids, *refs):
    me = ids[3]
    count_of = len(layout)
    q_ref, do_ref, dd_ref, k_ref, v_ref = refs[0:5]
    ps, dpos = refs[5 : 5 + count_of], refs[5 + count_of : 5 + 2 * count_of]
    dls = refs[5 + 2 * count_of : 5 + 3 * count_of]
    dq_ref, dk_ref, dv_ref = refs[5 + 3 * count_of :]
    ranks = k_ref.shape[0]
    origin = layout[0][0]
    for (start, mols, rows, slots), p_ref, dpo_ref, dl_ref in zip(layout, ps, dpos, dls):
        count = min(heads, max(1, 1024 // rows))
        base = (start - origin) * ranks
        for group in range(groups):
            lanes = slice(group * LANES, (group + 1) * LANES)
            dk_all = []
            dv_all = []
            for mol in range(mols):
                at_row = start - origin + mol * rows
                rs = slice(at_row, at_row + rows)
                q = q_ref[rs, lanes]
                do = do_ref[rs, lanes]
                dd = dd_ref[rs, lanes]
                k = key_rows(k_ref, me, at_row, rows, lanes)
                v = key_rows(v_ref, me, at_row, rows, lanes)
                v_aug = jnp.concatenate([v, jnp.ones_like(v)], axis=1)
                total = jnp.zeros((rows, LANES), F32)
                dk = jnp.zeros((LANES, slots), F32)
                dv = jnp.zeros((LANES, slots), F32)
                for first in range(0, heads, count):
                    at = slice(group * heads + first, group * heads + first + count)
                    do_s = stacked(do, heads, first, count)
                    t = dot_nt(
                        jnp.concatenate([do_s, stacked(dd, heads, first, count)], axis=1), v_aug
                    )
                    p = p_ref[mol, at]
                    dl = p.astype(F32) * t.reshape(count, rows, slots)
                    dl = (dl + dpo_ref[mol, at].astype(F32)).astype(BF)
                    dl_ref[mol, at] = dl
                    dl = dl.reshape(count * rows, slots)
                    total = unstacked(total, dot_nn(dl, k), heads, first, count, rows)
                    dk = dk + dot_tn(stacked(q, heads, first, count), dl)
                    dv = dv + dot_tn(do_s, p.reshape(count * rows, slots))
                dq_ref[rs, lanes] = (total * scale).astype(BF)
                dk_all.append((dk * scale).astype(BF))
                dv_all.append(dv.astype(BF))
            dk_ref[lanes, base : base + mols * slots] = jnp.concatenate(dk_all, axis=1)
            dv_ref[lanes, base : base + mols * slots] = jnp.concatenate(dv_all, axis=1)


def back_kernel(layout, share, parts, ids, *refs):
    dqs, dks, dvs = (refs[i * parts : (i + 1) * parts] for i in range(3))
    a_ref, h_ref, wq, wk, wv, gs_two = refs[3 * parts : 3 * parts + 6]
    own_ref, keep_ref, send_ref, w_send, w_keep = refs[3 * parts + 6 : 3 * parts + 11]
    gq_ref, gk_ref, gv_ref, gs_ref, da_s = refs[3 * parts + 11 :]
    step = pl.program_id(0)
    me = ids[3]
    ranks = a_ref.shape[0]

    @pl.when(step == 0)
    def _():
        for ref in (gq_ref, gk_ref, gv_ref, gs_ref):
            ref[...] = jnp.zeros_like(ref)

    def molecules(ref):
        return jnp.concatenate(
            [
                key_rows(ref, me, start + mol * rows, rows, slice(None))
                for start, mols, rows, slots in layout
                for mol in range(mols)
            ],
            axis=0,
        )

    dq = jnp.concatenate([ref[...] for ref in dqs], axis=0)
    dk = jnp.concatenate([ref[...] for ref in dks], axis=1)
    dv = jnp.concatenate([ref[...] for ref in dvs], axis=1)
    a1 = molecules(a_ref)
    gk_ref[...] += dot_nn(dk, a1)
    gv_ref[...] += dot_nn(dv, a1)
    gq_ref[...] += dot_tn(a_ref[0], dq)
    daq = dot_nt(dq, wq[...])
    across = (((0,), (1,)), ((), ()))
    da = lax.dot_general(dk, wk[...], across, preferred_element_type=F32) + lax.dot_general(
        dv, wv[...], across, preferred_element_type=F32
    )
    da_s[...] = da
    gs_ref[0:1, :] += jnp.sum(da * molecules(h_ref).astype(F32), axis=0, keepdims=True) + jnp.sum(
        daq * h_ref[0].astype(F32), axis=0, keepdims=True
    )
    gs_ref[1:2, :] += jnp.sum(da, axis=0, keepdims=True) + jnp.sum(daq, axis=0, keepdims=True)
    for piece in range(ranks):
        for start, mols, rows, slots in layout:
            for mol in range(mols):
                at = pl.multiple_of(start * ranks + mol * slots + (me ^ piece) * rows, rows)
                value = da_s[pl.ds(at, rows), :]
                to = slice(start + mol * rows, start + (mol + 1) * rows)
                if piece == 0:
                    own_ref[to, :] = value + daq[to]
                elif piece == 2:
                    keep_ref[to, :] = value.astype(BF)
                else:
                    send_ref[piece // 2, to, :] = value.astype(BF)

    @pl.when(step == pl.num_programs(0) - 1)
    def _():
        width = gq_ref.shape[1]
        size = width // CHUNKS
        half = width // 2
        gains = jnp.concatenate(
            [gs_ref[0:2, :], gs_two[0:2, :], jnp.zeros((12, width), F32)], axis=0
        ).astype(BF)
        for value in (0, 1):

            @pl.when(ids[0] == value)
            def _(value=value):
                for ref, owner, mine in ((w_keep, value, ids[1]), (w_send, 1 - value, ids[2])):
                    shard_rows(ref, (gk_ref if owner else gq_ref)[...], 0, share, mine)
                    gv = gv_ref[owner * half : (owner + 1) * half, :]
                    shard_rows(ref, gv, size, share, mine)

        w_keep[CHUNKS * share :, :] = gains
        w_send[CHUNKS * share :, :] = gains


def shard_rows(ref, value, at, rows, mine):
    size = value.shape[0] // CHUNKS
    if isinstance(ref, tuple):
        for chunk in range(CHUNKS):
            place = chunk ^ mine
            to = pl.multiple_of((place % 2) * rows + at, 16)
            for half, part in enumerate(ref):

                @pl.when(place // 2 == half)
                def _(part=part, to=to, chunk=chunk):
                    block = value[chunk * size : (chunk + 1) * size]
                    part[pl.ds(to, size), :] = block.astype(part.dtype)

        return
    for chunk in range(CHUNKS):
        to = pl.multiple_of((chunk ^ mine) * rows + at, 16)
        ref[pl.ds(to, size), :] = value[chunk * size : (chunk + 1) * size].astype(ref.dtype)


def store_by_bucket(refs, value):
    row = 0
    for micro in range(refs[0].shape[0]):
        for ref in refs:
            ref[micro] = value[row : row + ref.shape[1]]
            row += ref.shape[1]


def store_tile(send_ref, keep_ref, value, step, at, half_tiles, rows, ids):
    size = value.shape[0] // CHUNKS

    @pl.when(step < half_tiles)
    def _():
        shard_rows(send_ref, value, (2 * step + at) * size, rows, ids[2])

    @pl.when(step >= half_tiles)
    def _():
        shard_rows(keep_ref, value, (2 * (step - half_tiles) + at) * size, rows, ids[1])


def dense_kernel(
    tiles, rows, ids, x_ref, o_ref, dy_ref, wo, wu, wd, gain, shift,
    yb, ym, ys, dh_ref, do_ref, dd_ref, gs_ref, send_low, send_high, keep_ref,
    a2_s, a2t_s, y_s, xhat_s, inv_s, da_s,
):
    step = pl.program_id(0)
    half_tiles = tiles // 2
    send_ref = (send_low, send_high)

    @pl.when(step == 0)
    def _():
        hidden = x_ref[...].astype(F32) + dot_nn(o_ref[...].astype(BF), wo[...])
        xhat, inv = normalize(hidden)
        y_s[...] = hidden
        xhat_s[...] = xhat
        inv_s[...] = jnp.broadcast_to(inv, inv_s.shape)
        a2 = (xhat * gain[...] + shift[...]).astype(BF)
        a2_s[...] = a2
        a2t_s[...] = a2.T
        da_s[...] = jnp.zeros_like(da_s)

    dy = dy_ref[...]
    u = dot_nn(a2_s[...], wu[...])
    u2 = u * u
    th = jnp.tanh(u * (GELU_C + (GELU_C * GELU_A) * u2))
    half = 0.5 + 0.5 * th
    g = u * half
    slope = half + g * (1.0 - th) * (GELU_C + (3.0 * GELU_C * GELU_A) * u2)
    g = g.astype(BF)
    y_s[...] += dot_nn(g, wd[...])
    store_tile(send_ref, keep_ref, dot_tn(g, dy), step, 1, half_tiles, rows, ids)
    du = (dot_nt(dy, wd[...]) * slope).astype(BF)
    store_tile(send_ref, keep_ref, dot_nn(a2t_s[...], du), step, 0, half_tiles, rows, ids)
    da_s[...] += dot_nt(du, wu[...])

    @pl.when(step == tiles - 1)
    def _():
        store_by_bucket((yb, ym, ys), y_s[...].astype(BF))
        da = da_s[...]
        xhat = xhat_s[...]
        gs_ref[0:1, :] = jnp.sum(da * xhat, axis=0, keepdims=True)
        gs_ref[1:2, :] = jnp.sum(da, axis=0, keepdims=True)
        dh = dy.astype(F32) + norm_back(da, gain[...], xhat, inv_s[:, 0:1])
        dh_ref[...] = dh
        dh = dh.astype(BF)
        o = o_ref[...]
        do = dot_nt(dh, wo[...]).astype(BF)
        do_ref[...] = do
        dd_ref[...] = (-(do.astype(F32) * o)).astype(BF)
        da_s[...] = dot_tn(o.astype(BF), dh)
        width = da.shape[1]
        part = width // 2
        for ref, core, mine in ((send_ref, ids[4], ids[2]), (keep_ref, ids[0], ids[1])):
            value = da_s[pl.ds(pl.multiple_of(core * part, part), part), :]
            shard_rows(ref, value, 2 * half_tiles * (width // CHUNKS), rows, mine)


def last_kernel(parts, x_ref, dh, gain, *refs):
    grads = []
    row = 0
    for part in range(parts):
        own, near, far = refs[3 * part : 3 * part + 3]
        at = slice(row, row + own.shape[0])
        row += own.shape[0]
        xhat, inv = normalize(x_ref[at, :].astype(F32))
        da = own[...] + near[0].astype(F32) + far[...].astype(F32)
        grads.append((dh[at, :] + norm_back(da, gain[...], xhat, inv)).astype(BF))
    store_by_bucket(refs[3 * parts :], jnp.concatenate(grads, axis=0))


def exchange(value, axis, distance, size):
    return lax.ppermute(value, axis, [(i, i ^ distance) for i in range(size)])


def add_low(first, *others):
    total = first.astype(F32)
    for other in others:
        total = total + other.astype(F32)
    return total.astype(BF)


def stage_permutes(sizes):
    rows = sizes["rows"]
    x, y, z_near, z_far = rows, 2, 2 * rows, 4 * rows
    pairs = [(x, y), (y, x), (z_near, z_far), (z_far, z_near)]
    extra = 8
    while extra < sizes["dp"]:
        pairs.append((extra * rows, extra * rows))
        extra *= 2
    total = rows * sizes["dp"]
    return [[(i, i ^ pair[i % 2]) for i in range(total)] for pair in pairs]


def send_all(value, perm):
    return lax.ppermute(value, ("dp", "rows"), perm)


def after(value, *others):
    return lax.optimization_barrier((value,) + others)[0]


def after_all(values, *others):
    return list(lax.optimization_barrier((*values, *others)))[: len(values)]


class SumOverAll:
    def __init__(self, keep, send, tail, sizes):
        self.stages = stage_permutes(sizes)
        self.swap = functools.partial(exchange, axis="rows", distance=1, size=sizes["rows"])
        self.tail = tail
        self.block = (keep.shape[0] - tail) // CHUNKS
        self.size = CHUNKS * self.block
        self.terms = [keep]
        self.send = send

    def cut(self, value, start, stop):
        if not self.tail:
            return value[start:stop]
        return jnp.concatenate([value[start:stop], value[value.shape[0] - self.tail :]], axis=0)

    def split(self, got):
        self.terms.append(got)
        half = self.size // 2
        send = add_low(*[self.cut(v, half, self.size) for v in self.terms])
        self.size = half
        return send

    def reduce(self):
        if isinstance(self.send, tuple):
            half = self.size // 2
            low = self.swap(self.send[0])
            high = yield self.send[1], self.swap
            first = add_low(self.terms[0][half:], high)
            self.size = half
            got = yield first, functools.partial(send_all, perm=self.stages[0])
            self.terms.append(low)
        else:
            got = yield self.send, self.swap
            got = yield self.split(got), functools.partial(send_all, perm=self.stages[0])
        got = yield self.split(got), functools.partial(send_all, perm=self.stages[1])
        part = add_low(*[self.cut(v, 0, self.size) for v in self.terms + [got]])
        for stage in self.stages[2:4]:
            got = yield part, functools.partial(send_all, perm=stage)
            part = add_low(part, got)
        for stage in self.stages[4:]:
            part = add_low(part, send_all(part, stage))
        block = part[: self.block]
        self.own = [part]
        self.other = [self.swap(part)]
        second = yield block, functools.partial(send_all, perm=self.stages[1])
        self.own.append(second)
        self.other.append(self.swap(second))
        low = jnp.concatenate([block, second], axis=0)
        high = yield low, functools.partial(send_all, perm=self.stages[0])
        self.own.append(high)
        got = yield high, self.swap
        self.other.append(got)
        yield None, None

    def begin(self):
        self.run = self.reduce()
        return self.step(None)

    def step(self, got, *deps):
        self.operand, move = self.run.send(got)
        return None if move is None else move(after(self.operand, *deps))


def cost(micros):
    return pl.CostEstimate(flops=0, bytes_accessed=int(micros * 0.8e6), transcendentals=0)


def params():
    return pltpu.CompilerParams(vmem_limit_bytes=LIMIT * MIB)


def shards(sizes, *args):
    atoms, pairs, lengths = args[0:3], args[3:6], args[6:9]
    wq, wk, wv, wo, wu, wd = args[9:15]
    gain_one, shift_one, gain_two, shift_two = (v.reshape(1, -1) for v in args[15:19])
    dys, dpos = args[19:22], args[22:25]
    width = atoms[0].shape[-1]
    micros = atoms[0].shape[0]
    hidden_units = wu.shape[1]
    head_count = pairs[0].shape[2]
    heads = head_count * LANES // width
    scale = float((width // head_count) ** -0.5)
    groups = width // LANES
    ranks = sizes["rows"]

    rows_at = lax.axis_index("rows")
    core, y = rows_at % 2, rows_at // 2
    xa = lax.axis_index("dp") % 2
    order = (xa * 2 + y, y * 2 + xa)
    mine = jnp.where(core == 0, order[0], order[1])
    other = jnp.where(core == 0, order[1], order[0])
    ids = jnp.stack([core, mine, other, rows_at, core ^ 1]).astype(jnp.int32)

    layout = []
    start = 0
    for a in atoms:
        layout.append((start, a.shape[1], a.shape[2], a.shape[2] * ranks))
        start += a.shape[1] * a.shape[2]
    layout = tuple(layout)
    micro_rows = start
    local = micros * micro_rows

    def by_micro(arrays):
        return jnp.concatenate(
            [a.reshape(micros, -1, width) for a in arrays], axis=1
        ).reshape(local, width)

    x = by_micro(atoms)
    dy = by_micro(dys)
    pair = [p.reshape((-1,) + p.shape[2:]) for p in pairs]
    dpo = [p.reshape((-1,) + p.shape[2:]) for p in dpos]
    lens = [n.reshape(-1) for n in lengths]

    near_rows = functools.partial(exchange, axis="rows", distance=1, size=ranks)
    far_rows = functools.partial(exchange, axis="rows", distance=2, size=ranks)
    x2 = far_rows(x)
    x1 = near_rows(x)

    smem = pl.BlockSpec(memory_space=pltpu.SMEM)
    anywhere = pl.BlockSpec(memory_space=pl.ANY)

    def whole(shape):
        return pl.BlockSpec(tuple(shape), lambda *_: (0,) * len(shape))

    def call(kernel, name, micros, grid, operands, in_specs, outs, out_specs, scratch=(), **kw):
        return pl.pallas_call(
            kernel,
            grid_spec=pltpu.PrefetchScalarGridSpec(
                num_scalar_prefetch=1,
                grid=grid,
                in_specs=in_specs,
                out_specs=out_specs,
                scratch_shapes=list(scratch),
            ),
            out_shape=[jax.ShapeDtypeStruct(tuple(shape), kind) for shape, kind in outs],
            compiler_params=params(),
            cost_estimate=cost(micros),
            name=name,
            **kw,
        )(ids, *operands)

    near = 2
    gathered = ((ranks, local, width), BF)
    operands = [x, x1, wq, wk, wv, gain_one, shift_one]
    q, *fronts = call(
        front_kernel,
        "front",
        4,
        (near,),
        operands,
        [whole(v.shape) for v in operands],
        [((local, width), BF)] + [gathered] * 4,
        [whole((local, width))] + [pl.BlockSpec((1, local, width), lambda t, ids: (t, 0, 0))] * 4,
    )
    x2 = after(x2, q, dy, *lens)
    x3 = near_rows(x2)

    row_spec = pl.BlockSpec((micro_rows, width), lambda m, ids: (m, 0))
    rank_spec = pl.BlockSpec((ranks, micro_rows, width), lambda m, ids: (0, m, 0))
    pair_specs = [
        pl.BlockSpec((p.shape[0] // micros,) + p.shape[1:], lambda m, ids: (m, 0, 0, 0))
        for p in pair
    ]
    pair_outs = [(p.shape, BF) for p in pair]
    near_spec = pl.BlockSpec((near, micro_rows, width), lambda m, ids: (0, m, 0))
    far_spec = pl.BlockSpec((ranks - near, micro_rows, width), lambda m, ids: (1, m, 0))
    operands = [*lens, q, x2, x3, wk, wv, gain_one, shift_one, *pair, *fronts]
    res = call(
        functools.partial(attn_fwd_kernel, layout, groups, heads, scale),
        "attend",
        18,
        (micros,),
        operands,
        [smem] * 3
        + [row_spec] * 3
        + [whole(v.shape) for v in operands[6:10]]
        + pair_specs
        + [near_spec] * 2
        + [anywhere] * 2,
        pair_outs * 2 + [((local, width), F32)] + [gathered] * 4,
        pair_specs * 2 + [row_spec] + [far_spec] * 4,
        [pltpu.VMEM((ranks, micro_rows, width), BF)] * 2,
        input_output_aliases={14 + i: 7 + i for i in range(4)},
    )
    o = res[6]
    ks, vs, a1s, xhats = res[7:11]
    pair_out, probs = res[0:3], res[3:6]

    tiles = 4
    tile = hidden_units // tiles
    half = tiles // 2

    def tile_at(t, ids):
        return (t + half * ids[4]) % tiles

    up_spec = pl.BlockSpec((width, tile), lambda t, ids: (0, tile_at(t, ids)))
    down_spec = pl.BlockSpec((tile, width), lambda t, ids: (tile_at(t, ids), 0))
    local_shape = (local, width)
    flat = whole(local_shape)
    ff_rows = (2 * half * tile + width // 2) // CHUNKS
    ff_shape = (CHUNKS * ff_rows, width)
    ff_half = (CHUNKS // 2 * ff_rows, width)
    atom_outs = [((micros, a.shape[1] * a.shape[2], width), BF) for a in atoms]
    atom_specs = [whole(shape) for shape, _ in atom_outs]
    *atoms_out, dh, do, dd, gs_two, ff_low, ff_high, ff_keep = call(
        functools.partial(dense_kernel, tiles, ff_rows),
        "dense",
        16,
        (tiles,),
        [x, o, dy, wo, wu, wd, gain_two, shift_two],
        [flat, flat, flat, whole(wo.shape), up_spec, down_spec] + [whole((1, width))] * 2,
        atom_outs
        + [(local_shape, F32), (local_shape, BF), (local_shape, BF), ((8, width), F32)]
        + [(ff_half, BF), (ff_half, BF), (ff_shape, BF)],
        atom_specs
        + [flat, flat, flat, whole((8, width)), whole(ff_half), whole(ff_half), whole(ff_shape)],
        [
            pltpu.VMEM(local_shape, BF),
            pltpu.VMEM((width, local), BF),
            pltpu.VMEM(local_shape, F32),
            pltpu.VMEM(local_shape, F32),
            pltpu.VMEM((local, LANES), F32),
            pltpu.VMEM(local_shape, F32),
        ],
    )
    ff = SumOverAll(ff_keep, (ff_low, ff_high), 0, sizes)
    moving = ff.step(ff.begin())
    do = after(do, ff.operand)

    dls = []
    dqs, dks, dvs = [], [], []
    for name, buckets in (("attend_back_big", (0,)), ("attend_back_rest", (1, 2))):
        here = tuple(layout[b] for b in buckets)
        rows_here = sum(mols * rows for _, mols, rows, _ in here)
        specs = [pair_specs[b] for b in buckets]
        per, at = micro_rows // rows_here, here[0][0] // rows_here
        rows_spec = pl.BlockSpec(
            (rows_here, width), lambda m, ids, per=per, at=at: (m * per + at, 0)
        )
        ranks_spec = pl.BlockSpec(
            (ranks, rows_here, width), lambda m, ids, per=per, at=at: (0, m * per + at, 0)
        )
        key_spec = pl.BlockSpec((width, rows_here * ranks), lambda m, ids: (0, m))
        key_out = ((width, micros * rows_here * ranks), BF)
        res = call(
            functools.partial(attn_bwd_kernel, here, groups, heads, scale),
            name,
            15,
            (micros,),
            [q, do, dd, ks, vs] + [probs[b] for b in buckets] + [dpo[b] for b in buckets],
            [rows_spec] * 3 + [ranks_spec] * 2 + specs * 2,
            [pair_outs[b] for b in buckets]
            + [((micros * rows_here, width), BF), key_out, key_out],
            specs
            + [pl.BlockSpec((rows_here, width), lambda m, ids: (m, 0)), key_spec, key_spec],
        )
        dls += res[: len(buckets)]
        for values, value in zip((dqs, dks, dvs), res[len(buckets) :]):
            values.append(value)
        moving = ff.step(after(moving, dqs[-1]))
        if len(dqs) == 1:
            do = after(do, ff.operand)
        else:
            dqs[-1] = after(dqs[-1], ff.operand)

    share = (width + width // 2) // CHUNKS
    w_shape = (CHUNKS * share + 16, width)
    operands = [*dqs, *dks, *dvs, a1s, xhats, wq, wk, wv, gs_two]
    own, keep, send, w_send, w_keep = call(
        functools.partial(back_kernel, layout, share, len(dqs)),
        "back",
        9,
        (micros,),
        operands,
        [pl.BlockSpec((v.shape[0] // micros, width), lambda m, ids: (m, 0)) for v in dqs]
        + [pl.BlockSpec((width, v.shape[1] // micros), lambda m, ids: (0, m)) for v in dks + dvs]
        + [rank_spec] * 2
        + [whole(v.shape) for v in operands[-4:]],
        [
            (local_shape, F32),
            (local_shape, BF),
            ((2,) + local_shape, BF),
            (w_shape, BF),
            (w_shape, BF),
        ],
        [
            row_spec,
            row_spec,
            pl.BlockSpec((2, micro_rows, width), lambda m, ids: (0, m, 0)),
            whole(w_shape),
            whole(w_shape),
        ],
        [
            pltpu.VMEM((width, width), F32),
            pltpu.VMEM((width, width), F32),
            pltpu.VMEM((width, width), F32),
            pltpu.VMEM((8, width), F32),
            pltpu.VMEM((ranks * micro_rows, width), F32),
        ],
    )
    moving = ff.step(after(moving, w_send))
    ff_outs = [
        ((CHUNKS, width // CHUNKS, hidden_units), F32),
        ((2, half, CHUNKS, tile // CHUNKS, width), F32),
        ((2, CHUNKS, width // 2 // CHUNKS, width), F32),
    ]

    def finish_ff(name, own, other, first, offsets, old):
        def place(h, j, ids):
            core = jnp.where(h == 0, ids[0], ids[4])
            mine = jnp.where(h == 0, ids[1], ids[2])
            return core, (first + j) ^ mine

        def up_at(h, j, ids):
            core, chunk = place(h, j, ids)
            return chunk, 0, core

        def down_at(h, j, ids):
            core, chunk = place(h, j, ids)
            return core, 0, chunk, 0, 0

        def out_at(h, j, ids):
            core, chunk = place(h, j, ids)
            return core, chunk, 0, 0

        def kernel(ids, *refs):
            gu, gd, go = refs[-3:]
            size = width // CHUNKS
            for h in range(2):
                for j in range(2):

                    @pl.when((pl.program_id(0) == h) & (pl.program_id(1) == j))
                    def _(ref=refs[len(own) * h + j % len(own)], at=offsets[j]):
                        for t in range(half):
                            row = at + 2 * t * size
                            columns = slice(t * tile, (t + 1) * tile)
                            gu[0, :, columns] = ref[row : row + size, :].astype(F32)
                            gd[0, t, 0] = ref[row + size : row + 2 * size, :].astype(F32)
                        row = at + 2 * half * size
                        go[0, 0] = ref[row : row + size // 2, :].astype(F32)

        operands = [*own, *other]
        return call(
            kernel,
            name,
            4,
            (2, 2),
            operands + list(old),
            [whole(v.shape) for v in operands] + [anywhere] * len(old),
            ff_outs,
            [
                pl.BlockSpec((1, width // CHUNKS, half * tile), up_at),
                pl.BlockSpec((1, half, 1, tile // CHUNKS, width), down_at),
                pl.BlockSpec((1, 1, width // 2 // CHUNKS, width), out_at),
            ],
            input_output_aliases={1 + len(operands) + i: i for i in range(len(old))},
        )

    near_da = near_rows(after(send, ff.operand))
    w_sum = SumOverAll(w_keep, after(w_send, ff.operand), 16, sizes)
    w = w_sum.begin()
    far = add_low(keep, near_da[1])
    w = w_sum.step(after(w, far))
    far = far_rows(far)
    w = w_sum.step(w)
    moving = ff.step(after(moving, w_sum.operand))
    far = after(far, ff.operand)
    w = w_sum.step(after(w, far))
    last_args = [x, dh, gain_one, own, near_da, after(far, ff.operand)]
    grad_atoms = call(
        lambda ids, *refs: last_kernel(1, *refs),
        "last",
        2,
        (1,),
        last_args,
        [whole(v.shape) for v in last_args],
        atom_outs,
        atom_specs,
    )
    w = w_sum.step(after(w, grad_atoms[0]))
    moving = ff.step(after(moving, w_sum.operand))
    w = w_sum.step(after(w, ff.operand))
    grads = finish_ff(
        "finish_ff_early", ff.own, after_all(ff.other, w_sum.operand), 0, (0, 0), []
    )
    w = w_sum.step(after(w, *grads))
    moving = ff.step(after(moving, w_sum.operand))
    ff.step(moving)
    grad_up, grad_down, go = finish_ff(
        "finish_ff", ff.own[2:], ff.other[2:], 2, (0, ff_rows), grads
    )

    def ordered(pieces, at, size, rows, mine):
        blocks = []
        for chunk in range(CHUNKS):
            place = chunk ^ mine
            start = at + (rows if place == 3 else 0)
            blocks.append(pieces[min(place, 2)][pl.ds(start, size), :])
        return jnp.concatenate(blocks, axis=0)

    def for_each_order(mine, put):
        for value in range(CHUNKS):
            pl.when(mine == value)(lambda value=value: put(value))

    w = w_sum.step(after(w, grad_down))
    w_sum.step(w)

    def finish_rest(ids, *refs):
        own_refs, other_refs = refs[0:3], refs[3:6]
        gq_out, gk_out, gv_out = refs[6:9]
        gains = refs[9:13]
        size = width // CHUNKS

        def put_zero(refs, mine):
            gq_out[...] = ordered(refs, 0, size, share, mine).astype(F32)
            gv_out[:, : width // 2] = ordered(refs, size, size // 2, share, mine).T.astype(F32)

        def put_gains(ref):
            rows = ref[share : share + 16, :].astype(F32)
            for at, out in enumerate(gains):
                out[...] = rows[at]

        def put_one(refs, mine):
            gk_out[...] = ordered(refs, 0, size, share, mine).T.astype(F32)
            gv_out[:, width // 2 :] = ordered(refs, size, size // 2, share, mine).T.astype(F32)

        @pl.when(ids[0] == 0)
        def _():
            for_each_order(ids[1], functools.partial(put_zero, own_refs))
            for_each_order(ids[2], functools.partial(put_one, other_refs))
            put_gains(own_refs[0])

        @pl.when(ids[0] == 1)
        def _():
            for_each_order(ids[2], functools.partial(put_zero, other_refs))
            for_each_order(ids[1], functools.partial(put_one, own_refs))
            put_gains(other_refs[0])

    pieces = w_sum.own + w_sum.other
    gq, gk, gv, *gs = call(
        finish_rest,
        "finish_rest",
        3,
        (1,),
        pieces,
        [whole(v.shape) for v in pieces],
        [(wq.shape, F32)] * 3 + [((width,), F32)] * 4,
        [whole(wq.shape)] * 3 + [whole((width,))] * 4,
    )

    return (
        *[v.reshape(a.shape) for v, a in zip(atoms_out, atoms)],
        *[v.reshape(a.shape) for v, a in zip(pair_out, pairs)],
        *[v.reshape(a.shape) for v, a in zip(grad_atoms, atoms)],
        *[v.reshape(a.shape) for v, a in zip(dls, pairs)],
        gq,
        gk,
        gv,
        go.reshape(wo.shape),
        grad_up.reshape(wu.shape),
        grad_down.reshape(wd.shape),
        *gs,
    )


def solution(mesh):
    atom = P(None, "dp", "rows", None)
    pair = P(None, "dp", None, "rows", None)
    length = P(None, "dp")
    in_specs = (
        (atom,) * 3 + (pair,) * 3 + (length,) * 3 + (P(),) * 10 + (atom,) * 3 + (pair,) * 3
    )
    out_specs = (atom,) * 3 + (pair,) * 3 + (atom,) * 3 + (pair,) * 3 + (P(),) * 10
    body = functools.partial(shards, dict(mesh.shape))
    return jax.shard_map(
        body, mesh=mesh, in_specs=in_specs, out_specs=out_specs, check_vma=False
    )
```
